32 devices in a mesh: group: 2 (over y), expert: 4 (over z), etp: 4 (over x, core).
Axes of the slice: x: 2, y: 2, z: 4, core: 2. Of those that a mesh axis runs over, the one named last changes fastest.
Arguments:
- tokens: bfloat16 [128, 4096], P(('group', 'expert')), parts along dimension 0, may hold values from -6 to 6
- expert_ids: int32 [128, 2], P(('group', 'expert')), parts along dimension 0, may hold values from 0 to 3, all different within a row; in each aligned block of 4 rows (0 to 3, 4 to 7, ...) at most 4 rows name the same one
- route_weights: float32 [128, 2], P(('group', 'expert', 'etp')), parts along dimension 0, may hold values from 0.05 to 1
- w_gate: bfloat16 [4, 1536, 4096], P('expert', 'etp'), may hold values from -0.09375 to 0.09375
- w_up: bfloat16 [4, 1536, 4096], P('expert', 'etp'), may hold values from -0.09375 to 0.09375
- w_down: bfloat16 [4, 1536, 4096], P('expert', 'etp'), may hold values from -0.15625 to 0.15625
Outputs:
- mixed: bfloat16 [128, 4096], P(('group', 'expert', 'etp')), parts along dimension 0
The draws below stay inside these ranges and needn't reach their ends.
There are 2 independent parts, one for each index of `group`. The reference program is written for one: setup_inputs(seed, part) draws one part's arguments, and reference() takes and returns one part's arrays. A program takes and returns all parts, laid end to end along the dimension named above; an argument that names none is the same for every part. Nothing has to cross between parts.
Inputs may be any that keep to these rules, and one draw needn't show every extreme that they name: `expert_ids`: each row names 2 different experts; in each aligned block of 4 rows no expert is named by more than 4 rows, a bound that some block reaches.
All inputs are finite; a program needn't handle non-finite values.
Results may differ from the reference program's by a relative error of at most 0.015.
Values may be sent and summed in bfloat16 or wider, within the bound.
No kernel may reach another device: no remote copies, remote signals or barrier semaphores. Data moves between devices by JAX's collectives and lax.ppermute only.
A program may use at most 64 MiB of HBM per device.

```python
import math
import jax
import jax.numpy as jnp
import numpy as np
from jax import lax

D = 4096
FF = 1536
ROWS_DEV = 4
EXPERTS = 4
TOP = 2
CAPSUB = 4
TOKENS = 64
NBLK = 16
N_ETP = 4


def block_scale(rng, extent, shards, smallest, largest):
    loudness = 1.0
    for position, shards_of in shards:
        steps = jax.random.uniform(jax.random.fold_in(jax.random.fold_in(rng, 6), position), (shards_of,), jnp.float32, smallest / len(shards), largest / len(shards))
        loudness = loudness * jnp.repeat(jnp.exp(steps), extent[position] // shards_of).reshape((-1,) + (1,) * (len(extent) - 1 - position))
    return loudness


def deal_out(key, own, number, rows, number_of, top, reach, slope):
    order = jax.random.permutation(key, number_of)
    crowded, common = shares(number_of, rows * top, reach, slope, True), shares(number_of, rows * top, reach, slope, False)
    places = jnp.arange(number_of)

    def named(tallies, offset_by):
        used = int((tallies > 0).sum())
        fixed = max(1, used // 4)
        moved = fixed + (places - fixed + offset_by * (used - fixed)) % max(1, number_of - fixed)
        return jnp.zeros((number_of,), jnp.int32).at[order[jnp.where(places < fixed, places, moved)]].set(jnp.asarray(tallies, jnp.int32))

    tallies = jnp.where(number % 4 == 0, named(crowded, number // 4), named(common, number - number // 4 - 1))
    mixed = jax.random.permutation(jax.random.fold_in(own, 3), number_of)
    donor, taker = mixed[0:number_of // 2 * 2:2], mixed[1:number_of // 2 * 2:2]
    room = jnp.minimum(tallies[donor] - 1, reach - tallies[taker]) // 2
    room = jnp.where((donor == order[0]) | (taker == order[0]) | (tallies[taker] == 0), 0, jnp.maximum(room, 0))
    moved = jax.random.randint(jax.random.fold_in(own, 4), (number_of // 2,), 0, 1 << 20) % (room + 1)
    tallies = tallies.at[donor].add(-moved).at[taker].add(moved)
    members = jnp.searchsorted(jnp.cumsum(tallies), jnp.arange(rows * top), side="right").astype(jnp.int32)
    listing = members.reshape(top, rows).T
    listing = listing[jax.random.permutation(jax.random.fold_in(own, 1), rows)]
    offset_by = jax.random.randint(jax.random.fold_in(own, 2), (rows, 1), 0, top)
    return jnp.take_along_axis(listing, (jnp.arange(top)[None, :] + offset_by) % top, axis=1)


def shares(number_of, total, reach, slope, full):
    weights = [(1 << 20) // math.isqrt(rank ** slope) + 1 for rank in range(1, number_of + 1)]
    largest = reach if full else min(reach, max(-(-total // number_of), total * weights[0] // sum(weights)))
    least = 1 if total - largest >= number_of - 1 else 0
    counts, spare = [largest] + [least] * (number_of - 1), total - largest - least * (number_of - 1)
    while spare > 0:
        free = [i for i in range(1, number_of) if counts[i] < largest] or [i for i in range(1, number_of) if counts[i] < reach]
        whole, left = sum([weights[i] for i in free]), spare
        for i in free:
            extra = min(reach - counts[i], max(1, left * weights[i] // whole), spare)
            counts[i] = counts[i] + extra
            spare = spare - extra
    return np.array(counts)


def normal_values(stream_key, extent, width, bound, cuts=(), held_as=jnp.bfloat16):
    gain = block_scale(stream_key, extent, cuts, -0.22, 0.18) if cuts else 1.0
    array = jax.random.normal(stream_key, extent, jnp.float32) * width * gain
    return jnp.minimum(jnp.maximum(array, -bound), bound).astype(held_as)


def setup_inputs(seed: int = 0, part: int = 0) -> dict:
    key_list = jax.random.split(jax.random.key(seed), 7)
    part_keys = jax.random.split(jax.random.fold_in(key_list[6], part), 7)
    tokens = normal_values(part_keys[0], (TOKENS, D), 1.0, 6.0, ((0, 4),))
    expert_ids_keys = jax.random.split(jax.random.fold_in(part_keys[1], 1), TOKENS // ROWS_DEV)
    expert_ids_turns = jax.random.permutation(jax.random.fold_in(part_keys[1], 3), TOKENS // ROWS_DEV)
    expert_ids = jax.vmap(lambda own, number: deal_out(jax.random.fold_in(part_keys[1], 2), own, number, ROWS_DEV, EXPERTS, TOP, CAPSUB, 2))(expert_ids_keys, expert_ids_turns).reshape((TOKENS, TOP))
    route_weights = jnp.clip(jnp.exp(math.log(1.0) - 2.9957323 * jax.random.uniform(part_keys[2], (TOKENS, TOP), jnp.float32) ** block_scale(part_keys[2], (TOKENS, TOP), ((0, 16),), -0.2, 0.2)), 0.05, 1.0)
    w_gate = normal_values(key_list[3], (EXPERTS, FF, D), D ** -0.5, 0.09375, ((0, 4), (1, 4)))
    w_up = normal_values(key_list[4], (EXPERTS, FF, D), D ** -0.5, 0.09375, ((0, 4), (1, 4)))
    w_down = normal_values(key_list[5], (EXPERTS, FF, D), FF ** -0.5, 0.15625, ((0, 4), (1, 4)))
    return dict(tokens=tokens, expert_ids=expert_ids, route_weights=route_weights, w_gate=w_gate, w_up=w_up, w_down=w_down)


def reference(tokens, expert_ids, route_weights, w_gate, w_up, w_down):
    ffd = FF // N_ETP
    flat = expert_ids.reshape(-1)
    count = flat.shape[0]
    row = jnp.arange(count, dtype=jnp.int32) // TOP
    block = row // ROWS_DEV
    by_block = expert_ids.reshape(NBLK, ROWS_DEV * TOP)
    onehot = (by_block[:, :, None] == jnp.arange(EXPERTS, dtype=jnp.int32)[None, None, :]).astype(jnp.int32)
    ranks = jnp.cumsum(onehot, axis=1) - onehot
    slot = jnp.sum(ranks * onehot, axis=2).reshape(-1)
    pos = (flat * (NBLK * CAPSUB) + block * CAPSUB + slot).astype(jnp.int32)
    source = jnp.zeros((EXPERTS * NBLK * CAPSUB,), jnp.int32).at[pos].set(row)

    def one_expert(items):
        index, gate_e, up_e, down_e = items
        rows_in = tokens[index]
        gate = jnp.dot(rows_in, gate_e.T, preferred_element_type=jnp.float32)
        upper = jnp.dot(rows_in, up_e.T, preferred_element_type=jnp.float32)
        hidden = (jax.nn.silu(gate) * upper).astype(jnp.bfloat16)
        parts = jnp.einsum('rsf,sfd->rsd', hidden.reshape(-1, N_ETP, ffd).astype(jnp.float32),
                           down_e.reshape(N_ETP, ffd, D).astype(jnp.float32))
        parts = lax.optimization_barrier(parts.astype(jnp.bfloat16)).astype(jnp.float32)
        return jnp.sum(parts, axis=1).astype(jnp.bfloat16)

    results = lax.map(one_expert, (source.reshape(EXPERTS, NBLK * CAPSUB), w_gate, w_up, w_down))
    picked = results.reshape(-1, D)[pos].astype(jnp.float32).reshape(TOKENS, TOP, D)
    combine = route_weights / jnp.sum(route_weights, axis=1, keepdims=True)
    return jnp.sum(picked * combine[:, :, None], axis=1).astype(jnp.bfloat16)
```

```python
import functools

import jax
import jax.numpy as jnp
from jax import lax
from jax.experimental import pallas as pl
from jax.experimental.pallas import tpu as pltpu
from jax.sharding import PartitionSpec as P

VMEM = pl.BlockSpec(memory_space=pltpu.VMEM)
HBM = pl.BlockSpec(memory_space=pl.ANY)


def order_matrix(n_expert, pairs, rows, me):
    total = n_expert * pairs * 2 * rows
    core, pair = lax.rem(me, 2), lax.div(me, 2)
    place = lax.broadcasted_iota(jnp.int32, (total, total), 0)
    source = lax.broadcasted_iota(jnp.int32, (total, total), 1)
    row = lax.rem(place, rows)
    h = lax.rem(lax.div(place, rows), pairs)
    k = lax.rem(lax.div(place, rows * pairs), n_expert)
    sent = lax.div(place, rows * pairs * n_expert)
    block = 2 * lax.rem(pair + h, pairs) + lax.rem(core + sent, 2)
    wanted = (k * pairs * 2 + block) * rows + row
    return jnp.where(source == wanted, 1.0, 0.0).astype(jnp.bfloat16)


def ffn_kernel(n_expert, n_etp, rows, parts, own, *refs):
    near = refs[: n_expert - 1]
    far = refs[n_expert - 1 : 2 * n_expert - 2]
    w_gate, w_up, w_down, kept, sent, x, gate_v, up_v, down_v, sems = refs[2 * n_expert - 2 :]
    me = lax.axis_index("etp")
    core = lax.rem(me, 2)
    width = own.shape[1]
    half = width // 2
    step = width // parts
    copies = []
    for i, (src, dst) in enumerate(((w_gate, gate_v), (w_up, up_v), (w_down, down_v))):
        group = []
        for c in range(parts):
            cols = pl.ds(c * step, step)
            copy = pltpu.make_async_copy(src.at[0, :, cols], dst.at[:, cols], sems.at[i, c])
            copy.start()
            group.append(copy)
        copies.append(group)
    tok = own.shape[0]
    x[0:tok, :] = own[...]
    mine = pl.ds(pl.multiple_of(core * half, half), half)
    other = pl.ds(pl.multiple_of((1 - core) * half, half), half)
    for k in range(1, n_expert):
        x[k * tok : (k + 1) * tok, mine] = near[k - 1][...]
        x[k * tok : (k + 1) * tok, other] = far[k - 1][...]
    contract = (((1,), (1,)), ((), ()))
    sums = []
    for group, w in ((copies[0], gate_v), (copies[1], up_v)):
        total = None
        for c in range(parts):
            group[c].wait()
            cols = slice(c * step, (c + 1) * step)
            part = lax.dot_general(
                x[:, cols], w[:, cols], contract, preferred_element_type=jnp.float32
            )
            total = part if total is None else total + part
        sums.append(total)
    gate, upper = sums
    hidden = (gate / (1.0 + jnp.exp(-gate)) * upper).astype(jnp.bfloat16)
    order = order_matrix(n_expert, n_etp // 2, rows, me)
    hidden = jnp.dot(order, hidden, preferred_element_type=jnp.float32).astype(jnp.bfloat16)
    side = kept.shape[0]
    for c in range(parts):
        copies[2][c].wait()
        cols = slice(c * step, (c + 1) * step)
        out = jnp.dot(hidden, down_v[:, cols], preferred_element_type=jnp.float32)
        kept[:, cols] = out[:side]
        sent[:, cols] = out[side:].astype(jnp.bfloat16)


def add_kernel(rows, kept, arrived, *pieces):
    for i, piece in enumerate(pieces):
        span = slice(i * rows, (i + 1) * rows)
        piece[...] = (kept[span, :] + arrived[span, :].astype(jnp.float32)).astype(jnp.bfloat16)


def mix_kernel(n_expert, pairs, ids, weights, *refs):
    pieces, out = refs[:-1], refs[-1]
    rows = out.shape[0]
    me, expert = lax.axis_index("etp"), lax.axis_index("expert")
    own_ids = ids[pl.ds(me * rows, rows), :]
    scale = weights[...]
    scale = scale / jnp.sum(scale, axis=1, keepdims=True)
    total = None
    for k in range(n_expert):
        owner = lax.rem(expert + k, n_expert)
        factor = jnp.sum(jnp.where(own_ids == owner, scale, 0.0), axis=1, keepdims=True)
        summed = None
        for h in range(pairs):
            piece = pieces[k * pairs + h][...].astype(jnp.float32)
            summed = piece if summed is None else summed + piece
        term = summed * factor
        total = term if total is None else total + term
    out[...] = total.astype(out.dtype)


def on_device(n_expert, n_etp, tokens, expert_ids, route_weights, w_gate, w_up, w_down):
    tok, width = tokens.shape
    hidden = w_gate.shape[1]
    rows = tok // n_etp
    pairs = n_etp // 2
    side = n_expert * tok // 2
    half = width // 2
    me = lax.axis_index("etp")
    core = lax.rem(me, 2)

    own_half = lax.dynamic_slice_in_dim(tokens, core * half, half, 1)
    near, far = [], []
    swap = [(i, i ^ 1) for i in range(n_etp)]
    for k in range(1, n_expert):
        hop = [(i, (i + k) % n_expert) for i in range(n_expert)]
        near.append(lax.ppermute(own_half, "expert", hop))
    for block in near:
        far.append(lax.ppermute(block, "etp", swap))

    parts = 4
    kept, sent = pl.pallas_call(
        functools.partial(ffn_kernel, n_expert, n_etp, rows, parts),
        out_shape=(
            jax.ShapeDtypeStruct((side, width), jnp.float32),
            jax.ShapeDtypeStruct((side, width), jnp.bfloat16),
        ),
        in_specs=[VMEM] * (2 * n_expert - 1) + [HBM] * 3,
        out_specs=(VMEM, VMEM),
        scratch_shapes=[
            pltpu.VMEM((n_expert * tok, width), jnp.bfloat16),
            pltpu.VMEM((hidden, width), jnp.bfloat16),
            pltpu.VMEM((hidden, width), jnp.bfloat16),
            pltpu.VMEM((hidden, width), jnp.bfloat16),
            pltpu.SemaphoreType.DMA((3, parts)),
        ],
        compiler_params=pltpu.CompilerParams(vmem_limit_bytes=56 * 1024 * 1024),
        name="ffn",
    )(tokens, *near, *far, w_gate, w_up, w_down)

    arrived = lax.ppermute(sent, "etp", swap)
    count = n_expert * pairs
    pieces = pl.pallas_call(
        functools.partial(add_kernel, rows),
        out_shape=[jax.ShapeDtypeStruct((rows, width), jnp.bfloat16)] * count,
        in_specs=[VMEM] * 2,
        out_specs=[VMEM] * count,
        compiler_params=pltpu.CompilerParams(vmem_limit_bytes=56 * 1024 * 1024),
        name="add",
    )(kept, arrived)

    landed = []
    for i, piece in enumerate(pieces):
        k, h = divmod(i, pairs)
        route = []
        for e in range(n_expert):
            for t in range(n_etp):
                to_e, to_t = (e - k) % n_expert, 2 * ((t // 2 + h) % pairs) + t % 2
                route.append((e * n_etp + t, to_e * n_etp + to_t))
        landed.append(lax.ppermute(piece, ("expert", "etp"), route) if i else piece)

    return pl.pallas_call(
        functools.partial(mix_kernel, n_expert, pairs),
        out_shape=jax.ShapeDtypeStruct((rows, width), jnp.bfloat16),
        in_specs=[VMEM] * (2 + count),
        out_specs=VMEM,
        compiler_params=pltpu.CompilerParams(vmem_limit_bytes=56 * 1024 * 1024),
        name="mix",
    )(expert_ids, route_weights, *landed)


def solution(mesh):
    in_specs = (
        P(("group", "expert"), None),
        P(("group", "expert"), None),
        P(("group", "expert", "etp"), None),
        P("expert", "etp", None),
        P("expert", "etp", None),
        P("expert", "etp", None),
    )
    out_specs = P(("group", "expert", "etp"), None)
    return jax.shard_map(
        functools.partial(on_device, mesh.shape["expert"], mesh.shape["etp"]),
        mesh=mesh,
        in_specs=in_specs,
        out_specs=out_specs,
        check_vma=False,
    )
```

```python
import functools

import jax
import jax.numpy as jnp
from jax import lax
from jax.experimental import pallas as pl
from jax.experimental.pallas import tpu as pltpu
from jax.sharding import PartitionSpec as P

VMEM = pl.BlockSpec(memory_space=pltpu.VMEM)
HBM = pl.BlockSpec(memory_space=pltpu.HBM)


def order_matrix(n_expert, pairs, rows, me):
    total = n_expert * pairs * 2 * rows
    core, pair = lax.rem(me, 2), lax.div(me, 2)
    place = lax.broadcasted_iota(jnp.int32, (total, total), 0)
    source = lax.broadcasted_iota(jnp.int32, (total, total), 1)
    row = lax.rem(place, rows)
    h = lax.rem(lax.div(place, rows), pairs)
    k = lax.rem(lax.div(place, rows * pairs), n_expert)
    sent = lax.div(place, rows * pairs * n_expert)
    block = 2 * lax.rem(pair + h, pairs) + lax.rem(core + sent, 2)
    wanted = (k * pairs * 2 + block) * rows + row
    return jnp.where(source == wanted, 1.0, 0.0).astype(jnp.bfloat16)


def load_kernel(count, *refs):
    sources, targets, sems = refs[:count], refs[count : 2 * count], refs[-1]
    copies = [
        pltpu.make_async_copy(source, target, sems.at[i])
        for i, (source, target) in enumerate(zip(sources, targets))
    ]
    for copy in copies:
        copy.start()
    for copy in copies:
        copy.wait()


def ffn_kernel(n_expert, n_etp, rows, parts, own, *refs):
    near = refs[: n_expert - 1]
    far = refs[n_expert - 1 : 2 * n_expert - 2]
    w_gate, w_up, w_down, kept, sent, x = refs[2 * n_expert - 2 :]
    me = lax.axis_index("etp")
    core = lax.rem(me, 2)
    tok, width = own.shape
    half = width // 2
    step = width // parts
    x[0:tok, :] = own[...]
    mine = pl.ds(pl.multiple_of(core * half, half), half)
    other = pl.ds(pl.multiple_of((1 - core) * half, half), half)
    for k in range(1, n_expert):
        x[k * tok : (k + 1) * tok, mine] = near[k - 1][...]
        x[k * tok : (k + 1) * tok, other] = far[k - 1][...]
    contract = (((1,), (1,)), ((), ()))
    gate = lax.dot_general(w_gate[0], x[...], contract, preferred_element_type=jnp.float32)
    upper = lax.dot_general(w_up[0], x[...], contract, preferred_element_type=jnp.float32)
    hidden = (gate / (1.0 + jnp.exp(-gate)) * upper).astype(jnp.bfloat16)
    order = order_matrix(n_expert, n_etp // 2, rows, me)
    hidden = lax.dot_general(order, hidden, contract, preferred_element_type=jnp.float32)
    hidden = hidden.astype(jnp.bfloat16)
    side = kept.shape[0]
    for c in range(parts):
        cols = slice(c * step, (c + 1) * step)
        out = jnp.dot(hidden, w_down[0, :, cols], preferred_element_type=jnp.float32)
        kept[:, cols] = out[:side]
        sent[:, cols] = out[side:].astype(jnp.bfloat16)


def add_kernel(rows, kept, arrived, *pieces):
    for i, piece in enumerate(pieces):
        span = slice(i * rows, (i + 1) * rows)
        piece[...] = (kept[span, :] + arrived[span, :].astype(jnp.float32)).astype(jnp.bfloat16)


def mix_kernel(n_expert, pairs, ids, weights, *refs):
    pieces, out = refs[:-1], refs[-1]
    rows = out.shape[0]
    me, expert = lax.axis_index("etp"), lax.axis_index("expert")
    top, tok = ids.shape

    def column(ref, start, i):
        lane = lax.broadcasted_iota(jnp.int32, (rows, ref.shape[1]), 1)
        row = lax.broadcasted_iota(jnp.int32, (rows, ref.shape[1]), 0)
        values = jnp.where(lane == start + row, ref[i : i + 1, :], 0)
        return jnp.sum(values, axis=1, keepdims=True)

    own_ids = [column(ids, me * rows, i) for i in range(top)]
    own_weights = [column(weights, 0, i) for i in range(top)]
    scale = sum(own_weights)
    total = None
    for k in range(n_expert):
        owner = lax.rem(expert + k, n_expert)
        factor = sum(jnp.where(own_ids[i] == owner, own_weights[i], 0.0) for i in range(top)) / scale
        summed = None
        for h in range(pairs):
            piece = pieces[k * pairs + h][...].astype(jnp.float32)
            summed = piece if summed is None else summed + piece
        term = summed * factor
        total = term if total is None else total + term
    out[...] = total.astype(out.dtype)


def on_device(n_expert, n_etp, tokens, expert_ids, route_weights, w_gate, w_up, w_down):
    tok, width = tokens.shape
    rows = tok // n_etp
    pairs = n_etp // 2
    side = n_expert * tok // 2
    half = width // 2
    me = lax.axis_index("etp")
    core = lax.rem(me, 2)

    own_half = lax.dynamic_slice_in_dim(tokens, core * half, half, 1)
    near, far = [], []
    swap = [(i, i ^ 1) for i in range(n_etp)]
    for k in range(1, n_expert):
        hop = [(i, (i + k) % n_expert) for i in range(n_expert)]
        near.append(lax.ppermute(own_half, "expert", hop))
    for block in near:
        far.append(lax.ppermute(block, "etp", swap))

    weights = (w_gate, w_up, w_down)
    size = sum(w.size * 2 for w in weights)
    weights = pl.pallas_call(
        functools.partial(load_kernel, len(weights)),
        out_shape=[jax.ShapeDtypeStruct(w.shape, w.dtype) for w in weights],
        in_specs=[HBM] * len(weights),
        out_specs=[VMEM] * len(weights),
        scratch_shapes=[pltpu.SemaphoreType.DMA((len(weights),))],
        cost_estimate=pl.CostEstimate(flops=0, bytes_accessed=2 * size, transcendentals=0),
        name="load",
    )(*(pltpu.with_memory_space_constraint(w, pltpu.HBM) for w in weights))

    parts = 4
    kept, sent = pl.pallas_call(
        functools.partial(ffn_kernel, n_expert, n_etp, rows, parts),
        out_shape=(
            jax.ShapeDtypeStruct((side, width), jnp.float32),
            jax.ShapeDtypeStruct((side, width), jnp.bfloat16),
        ),
        in_specs=[VMEM] * (2 * n_expert + 2),
        out_specs=(VMEM, VMEM),
        scratch_shapes=[
            pltpu.VMEM((n_expert * tok, width), jnp.bfloat16),
        ],
        compiler_params=pltpu.CompilerParams(vmem_limit_bytes=16 * 1024 * 1024),
        name="ffn",
    )(tokens, *near, *far, *weights)

    arrived = lax.ppermute(sent, "etp", swap)
    count = n_expert * pairs
    pieces = pl.pallas_call(
        functools.partial(add_kernel, rows),
        out_shape=[jax.ShapeDtypeStruct((rows, width), jnp.bfloat16)] * count,
        in_specs=[VMEM] * 2,
        out_specs=[VMEM] * count,
        name="add",
    )(kept, arrived)

    landed = []
    for i, piece in enumerate(pieces):
        k, h = divmod(i, pairs)
        route = []
        for e in range(n_expert):
            for t in range(n_etp):
                to_e, to_t = (e - k) % n_expert, 2 * ((t // 2 + h) % pairs) + t % 2
                route.append((e * n_etp + t, to_e * n_etp + to_t))
        landed.append(lax.ppermute(piece, ("expert", "etp"), route) if i else piece)

    return pl.pallas_call(
        functools.partial(mix_kernel, n_expert, pairs),
        out_shape=jax.ShapeDtypeStruct((rows, width), jnp.bfloat16),
        in_specs=[VMEM] * (2 + count),
        out_specs=VMEM,
        name="mix",
    )(expert_ids.T, route_weights.T, *landed)


def solution(mesh):
    in_specs = (
        P(("group", "expert"), None),
        P(("group", "expert"), None),
        P(("group", "expert", "etp"), None),
        P("expert", "etp", None),
        P("expert", "etp", None),
        P("expert", "etp", None),
    )
    out_specs = P(("group", "expert", "etp"), None)
    return jax.shard_map(
        functools.partial(on_device, mesh.shape["expert"], mesh.shape["etp"]),
        mesh=mesh,
        in_specs=in_specs,
        out_specs=out_specs,
        check_vma=False,
    )
```

```python
import functools

import jax
import jax.numpy as jnp
from jax import lax
from jax.experimental import pallas as pl
from jax.experimental.pallas import tpu as pltpu
from jax.sharding import PartitionSpec as P

VMEM = pl.BlockSpec(memory_space=pltpu.VMEM)
GRANT = pltpu.CompilerParams(vmem_limit_bytes=16 * 1024 * 1024)
HBM = pl.BlockSpec(memory_space=pltpu.HBM)


def order_matrix(n_expert, pairs, rows, me):
    total = n_expert * pairs * 2 * rows
    core, pair = lax.rem(me, 2), lax.div(me, 2)
    place = lax.broadcasted_iota(jnp.int32, (total, total), 0)
    source = lax.broadcasted_iota(jnp.int32, (total, total), 1)
    row = lax.rem(place, rows)
    h = lax.rem(lax.div(place, rows), pairs)
    k = lax.rem(lax.div(place, rows * pairs), n_expert)
    sent = lax.div(place, rows * pairs * n_expert)
    block = 2 * lax.rem(pair + h, pairs) + lax.rem(core + sent, 2)
    wanted = (k * pairs * 2 + block) * rows + row
    return jnp.where(source == wanted, 1.0, 0.0).astype(jnp.bfloat16)


def load_kernel(count, parts, *refs):
    sources, targets, sems = refs[:count], refs[count : 2 * count], refs[-1]
    copies = []
    for i, (source, target) in enumerate(zip(sources, targets)):
        step = source.shape[1] // parts
        for c in range(parts):
            span = pl.ds(c * step, step)
            copies.append(
                pltpu.make_async_copy(source.at[:, span], target.at[:, span], sems.at[i, c])
            )
    for copy in copies:
        copy.start()
    for copy in copies:
        copy.wait()


def ffn_kernel(n_expert, n_etp, rows, parts, own, *refs):
    near = refs[: n_expert - 1]
    far = refs[n_expert - 1 : 2 * n_expert - 2]
    w_gate, w_up, w_down, kept, sent, x = refs[2 * n_expert - 2 :]
    me = lax.axis_index("etp")
    core = lax.rem(me, 2)
    tok, width = own.shape
    half = width // 2
    step = width // parts
    x[0:tok, :] = own[...]
    mine = pl.ds(pl.multiple_of(core * half, half), half)
    other = pl.ds(pl.multiple_of((1 - core) * half, half), half)
    for k in range(1, n_expert):
        x[k * tok : (k + 1) * tok, mine] = near[k - 1][...]
        x[k * tok : (k + 1) * tok, other] = far[k - 1][...]
    contract = (((1,), (1,)), ((), ()))
    gate = lax.dot_general(w_gate[0], x[...], contract, preferred_element_type=jnp.float32)
    upper = lax.dot_general(w_up[0], x[...], contract, preferred_element_type=jnp.float32)
    hidden = (gate / (1.0 + jnp.exp(-gate)) * upper).astype(jnp.bfloat16)
    order = order_matrix(n_expert, n_etp // 2, rows, me)
    hidden = lax.dot_general(order, hidden, contract, preferred_element_type=jnp.float32)
    hidden = hidden.astype(jnp.bfloat16)
    side = kept.shape[0]
    for c in range(parts):
        cols = slice(c * step, (c + 1) * step)
        out = jnp.dot(hidden, w_down[0, :, cols], preferred_element_type=jnp.float32)
        kept[:, cols] = out[:side]
        sent[:, cols] = out[side:].astype(jnp.bfloat16)


def add_kernel(rows, kept, arrived, *pieces):
    for i, piece in enumerate(pieces):
        span = slice(i * rows, (i + 1) * rows)
        piece[...] = (kept[span, :] + arrived[span, :].astype(jnp.float32)).astype(jnp.bfloat16)


def mix_kernel(n_expert, pairs, ids, weights, *refs):
    pieces, out = refs[:-1], refs[-1]
    rows = out.shape[0]
    me, expert = lax.axis_index("etp"), lax.axis_index("expert")
    top, tok = ids.shape

    def column(ref, start, i):
        lane = lax.broadcasted_iota(jnp.int32, (rows, ref.shape[1]), 1)
        row = lax.broadcasted_iota(jnp.int32, (rows, ref.shape[1]), 0)
        values = jnp.where(lane == start + row, ref[i : i + 1, :], 0)
        return jnp.sum(values, axis=1, keepdims=True)

    own_ids = [column(ids, me * rows, i) for i in range(top)]
    own_weights = [column(weights, 0, i) for i in range(top)]
    scale = sum(own_weights)
    total = None
    for k in range(n_expert):
        owner = lax.rem(expert + k, n_expert)
        factor = sum(jnp.where(own_ids[i] == owner, own_weights[i], 0.0) for i in range(top)) / scale
        summed = None
        for h in range(pairs):
            piece = pieces[k * pairs + h][...].astype(jnp.float32)
            summed = piece if summed is None else summed + piece
        term = summed * factor
        total = term if total is None else total + term
    out[...] = total.astype(out.dtype)


def on_device(n_expert, n_etp, tokens, expert_ids, route_weights, w_gate, w_up, w_down):
    tok, width = tokens.shape
    rows = tok // n_etp
    pairs = n_etp // 2
    side = n_expert * tok // 2
    half = width // 2
    me = lax.axis_index("etp")
    core = lax.rem(me, 2)

    own_half = lax.dynamic_slice_in_dim(tokens, core * half, half, 1)
    near, far = [], []
    swap = [(i, i ^ 1) for i in range(n_etp)]
    for k in range(1, n_expert):
        hop = [(i, (i + k) % n_expert) for i in range(n_expert)]
        near.append(lax.ppermute(own_half, "expert", hop))
    for block in near:
        far.append(lax.ppermute(block, "etp", swap))

    parts = 4
    weights = (w_gate, w_up, w_down)
    size = sum(w.size * 2 for w in weights)
    weights = pl.pallas_call(
        functools.partial(load_kernel, len(weights), parts),
        out_shape=[jax.ShapeDtypeStruct(w.shape, w.dtype) for w in weights],
        in_specs=[HBM] * len(weights),
        out_specs=[VMEM] * len(weights),
        scratch_shapes=[pltpu.SemaphoreType.DMA((len(weights), parts))],
        cost_estimate=pl.CostEstimate(flops=0, bytes_accessed=2 * size, transcendentals=0),
        compiler_params=GRANT,
        name="load",
    )(*(pltpu.with_memory_space_constraint(w, pltpu.HBM) for w in weights))

    kept, sent = pl.pallas_call(
        functools.partial(ffn_kernel, n_expert, n_etp, rows, parts),
        out_shape=(
            jax.ShapeDtypeStruct((side, width), jnp.float32),
            jax.ShapeDtypeStruct((side, width), jnp.bfloat16),
        ),
        in_specs=[VMEM] * (2 * n_expert + 2),
        out_specs=(VMEM, VMEM),
        scratch_shapes=[
            pltpu.VMEM((n_expert * tok, width), jnp.bfloat16),
        ],
        compiler_params=GRANT,
        name="ffn",
    )(tokens, *near, *far, *weights)

    arrived = lax.ppermute(sent, "etp", swap)
    count = n_expert * pairs
    pieces = pl.pallas_call(
        functools.partial(add_kernel, rows),
        out_shape=[jax.ShapeDtypeStruct((rows, width), jnp.bfloat16)] * count,
        in_specs=[VMEM] * 2,
        out_specs=[VMEM] * count,
        compiler_params=GRANT,
        name="add",
    )(kept, arrived)

    landed = []
    for i, piece in enumerate(pieces):
        k, h = divmod(i, pairs)
        route = []
        for e in range(n_expert):
            for t in range(n_etp):
                to_e, to_t = (e - k) % n_expert, 2 * ((t // 2 + h) % pairs) + t % 2
                route.append((e * n_etp + t, to_e * n_etp + to_t))
        landed.append(lax.ppermute(piece, ("expert", "etp"), route) if i else piece)

    return pl.pallas_call(
        functools.partial(mix_kernel, n_expert, pairs),
        out_shape=jax.ShapeDtypeStruct((rows, width), jnp.bfloat16),
        in_specs=[VMEM] * (2 + count),
        out_specs=VMEM,
        compiler_params=GRANT,
        name="mix",
    )(expert_ids.T, route_weights.T, *landed)


def solution(mesh):
    in_specs = (
        P(("group", "expert"), None),
        P(("group", "expert"), None),
        P(("group", "expert", "etp"), None),
        P("expert", "etp", None),
        P("expert", "etp", None),
        P("expert", "etp", None),
    )
    out_specs = P(("group", "expert", "etp"), None)
    return jax.shard_map(
        functools.partial(on_device, mesh.shape["expert"], mesh.shape["etp"]),
        mesh=mesh,
        in_specs=in_specs,
        out_specs=out_specs,
        check_vma=False,
    )
```

```python
import functools

import jax
import jax.numpy as jnp
from jax import lax
from jax.experimental import pallas as pl
from jax.experimental.pallas import tpu as pltpu
from jax.sharding import PartitionSpec as P

VMEM = pl.BlockSpec(memory_space=pltpu.VMEM)
GRANT = pltpu.CompilerParams(vmem_limit_bytes=16 * 1024 * 1024)
HBM = pl.BlockSpec(memory_space=pltpu.HBM)


def order_matrix(n_expert, pairs, rows, me):
    total = n_expert * pairs * 2 * rows
    core, pair = lax.rem(me, 2), lax.div(me, 2)
    place = lax.broadcasted_iota(jnp.int32, (total, total), 0)
    source = lax.broadcasted_iota(jnp.int32, (total, total), 1)
    row = lax.rem(place, rows)
    k = lax.rem(lax.div(place, rows), n_expert)
    h = lax.rem(lax.div(place, rows * n_expert), pairs)
    sent = lax.div(place, rows * pairs * n_expert)
    block = 2 * lax.rem(pair + h, pairs) + lax.rem(core + sent, 2)
    wanted = (k * pairs * 2 + block) * rows + row
    return jnp.where(source == wanted, 1.0, 0.0).astype(jnp.bfloat16)


def load_kernel(count, parts, *refs):
    sources, targets, sems = refs[:count], refs[count : 2 * count], refs[-1]
    copies = []
    for i, (source, target) in enumerate(zip(sources, targets)):
        step = source.shape[1] // parts
        for c in range(parts):
            span = pl.ds(c * step, step)
            copies.append(
                pltpu.make_async_copy(source.at[:, span], target.at[:, span], sems.at[i, c])
            )
    for copy in copies:
        copy.start()
    for copy in copies:
        copy.wait()


def ffn_kernel(n_expert, n_etp, rows, parts, own, *refs):
    near = refs[: n_expert - 1]
    far = refs[n_expert - 1 : 2 * n_expert - 2]
    w_gate, w_up, w_down, kept, sent, x = refs[2 * n_expert - 2 :]
    me = lax.axis_index("etp")
    core = lax.rem(me, 2)
    tok, width = own.shape
    half = width // 2
    step = width // parts
    x[0:tok, :] = own[...]
    mine = pl.ds(pl.multiple_of(core * half, half), half)
    other = pl.ds(pl.multiple_of((1 - core) * half, half), half)
    for k in range(1, n_expert):
        x[k * tok : (k + 1) * tok, mine] = near[k - 1][...]
        x[k * tok : (k + 1) * tok, other] = far[k - 1][...]
    contract = (((1,), (1,)), ((), ()))
    gate = lax.dot_general(w_gate[0], x[...], contract, preferred_element_type=jnp.float32)
    upper = lax.dot_general(w_up[0], x[...], contract, preferred_element_type=jnp.float32)
    hidden = (gate / (1.0 + jnp.exp(-gate)) * upper).astype(jnp.bfloat16)
    order = order_matrix(n_expert, n_etp // 2, rows, me)
    hidden = lax.dot_general(order, hidden, contract, preferred_element_type=jnp.float32)
    hidden = hidden.astype(jnp.bfloat16)
    side = kept.shape[0]
    for c in range(parts):
        cols = slice(c * step, (c + 1) * step)
        out = jnp.dot(hidden, w_down[0, :, cols], preferred_element_type=jnp.float32)
        kept[:, cols] = out[:side]
        sent[:, cols] = out[side:].astype(jnp.bfloat16)


def add_kernel(kept, arrived, own, *pieces):
    span = own.shape[0]
    own[...] = kept[:span, :] + arrived[:span, :].astype(jnp.float32)
    for i, piece in enumerate(pieces):
        at = slice((i + 1) * span, (i + 2) * span)
        piece[...] = (kept[at, :] + arrived[at, :].astype(jnp.float32)).astype(jnp.bfloat16)


def fold_kernel(pairs, own, *refs):
    arrived, pieces = refs[: pairs - 1], refs[pairs - 1 :]
    total = own[...]
    for block in arrived:
        total = total + block[...].astype(jnp.float32)
    rows = pieces[0].shape[0]
    for k, piece in enumerate(pieces):
        piece[...] = total[k * rows : (k + 1) * rows].astype(piece.dtype)


def mix_kernel(n_expert, ids, weights, *refs):
    pieces, out = refs[:-1], refs[-1]
    rows = out.shape[0]
    me, expert = lax.axis_index("etp"), lax.axis_index("expert")
    top, tok = ids.shape

    def column(ref, start, i):
        lane = lax.broadcasted_iota(jnp.int32, (rows, ref.shape[1]), 1)
        row = lax.broadcasted_iota(jnp.int32, (rows, ref.shape[1]), 0)
        values = jnp.where(lane == start + row, ref[i : i + 1, :], 0)
        return jnp.sum(values, axis=1, keepdims=True)

    own_ids = [column(ids, me * rows, i) for i in range(top)]
    own_weights = [column(weights, 0, i) for i in range(top)]
    scale = sum(own_weights)
    total = None
    for k in range(n_expert):
        owner = lax.rem(expert + k, n_expert)
        factor = sum(jnp.where(own_ids[i] == owner, own_weights[i], 0.0) for i in range(top)) / scale
        term = pieces[k][...].astype(jnp.float32) * factor
        total = term if total is None else total + term
    out[...] = total.astype(out.dtype)


def on_device(n_expert, n_etp, tokens, expert_ids, route_weights, w_gate, w_up, w_down):
    tok, width = tokens.shape
    rows = tok // n_etp
    pairs = n_etp // 2
    side = n_expert * tok // 2
    half = width // 2
    me = lax.axis_index("etp")
    core = lax.rem(me, 2)

    own_half = lax.dynamic_slice_in_dim(tokens, core * half, half, 1)
    near, far = [], []
    swap = [(i, i ^ 1) for i in range(n_etp)]
    for k in range(1, n_expert):
        hop = [(i, (i + k) % n_expert) for i in range(n_expert)]
        near.append(lax.ppermute(own_half, "expert", hop))
    for block in near:
        far.append(lax.ppermute(block, "etp", swap))

    parts = 4
    weights = (w_gate, w_up, w_down)
    size = sum(w.size * 2 for w in weights)
    weights = pl.pallas_call(
        functools.partial(load_kernel, len(weights), parts),
        out_shape=[jax.ShapeDtypeStruct(w.shape, w.dtype) for w in weights],
        in_specs=[HBM] * len(weights),
        out_specs=[VMEM] * len(weights),
        scratch_shapes=[pltpu.SemaphoreType.DMA((len(weights), parts))],
        cost_estimate=pl.CostEstimate(flops=0, bytes_accessed=2 * size, transcendentals=0),
        compiler_params=GRANT,
        name="load",
    )(*(pltpu.with_memory_space_constraint(w, pltpu.HBM) for w in weights))

    kept, sent = pl.pallas_call(
        functools.partial(ffn_kernel, n_expert, n_etp, rows, parts),
        out_shape=(
            jax.ShapeDtypeStruct((side, width), jnp.float32),
            jax.ShapeDtypeStruct((side, width), jnp.bfloat16),
        ),
        in_specs=[VMEM] * (2 * n_expert + 2),
        out_specs=(VMEM, VMEM),
        scratch_shapes=[
            pltpu.VMEM((n_expert * tok, width), jnp.bfloat16),
        ],
        compiler_params=GRANT,
        name="ffn",
    )(tokens, *near, *far, *weights)

    arrived = lax.ppermute(sent, "etp", swap)
    block = n_expert * rows
    own, *pieces = pl.pallas_call(
        add_kernel,
        out_shape=[jax.ShapeDtypeStruct((block, width), jnp.float32)]
        + [jax.ShapeDtypeStruct((block, width), jnp.bfloat16)] * (pairs - 1),
        in_specs=[VMEM] * 2,
        out_specs=[VMEM] * pairs,
        compiler_params=GRANT,
        name="add",
    )(kept, arrived)
    landed = []
    for h, piece in enumerate(pieces, 1):
        route = [(t, 2 * ((t // 2 + h) % pairs) + t % 2) for t in range(n_etp)]
        landed.append(lax.ppermute(piece, "etp", route))
    own, *pieces = pl.pallas_call(
        functools.partial(fold_kernel, pairs),
        out_shape=[jax.ShapeDtypeStruct((rows, width), jnp.float32)]
        + [jax.ShapeDtypeStruct((rows, width), jnp.bfloat16)] * (n_expert - 1),
        in_specs=[VMEM] * pairs,
        out_specs=[VMEM] * n_expert,
        compiler_params=GRANT,
        name="fold",
    )(own, *landed)
    landed = [own]
    for k, piece in enumerate(pieces, 1):
        route = [(e, (e - k) % n_expert) for e in range(n_expert)]
        landed.append(lax.ppermute(piece, "expert", route))

    return pl.pallas_call(
        functools.partial(mix_kernel, n_expert),
        out_shape=jax.ShapeDtypeStruct((rows, width), jnp.bfloat16),
        in_specs=[VMEM] * (2 + n_expert),
        out_specs=VMEM,
        compiler_params=GRANT,
        name="mix",
    )(expert_ids.T, route_weights.T, *landed)


def solution(mesh):
    in_specs = (
        P(("group", "expert"), None),
        P(("group", "expert"), None),
        P(("group", "expert", "etp"), None),
        P("expert", "etp", None),
        P("expert", "etp", None),
        P("expert", "etp", None),
    )
    out_specs = P(("group", "expert", "etp"), None)
    return jax.shard_map(
        functools.partial(on_device, mesh.shape["expert"], mesh.shape["etp"]),
        mesh=mesh,
        in_specs=in_specs,
        out_specs=out_specs,
        check_vma=False,
    )
```

```python
import functools

import jax
import jax.numpy as jnp
from jax import lax
from jax.experimental import pallas as pl
from jax.experimental.pallas import tpu as pltpu
from jax.sharding import PartitionSpec as P

VMEM = pl.BlockSpec(memory_space=pltpu.VMEM)
GRANT = pltpu.CompilerParams(vmem_limit_bytes=16 * 1024 * 1024)
AHEAD = pl.CostEstimate(flops=10**10, bytes_accessed=0, transcendentals=0)
HBM = pl.BlockSpec(memory_space=pltpu.HBM)


def order_matrix(n_expert, pairs, rows, me):
    total = n_expert * pairs * 2 * rows
    core, pair = lax.rem(me, 2), lax.div(me, 2)
    place = lax.broadcasted_iota(jnp.int32, (total, total), 0)
    source = lax.broadcasted_iota(jnp.int32, (total, total), 1)
    row = lax.rem(place, rows)
    k = lax.rem(lax.div(place, rows), n_expert)
    h = lax.rem(lax.div(place, rows * n_expert), pairs)
    sent = lax.div(place, rows * pairs * n_expert)
    block = 2 * lax.rem(pair + h, pairs) + lax.rem(core + sent, 2)
    wanted = (k * pairs * 2 + block) * rows + row
    return jnp.where(source == wanted, 1.0, 0.0).astype(jnp.bfloat16)


def half_kernel(tokens, out, sem):
    half = out.shape[1]
    core = lax.rem(lax.axis_index("etp"), 2)
    cols = pl.ds(pl.multiple_of(core * half, half), half)
    copy = pltpu.make_async_copy(tokens.at[:, cols], out, sem)
    copy.start()
    copy.wait()


def ffn_kernel(n_expert, n_etp, rows, parts, own, *refs):
    near = refs[: n_expert - 1]
    far = refs[n_expert - 1 : 2 * n_expert - 2]
    w_gate, w_up, w_down, kept, sent, x = refs[2 * n_expert - 2 :]
    me = lax.axis_index("etp")
    core = lax.rem(me, 2)
    tok, width = own.shape
    half = width // 2
    step = width // parts
    x[0:tok, :] = own[...]
    mine = pl.ds(pl.multiple_of(core * half, half), half)
    other = pl.ds(pl.multiple_of((1 - core) * half, half), half)
    for k in range(1, n_expert):
        x[k * tok : (k + 1) * tok, mine] = near[k - 1][...]
        x[k * tok : (k + 1) * tok, other] = far[k - 1][...]
    contract = (((1,), (1,)), ((), ()))
    gate = lax.dot_general(w_gate[0], x[...], contract, preferred_element_type=jnp.float32)
    upper = lax.dot_general(w_up[0], x[...], contract, preferred_element_type=jnp.float32)
    hidden = (gate / (1.0 + jnp.exp(-gate)) * upper).astype(jnp.bfloat16)
    order = order_matrix(n_expert, n_etp // 2, rows, me)
    hidden = lax.dot_general(order, hidden, contract, preferred_element_type=jnp.float32)
    hidden = hidden.astype(jnp.bfloat16)
    side = kept.shape[0]
    for c in range(parts):
        cols = slice(c * step, (c + 1) * step)
        out = jnp.dot(hidden, w_down[0, :, cols], preferred_element_type=jnp.float32)
        kept[:, cols] = out[:side]
        sent[:, cols] = out[side:].astype(jnp.bfloat16)


def add_kernel(kept, arrived, own, *pieces):
    span = own.shape[0]
    own[...] = kept[:span, :] + arrived[:span, :].astype(jnp.float32)
    for i, piece in enumerate(pieces):
        at = slice((i + 1) * span, (i + 2) * span)
        piece[...] = (kept[at, :] + arrived[at, :].astype(jnp.float32)).astype(jnp.bfloat16)


def fold_kernel(pairs, own, *refs):
    arrived, pieces = refs[: pairs - 1], refs[pairs - 1 :]
    total = own[...]
    for block in arrived:
        total = total + block[...].astype(jnp.float32)
    rows = pieces[0].shape[0]
    for k, piece in enumerate(pieces):
        piece[...] = total[k * rows : (k + 1) * rows].astype(piece.dtype)


def mix_kernel(n_expert, ids, weights, *refs):
    pieces, out = refs[:-1], refs[-1]
    rows = out.shape[0]
    me, expert = lax.axis_index("etp"), lax.axis_index("expert")
    top, tok = ids.shape

    def column(ref, start, i):
        lane = lax.broadcasted_iota(jnp.int32, (rows, ref.shape[1]), 1)
        row = lax.broadcasted_iota(jnp.int32, (rows, ref.shape[1]), 0)
        values = jnp.where(lane == start + row, ref[i : i + 1, :], 0)
        return jnp.sum(values, axis=1, keepdims=True)

    own_ids = [column(ids, me * rows, i) for i in range(top)]
    own_weights = [column(weights, 0, i) for i in range(top)]
    scale = sum(own_weights)
    total = None
    for k in range(n_expert):
        owner = lax.rem(expert + k, n_expert)
        factor = sum(jnp.where(own_ids[i] == owner, own_weights[i], 0.0) for i in range(top)) / scale
        term = pieces[k][...].astype(jnp.float32) * factor
        total = term if total is None else total + term
    out[...] = total.astype(out.dtype)


def on_device(n_expert, n_etp, tokens, expert_ids, route_weights, w_gate, w_up, w_down):
    tok, width = tokens.shape
    rows = tok // n_etp
    pairs = n_etp // 2
    side = n_expert * tok // 2
    half = width // 2

    own_half = pl.pallas_call(
        half_kernel,
        out_shape=jax.ShapeDtypeStruct((tok, half), tokens.dtype),
        in_specs=[HBM],
        out_specs=VMEM,
        scratch_shapes=[pltpu.SemaphoreType.DMA],
        cost_estimate=AHEAD,
        compiler_params=GRANT,
        name="half",
    )(pltpu.with_memory_space_constraint(tokens, pltpu.HBM))
    near, far = [], []
    swap = [(i, i ^ 1) for i in range(n_etp)]
    for k in range(1, n_expert):
        hop = [(i, (i + k) % n_expert) for i in range(n_expert)]
        near.append(lax.ppermute(own_half, "expert", hop))
    for block in near:
        far.append(lax.ppermute(block, "etp", swap))

    parts = 4
    kept, sent = pl.pallas_call(
        functools.partial(ffn_kernel, n_expert, n_etp, rows, parts),
        out_shape=(
            jax.ShapeDtypeStruct((side, width), jnp.float32),
            jax.ShapeDtypeStruct((side, width), jnp.bfloat16),
        ),
        in_specs=[VMEM] * (2 * n_expert + 2),
        out_specs=(VMEM, VMEM),
        scratch_shapes=[
            pltpu.VMEM((n_expert * tok, width), jnp.bfloat16),
        ],
        compiler_params=GRANT,
        name="ffn",
    )(tokens, *near, *far, w_gate, w_up, w_down)

    arrived = lax.ppermute(sent, "etp", swap)
    block = n_expert * rows
    own, *pieces = pl.pallas_call(
        add_kernel,
        out_shape=[jax.ShapeDtypeStruct((block, width), jnp.float32)]
        + [jax.ShapeDtypeStruct((block, width), jnp.bfloat16)] * (pairs - 1),
        in_specs=[VMEM] * 2,
        out_specs=[VMEM] * pairs,
        compiler_params=GRANT,
        name="add",
    )(kept, arrived)
    landed = []
    for h, piece in enumerate(pieces, 1):
        route = [(t, 2 * ((t // 2 + h) % pairs) + t % 2) for t in range(n_etp)]
        landed.append(lax.ppermute(piece, "etp", route))
    own, *pieces = pl.pallas_call(
        functools.partial(fold_kernel, pairs),
        out_shape=[jax.ShapeDtypeStruct((rows, width), jnp.float32)]
        + [jax.ShapeDtypeStruct((rows, width), jnp.bfloat16)] * (n_expert - 1),
        in_specs=[VMEM] * pairs,
        out_specs=[VMEM] * n_expert,
        compiler_params=GRANT,
        name="fold",
    )(own, *landed)
    landed = [own]
    for k, piece in enumerate(pieces, 1):
        route = [(e, (e - k) % n_expert) for e in range(n_expert)]
        landed.append(lax.ppermute(piece, "expert", route))

    return pl.pallas_call(
        functools.partial(mix_kernel, n_expert),
        out_shape=jax.ShapeDtypeStruct((rows, width), jnp.bfloat16),
        in_specs=[VMEM] * (2 + n_expert),
        out_specs=VMEM,
        compiler_params=GRANT,
        name="mix",
    )(expert_ids.T, route_weights.T, *landed)


def solution(mesh):
    in_specs = (
        P(("group", "expert"), None),
        P(("group", "expert"), None),
        P(("group", "expert", "etp"), None),
        P("expert", "etp", None),
        P("expert", "etp", None),
        P("expert", "etp", None),
    )
    out_specs = P(("group", "expert", "etp"), None)
    return jax.shard_map(
        functools.partial(on_device, mesh.shape["expert"], mesh.shape["etp"]),
        mesh=mesh,
        in_specs=in_specs,
        out_specs=out_specs,
        check_vma=False,
    )
```

```python
import functools

import jax
import jax.numpy as jnp
from jax import lax
from jax.experimental import pallas as pl
from jax.experimental.pallas import tpu as pltpu
from jax.sharding import PartitionSpec as P

VMEM = pl.BlockSpec(memory_space=pltpu.VMEM)
GRANT = pltpu.CompilerParams(vmem_limit_bytes=16 * 1024 * 1024)
AHEAD = pl.CostEstimate(flops=10**10, bytes_accessed=0, transcendentals=0)
HBM = pl.BlockSpec(memory_space=pltpu.HBM)


def order_kernel(n_expert, pairs, rows, out):
    total = out.shape[0]
    me = lax.axis_index("etp")
    core, pair = lax.rem(me, 2), lax.div(me, 2)
    place = lax.broadcasted_iota(jnp.int32, (total, total), 0)
    source = lax.broadcasted_iota(jnp.int32, (total, total), 1)
    row = lax.rem(place, rows)
    k = lax.rem(lax.div(place, rows), n_expert)
    h = lax.rem(lax.div(place, rows * n_expert), pairs)
    sent = lax.div(place, rows * pairs * n_expert)
    block = 2 * lax.rem(pair + h, pairs) + lax.rem(core + sent, 2)
    wanted = (k * pairs * 2 + block) * rows + row
    out[...] = jnp.where(source == wanted, 1.0, 0.0).astype(jnp.bfloat16)


def ffn_kernel(n_expert, parts, own, next_block, order, *refs):
    far = refs[: n_expert - 2]
    w_gate, w_up, w_down, kept, sent, x = refs[n_expert - 2 :]
    core = lax.rem(lax.axis_index("etp"), 2)
    tok, width = own.shape
    step = width // parts
    x[0:tok, :] = own[...]
    x[tok : 2 * tok, :] = next_block[...]
    for i in range(0, n_expert - 2, 2):
        for block, k in ((far[i], i + 2 + core), (far[i + 1], i + 3 - core)):
            x[pl.ds(pl.multiple_of(k * tok, tok), tok), :] = block[...]
    contract = (((1,), (1,)), ((), ()))
    gate = lax.dot_general(w_gate[0], x[...], contract, preferred_element_type=jnp.float32)
    upper = lax.dot_general(w_up[0], x[...], contract, preferred_element_type=jnp.float32)
    hidden = (gate / (1.0 + jnp.exp(-gate)) * upper).astype(jnp.bfloat16)
    hidden = lax.dot_general(order[...], hidden, contract, preferred_element_type=jnp.float32)
    hidden = hidden.astype(jnp.bfloat16)
    side = kept.shape[0]
    for c in range(parts):
        cols = slice(c * step, (c + 1) * step)
        out = jnp.dot(hidden, w_down[0, :, cols], preferred_element_type=jnp.float32)
        kept[:, cols] = out[:side]
        sent[:, cols] = out[side:].astype(jnp.bfloat16)


def add_kernel(kept, arrived, own, *pieces):
    span = own.shape[0]
    own[...] = kept[:span, :] + arrived[:span, :].astype(jnp.float32)
    for i, piece in enumerate(pieces):
        at = slice((i + 1) * span, (i + 2) * span)
        piece[...] = (kept[at, :] + arrived[at, :].astype(jnp.float32)).astype(jnp.bfloat16)


def fold_kernel(pairs, own, *refs):
    arrived, pieces = refs[: pairs - 1], refs[pairs - 1 :]
    total = own[...]
    for block in arrived:
        total = total + block[...].astype(jnp.float32)
    rows = pieces[0].shape[0]
    for k, piece in enumerate(pieces):
        piece[...] = total[k * rows : (k + 1) * rows].astype(piece.dtype)


def mix_kernel(n_expert, ids, weights, *refs):
    pieces, out = refs[:-1], refs[-1]
    rows = out.shape[0]
    me, expert = lax.axis_index("etp"), lax.axis_index("expert")
    top, tok = ids.shape

    def column(ref, start, i):
        lane = lax.broadcasted_iota(jnp.int32, (rows, ref.shape[1]), 1)
        row = lax.broadcasted_iota(jnp.int32, (rows, ref.shape[1]), 0)
        values = jnp.where(lane == start + row, ref[i : i + 1, :], 0)
        return jnp.sum(values, axis=1, keepdims=True)

    own_ids = [column(ids, me * rows, i) for i in range(top)]
    own_weights = [column(weights, 0, i) for i in range(top)]
    scale = sum(own_weights)
    total = None
    for k in range(n_expert):
        owner = lax.bitwise_xor(expert, k)
        factor = sum(jnp.where(own_ids[i] == owner, own_weights[i], 0.0) for i in range(top)) / scale
        term = pieces[k][...].astype(jnp.float32) * factor
        total = term if total is None else total + term
    out[...] = total.astype(out.dtype)


def on_device(n_expert, n_etp, tokens, expert_ids, route_weights, w_gate, w_up, w_down):
    tok, width = tokens.shape
    rows = tok // n_etp
    pairs = n_etp // 2
    side = n_expert * tok // 2

    order = pl.pallas_call(
        functools.partial(order_kernel, n_expert, pairs, rows),
        out_shape=jax.ShapeDtypeStruct((2 * side, 2 * side), jnp.bfloat16),
        out_specs=VMEM,
        cost_estimate=AHEAD,
        compiler_params=GRANT,
        name="order",
    )()
    tokens, order = lax.optimization_barrier((tokens, order))

    swap = [(t, t ^ 1) for t in range(n_etp)]
    far = []
    for k in range(2, n_expert, 2):
        route = [
            (e * n_etp + t, (e ^ (k + t % 2)) * n_etp + t)
            for e in range(n_expert)
            for t in range(n_etp)
        ]
        far.append(lax.ppermute(tokens, ("expert", "etp"), route))
    next_block = lax.ppermute(tokens, "expert", [(e, e ^ 1) for e in range(n_expert)])
    far = [b for block in far for b in (block, lax.ppermute(block, "etp", swap))]

    parts = 4
    kept, sent = pl.pallas_call(
        functools.partial(ffn_kernel, n_expert, parts),
        out_shape=(
            jax.ShapeDtypeStruct((side, width), jnp.float32),
            jax.ShapeDtypeStruct((side, width), jnp.bfloat16),
        ),
        in_specs=[VMEM] * (n_expert + 4),
        out_specs=(VMEM, VMEM),
        scratch_shapes=[
            pltpu.VMEM((n_expert * tok, width), jnp.bfloat16),
        ],
        compiler_params=GRANT,
        name="ffn",
    )(tokens, next_block, order, *far, w_gate, w_up, w_down)

    arrived = lax.ppermute(sent, "etp", swap)
    block = n_expert * rows
    own, *pieces = pl.pallas_call(
        add_kernel,
        out_shape=[jax.ShapeDtypeStruct((block, width), jnp.float32)]
        + [jax.ShapeDtypeStruct((block, width), jnp.bfloat16)] * (pairs - 1),
        in_specs=[VMEM] * 2,
        out_specs=[VMEM] * pairs,
        compiler_params=GRANT,
        name="add",
    )(kept, arrived)
    landed = []
    for h, piece in enumerate(pieces, 1):
        route = [(t, 2 * ((t // 2 + h) % pairs) + t % 2) for t in range(n_etp)]
        landed.append(lax.ppermute(piece, "etp", route))
    own, *pieces = pl.pallas_call(
        functools.partial(fold_kernel, pairs),
        out_shape=[jax.ShapeDtypeStruct((rows, width), jnp.float32)]
        + [jax.ShapeDtypeStruct((rows, width), jnp.bfloat16)] * (n_expert - 1),
        in_specs=[VMEM] * pairs,
        out_specs=[VMEM] * n_expert,
        compiler_params=GRANT,
        name="fold",
    )(own, *landed)
    landed = [own]
    for k, piece in enumerate(pieces, 1):
        route = [(e, e ^ k) for e in range(n_expert)]
        landed.append(lax.ppermute(piece, "expert", route))

    return pl.pallas_call(
        functools.partial(mix_kernel, n_expert),
        out_shape=jax.ShapeDtypeStruct((rows, width), jnp.bfloat16),
        in_specs=[VMEM] * (2 + n_expert),
        out_specs=VMEM,
        compiler_params=GRANT,
        name="mix",
    )(expert_ids.T, route_weights.T, *landed)


def solution(mesh):
    in_specs = (
        P(("group", "expert"), None),
        P(("group", "expert"), None),
        P(("group", "expert", "etp"), None),
        P("expert", "etp", None),
        P("expert", "etp", None),
        P("expert", "etp", None),
    )
    out_specs = P(("group", "expert", "etp"), None)
    return jax.shard_map(
        functools.partial(on_device, mesh.shape["expert"], mesh.shape["etp"]),
        mesh=mesh,
        in_specs=in_specs,
        out_specs=out_specs,
        check_vma=False,
    )
```

```python
import functools

import jax
import jax.numpy as jnp
from jax import lax
from jax.experimental import pallas as pl
from jax.experimental.pallas import tpu as pltpu
from jax.sharding import PartitionSpec as P

VMEM = pl.BlockSpec(memory_space=pltpu.VMEM)
GRANT = pltpu.CompilerParams(vmem_limit_bytes=16 * 1024 * 1024)
AHEAD = pl.CostEstimate(flops=10**10, bytes_accessed=0, transcendentals=0)
HBM = pl.BlockSpec(memory_space=pltpu.HBM)


def order_kernel(n_expert, pairs, rows, out):
    total = out.shape[0]
    me = lax.axis_index("etp")
    core, pair = lax.rem(me, 2), lax.div(me, 2)
    place = lax.broadcasted_iota(jnp.int32, (total, total), 0)
    source = lax.broadcasted_iota(jnp.int32, (total, total), 1)
    half = n_expert // 2
    row = lax.rem(place, rows)
    k = lax.rem(lax.div(place, rows), half)
    h = lax.rem(lax.div(place, rows * half), pairs)
    sent = lax.rem(lax.div(place, rows * half * pairs), 2)
    k = k + half * (1 - lax.div(place, rows * half * pairs * 2))
    block = 2 * lax.rem(pair + h, pairs) + lax.rem(core + sent, 2)
    wanted = (k * pairs * 2 + block) * rows + row
    out[...] = jnp.where(source == wanted, 1.0, 0.0).astype(jnp.bfloat16)


def ffn_kernel(n_expert, parts, own, next_block, order, *refs):
    far = refs[: n_expert - 2]
    w_gate, w_up, w_down, kept, sent, rest, x = refs[n_expert - 2 :]
    core = lax.rem(lax.axis_index("etp"), 2)
    tok = own.shape[0]
    x[0:tok, :] = own[...]
    x[tok : 2 * tok, :] = next_block[...]
    for i in range(0, n_expert - 2, 2):
        for block, k in ((far[i], i + 2 + core), (far[i + 1], i + 3 - core)):
            x[pl.ds(pl.multiple_of(k * tok, tok), tok), :] = block[...]
    contract = (((1,), (1,)), ((), ()))
    gate = lax.dot_general(w_gate[0], x[...], contract, preferred_element_type=jnp.float32)
    upper = lax.dot_general(w_up[0], x[...], contract, preferred_element_type=jnp.float32)
    hidden = (gate / (1.0 + jnp.exp(-gate)) * upper).astype(jnp.bfloat16)
    hidden = lax.dot_general(order[...], hidden, contract, preferred_element_type=jnp.float32)
    hidden = hidden.astype(jnp.bfloat16)
    now = rest.shape[0]
    rest[...] = hidden[now:]
    down(parts, hidden[:now], w_down, kept, sent)


def down(parts, hidden, w_down, kept, sent):
    side, width = kept.shape
    step = width // parts
    for c in range(parts):
        cols = slice(c * step, (c + 1) * step)
        out = jnp.dot(hidden, w_down[0, :, cols], preferred_element_type=jnp.float32)
        kept[:, cols] = out[:side]
        sent[:, cols] = out[side:].astype(jnp.bfloat16)


def down_kernel(parts, hidden, w_down, kept, sent):
    down(parts, hidden[...], w_down, kept, sent)


def add_kernel(kept, arrived, own, *pieces):
    span = own.shape[0]
    own[...] = kept[:span, :] + arrived[:span, :].astype(jnp.float32)
    for i, piece in enumerate(pieces):
        at = slice((i + 1) * span, (i + 2) * span)
        piece[...] = (kept[at, :] + arrived[at, :].astype(jnp.float32)).astype(jnp.bfloat16)


def fold_kernel(pairs, own, *refs):
    arrived, pieces = refs[: pairs - 1], refs[pairs - 1 :]
    total = own[...]
    for block in arrived:
        total = total + block[...].astype(jnp.float32)
    rows = pieces[0].shape[0]
    for k, piece in enumerate(pieces):
        piece[...] = total[k * rows : (k + 1) * rows].astype(piece.dtype)


def mix_kernel(n_expert, ids, weights, *refs):
    pieces, out = refs[:-1], refs[-1]
    rows = out.shape[0]
    me, expert = lax.axis_index("etp"), lax.axis_index("expert")
    top, tok = ids.shape

    def column(ref, start, i):
        lane = lax.broadcasted_iota(jnp.int32, (rows, ref.shape[1]), 1)
        row = lax.broadcasted_iota(jnp.int32, (rows, ref.shape[1]), 0)
        values = jnp.where(lane == start + row, ref[i : i + 1, :], 0)
        return jnp.sum(values, axis=1, keepdims=True)

    own_ids = [column(ids, me * rows, i) for i in range(top)]
    own_weights = [column(weights, 0, i) for i in range(top)]
    scale = sum(own_weights)
    total = None
    for k in range(n_expert):
        owner = lax.bitwise_xor(expert, k)
        factor = sum(jnp.where(own_ids[i] == owner, own_weights[i], 0.0) for i in range(top)) / scale
        term = pieces[k][...].astype(jnp.float32) * factor
        total = term if total is None else total + term
    out[...] = total.astype(out.dtype)


def on_device(n_expert, n_etp, tokens, expert_ids, route_weights, w_gate, w_up, w_down):
    tok, width = tokens.shape
    rows = tok // n_etp
    pairs = n_etp // 2
    side = n_expert * tok // 2

    order = pl.pallas_call(
        functools.partial(order_kernel, n_expert, pairs, rows),
        out_shape=jax.ShapeDtypeStruct((2 * side, 2 * side), jnp.bfloat16),
        out_specs=VMEM,
        cost_estimate=AHEAD,
        compiler_params=GRANT,
        name="order",
    )()
    tokens, order = lax.optimization_barrier((tokens, order))

    swap = [(t, t ^ 1) for t in range(n_etp)]
    far = []
    for k in range(2, n_expert, 2):
        route = [
            (e * n_etp + t, (e ^ (k + t % 2)) * n_etp + t)
            for e in range(n_expert)
            for t in range(n_etp)
        ]
        far.append(lax.ppermute(tokens, ("expert", "etp"), route))
    next_block = lax.ppermute(tokens, "expert", [(e, e ^ 1) for e in range(n_expert)])
    far = [b for block in far for b in (block, lax.ppermute(block, "etp", swap))]

    parts = 4
    halves = [
        jax.ShapeDtypeStruct((side // 2, width), jnp.float32),
        jax.ShapeDtypeStruct((side // 2, width), jnp.bfloat16),
    ]
    far_kept, far_sent, rest = pl.pallas_call(
        functools.partial(ffn_kernel, n_expert, parts),
        out_shape=halves + [jax.ShapeDtypeStruct((side, w_gate.shape[1]), jnp.bfloat16)],
        in_specs=[VMEM] * (n_expert + 4),
        out_specs=[VMEM] * 3,
        scratch_shapes=[pltpu.VMEM((n_expert * tok, width), jnp.bfloat16)],
        compiler_params=GRANT,
        name="ffn",
    )(tokens, next_block, order, *far, w_gate, w_up, w_down)
    near_kept, near_sent = pl.pallas_call(
        functools.partial(down_kernel, parts),
        out_shape=halves,
        in_specs=[VMEM] * 2,
        out_specs=[VMEM] * 2,
        compiler_params=GRANT,
        name="down",
    )(rest, w_down)

    block = n_expert // 2 * rows
    pieces = []
    for kept, sent in ((far_kept, far_sent), (near_kept, near_sent)):
        arrived = lax.ppermute(sent, "etp", swap)
        own, *others = pl.pallas_call(
            add_kernel,
            out_shape=[jax.ShapeDtypeStruct((block, width), jnp.float32)]
            + [jax.ShapeDtypeStruct((block, width), jnp.bfloat16)] * (pairs - 1),
            in_specs=[VMEM] * 2,
            out_specs=[VMEM] * pairs,
            compiler_params=GRANT,
            name="add",
        )(kept, arrived)
        landed = []
        for h, piece in enumerate(others, 1):
            route = [(t, 2 * ((t // 2 + h) % pairs) + t % 2) for t in range(n_etp)]
            landed.append(lax.ppermute(piece, "etp", route))
        folded = pl.pallas_call(
            functools.partial(fold_kernel, pairs),
            out_shape=[jax.ShapeDtypeStruct((rows, width), jnp.bfloat16)] * (n_expert // 2),
            in_specs=[VMEM] * pairs,
            out_specs=[VMEM] * (n_expert // 2),
            compiler_params=GRANT,
            name="fold",
        )(own, *landed)
        pieces = list(folded) + pieces
    landed = []
    for k in range(n_expert - 1, 0, -1):
        landed.insert(0, lax.ppermute(pieces[k], "expert", [(e, e ^ k) for e in range(n_expert)]))
    landed.insert(0, pieces[0])

    return pl.pallas_call(
        functools.partial(mix_kernel, n_expert),
        out_shape=jax.ShapeDtypeStruct((rows, width), jnp.bfloat16),
        in_specs=[VMEM] * (2 + n_expert),
        out_specs=VMEM,
        compiler_params=GRANT,
        name="mix",
    )(expert_ids.T, route_weights.T, *landed)


def solution(mesh):
    in_specs = (
        P(("group", "expert"), None),
        P(("group", "expert"), None),
        P(("group", "expert", "etp"), None),
        P("expert", "etp", None),
        P("expert", "etp", None),
        P("expert", "etp", None),
    )
    out_specs = P(("group", "expert", "etp"), None)
    return jax.shard_map(
        functools.partial(on_device, mesh.shape["expert"], mesh.shape["etp"]),
        mesh=mesh,
        in_specs=in_specs,
        out_specs=out_specs,
        check_vma=False,
    )
```

```python
import functools

import jax
import jax.numpy as jnp
from jax import lax
from jax.experimental import pallas as pl
from jax.experimental.pallas import tpu as pltpu
from jax.sharding import PartitionSpec as P

VMEM = pl.BlockSpec(memory_space=pltpu.VMEM)
GRANT = pltpu.CompilerParams(vmem_limit_bytes=16 * 1024 * 1024)
AHEAD = pl.CostEstimate(flops=10**10, bytes_accessed=0, transcendentals=0)
HBM = pl.BlockSpec(memory_space=pltpu.HBM)


def order_kernel(n_expert, pairs, rows, out):
    total = out.shape[0]
    me = lax.axis_index("etp")
    core, pair = lax.rem(me, 2), lax.div(me, 2)
    place = lax.broadcasted_iota(jnp.int32, (total, total), 0)
    source = lax.broadcasted_iota(jnp.int32, (total, total), 1)
    half, split = n_expert // 2, 2
    row = lax.rem(place, rows)
    k = lax.rem(lax.div(place, rows), half)
    h = lax.rem(lax.div(place, rows * half), pairs)
    sent = lax.rem(lax.div(place, rows * half * pairs), 2)
    k = k + half * (1 - lax.div(place, rows * half * pairs * 2))
    block = 2 * lax.rem(pair + h, pairs) + lax.rem(core + sent, 2)
    wanted = (k * pairs * 2 + block) * rows + row
    out[...] = jnp.where(source == wanted, 1.0, 0.0).astype(jnp.bfloat16)


def ffn_kernel(n_expert, parts, own, next_block, order, *refs):
    far = refs[: n_expert - 2]
    w_gate, w_up, w_down, kept, sent, rest, x = refs[n_expert - 2 :]
    core = lax.rem(lax.axis_index("etp"), 2)
    tok = own.shape[0]
    x[0:tok, :] = own[...]
    x[tok : 2 * tok, :] = next_block[...]
    for i in range(0, n_expert - 2, 2):
        for block, k in ((far[i], i + 2 + core), (far[i + 1], i + 3 - core)):
            x[pl.ds(pl.multiple_of(k * tok, tok), tok), :] = block[...]
    contract = (((1,), (1,)), ((), ()))
    gate = lax.dot_general(w_gate[0], x[...], contract, preferred_element_type=jnp.float32)
    upper = lax.dot_general(w_up[0], x[...], contract, preferred_element_type=jnp.float32)
    hidden = (gate / (1.0 + jnp.exp(-gate)) * upper).astype(jnp.bfloat16)
    hidden = lax.dot_general(order[...], hidden, contract, preferred_element_type=jnp.float32)
    hidden = hidden.astype(jnp.bfloat16)
    now = rest.shape[0]
    rest[...] = hidden[now:]
    down(parts, hidden[:now], w_down, kept, sent)


def down(parts, hidden, w_down, kept, sent):
    side, width = kept.shape
    step = width // parts
    for c in range(parts):
        cols = slice(c * step, (c + 1) * step)
        out = jnp.dot(hidden, w_down[0, :, cols], preferred_element_type=jnp.float32)
        kept[:, cols] = out[:side]
        sent[:, cols] = out[side:].astype(jnp.bfloat16)


def down_kernel(parts, hidden, w_down, kept, sent):
    down(parts, hidden[...], w_down, kept, sent)


def add_kernel(parts, pairs, rows, kept, arrived, *refs):
    count = kept.shape[0] // (pairs * rows)
    take = count // parts
    for h in range(pairs):
        at = slice(h * count * rows, (h + 1) * count * rows)
        total = kept[at, :] + arrived[at, :].astype(jnp.float32)
        for i in range(parts):
            out = refs[i * pairs + h]
            out[...] = total[i * take * rows : (i + 1) * take * rows].astype(out.dtype)


def fold_kernel(pairs, own, *refs):
    arrived, pieces = refs[: pairs - 1], refs[pairs - 1 :]
    total = own[...]
    for block in arrived:
        total = total + block[...].astype(jnp.float32)
    rows = pieces[0].shape[0]
    for k, piece in enumerate(pieces):
        piece[...] = total[k * rows : (k + 1) * rows].astype(piece.dtype)


def mix_kernel(n_expert, ids, weights, *refs):
    pieces, out = refs[:-1], refs[-1]
    rows = out.shape[0]
    me, expert = lax.axis_index("etp"), lax.axis_index("expert")
    top, tok = ids.shape

    def column(ref, start, i):
        lane = lax.broadcasted_iota(jnp.int32, (rows, ref.shape[1]), 1)
        row = lax.broadcasted_iota(jnp.int32, (rows, ref.shape[1]), 0)
        values = jnp.where(lane == start + row, ref[i : i + 1, :], 0)
        return jnp.sum(values, axis=1, keepdims=True)

    own_ids = [column(ids, me * rows, i) for i in range(top)]
    own_weights = [column(weights, 0, i) for i in range(top)]
    scale = sum(own_weights)
    total = None
    for k in range(n_expert):
        owner = lax.bitwise_xor(expert, k)
        factor = sum(jnp.where(own_ids[i] == owner, own_weights[i], 0.0) for i in range(top)) / scale
        term = pieces[k][...].astype(jnp.float32) * factor
        total = term if total is None else total + term
    out[...] = total.astype(out.dtype)


def on_device(n_expert, n_etp, tokens, expert_ids, route_weights, w_gate, w_up, w_down):
    tok, width = tokens.shape
    rows = tok // n_etp
    pairs = n_etp // 2
    side = n_expert * tok // 2

    order = pl.pallas_call(
        functools.partial(order_kernel, n_expert, pairs, rows),
        out_shape=jax.ShapeDtypeStruct((2 * side, 2 * side), jnp.bfloat16),
        out_specs=VMEM,
        cost_estimate=AHEAD,
        compiler_params=GRANT,
        name="order",
    )()
    tokens, order = lax.optimization_barrier((tokens, order))

    swap = [(t, t ^ 1) for t in range(n_etp)]
    far = []
    for k in range(2, n_expert, 2):
        route = [
            (e * n_etp + t, (e ^ (k + t % 2)) * n_etp + t)
            for e in range(n_expert)
            for t in range(n_etp)
        ]
        far.append(lax.ppermute(tokens, ("expert", "etp"), route))
    next_block = lax.ppermute(tokens, "expert", [(e, e ^ 1) for e in range(n_expert)])
    far = [b for block in far for b in (block, lax.ppermute(block, "etp", swap))]

    parts = 4
    halves = [
        jax.ShapeDtypeStruct((side // 2, width), jnp.float32),
        jax.ShapeDtypeStruct((side // 2, width), jnp.bfloat16),
    ]
    far_kept, far_sent, rest = pl.pallas_call(
        functools.partial(ffn_kernel, n_expert, parts),
        out_shape=halves + [jax.ShapeDtypeStruct((side, w_gate.shape[1]), jnp.bfloat16)],
        in_specs=[VMEM] * (n_expert + 4),
        out_specs=[VMEM] * 3,
        scratch_shapes=[pltpu.VMEM((n_expert * tok, width), jnp.bfloat16)],
        compiler_params=GRANT,
        name="ffn",
    )(tokens, next_block, order, *far, w_gate, w_up, w_down)
    near_kept, near_sent = pl.pallas_call(
        functools.partial(down_kernel, parts),
        out_shape=halves,
        in_specs=[VMEM] * 2,
        out_specs=[VMEM] * 2,
        compiler_params=GRANT,
        name="down",
    )(rest, w_down)

    pieces = []
    half, split = n_expert // 2, 2
    for far, sent in ((True, far_sent), (False, near_sent)):
        arrived = lax.ppermute(sent, "etp", swap)
        kept = far_kept if far else near_kept
        take = half // split
        shape = (take * rows, width)
        sums = pl.pallas_call(
            functools.partial(add_kernel, split, pairs, rows),
            out_shape=(
                [jax.ShapeDtypeStruct(shape, jnp.float32)]
                + [jax.ShapeDtypeStruct(shape, jnp.bfloat16)] * (pairs - 1)
            )
            * split,
            in_specs=[VMEM] * 2,
            out_specs=[VMEM] * (pairs * split),
            compiler_params=GRANT,
            name="add",
        )(kept, arrived)
        if far:
            near_kept, sums = lax.optimization_barrier((near_kept, sums))
        folded = []
        for i in range(split):
            own, *others = sums[i * pairs : (i + 1) * pairs]
            landed = []
            for h, piece in enumerate(others, 1):
                route = [(t, 2 * ((t // 2 + h) % pairs) + t % 2) for t in range(n_etp)]
                landed.append(lax.ppermute(piece, "etp", route))
            folded += pl.pallas_call(
                functools.partial(fold_kernel, pairs),
                out_shape=[jax.ShapeDtypeStruct((rows, width), jnp.bfloat16)] * take,
                in_specs=[VMEM] * pairs,
                out_specs=[VMEM] * take,
                compiler_params=GRANT,
                name="fold",
            )(own, *landed)
        pieces = folded + pieces
    landed = []
    for k in range(n_expert - 1, 0, -1):
        landed.insert(0, lax.ppermute(pieces[k], "expert", [(e, e ^ k) for e in range(n_expert)]))
    landed.insert(0, pieces[0])

    return pl.pallas_call(
        functools.partial(mix_kernel, n_expert),
        out_shape=jax.ShapeDtypeStruct((rows, width), jnp.bfloat16),
        in_specs=[VMEM] * (2 + n_expert),
        out_specs=VMEM,
        compiler_params=GRANT,
        name="mix",
    )(expert_ids.T, route_weights.T, *landed)


def solution(mesh):
    in_specs = (
        P(("group", "expert"), None),
        P(("group", "expert"), None),
        P(("group", "expert", "etp"), None),
        P("expert", "etp", None),
        P("expert", "etp", None),
        P("expert", "etp", None),
    )
    out_specs = P(("group", "expert", "etp"), None)
    return jax.shard_map(
        functools.partial(on_device, mesh.shape["expert"], mesh.shape["etp"]),
        mesh=mesh,
        in_specs=in_specs,
        out_specs=out_specs,
        check_vma=False,
    )
```

```python
import functools

import jax
import jax.numpy as jnp
from jax import lax
from jax.experimental import pallas as pl
from jax.experimental.pallas import tpu as pltpu
from jax.sharding import PartitionSpec as P

VMEM = pl.BlockSpec(memory_space=pltpu.VMEM)
GRANT = pltpu.CompilerParams(vmem_limit_bytes=16 * 1024 * 1024)
AHEAD = pl.CostEstimate(flops=10**10, bytes_accessed=0, transcendentals=0)
HBM = pl.BlockSpec(memory_space=pltpu.HBM)


def fetch_kernel(tokens, first, second, mine, sems):
    half = first.shape[1]
    core = lax.rem(lax.axis_index("etp"), 2)
    starts = (0, half, pl.multiple_of(core * half, half))
    copies = [
        pltpu.make_async_copy(tokens.at[:, pl.ds(start, half)], out, sems.at[i])
        for i, (start, out) in enumerate(zip(starts, (first, second, mine)))
    ]
    for copy in copies:
        copy.start()
    for copy in copies:
        copy.wait()


def order_kernel(n_expert, pairs, rows, first, out):
    del first
    total = out.shape[0]
    me = lax.axis_index("etp")
    core, pair = lax.rem(me, 2), lax.div(me, 2)
    place = lax.broadcasted_iota(jnp.int32, (total, total), 0)
    source = lax.broadcasted_iota(jnp.int32, (total, total), 1)
    half = n_expert // 2
    row = lax.rem(place, rows)
    k = lax.rem(lax.div(place, rows), half)
    h = lax.rem(lax.div(place, rows * half), pairs)
    sent = lax.rem(lax.div(place, rows * half * pairs), 2)
    k = k + half * (1 - lax.div(place, rows * half * pairs * 2))
    block = 2 * lax.rem(pair + h, pairs) + lax.rem(core + sent, 2)
    wanted = (k * pairs * 2 + block) * rows + row
    out[...] = jnp.where(source == wanted, 1.0, 0.0).astype(jnp.bfloat16)


CONTRACT = (((1,), (1,)), ((), ()))


def gate_up(part, own, next_block, next_swapped, far, w_gate, w_up, x):
    core = lax.rem(lax.axis_index("etp"), 2)
    tok, half = own.shape
    x[0:tok, :] = own[...]
    x[tok : 2 * tok, :] = jnp.where(core == part, next_block[...], next_swapped[...])
    for i in range(0, len(far), 2):
        for block, k in ((far[i], i + 2 + core), (far[i + 1], i + 3 - core)):
            x[pl.ds(pl.multiple_of(k * tok, tok), tok), :] = block[...]
    cols = slice(part * half, (part + 1) * half)
    return [
        lax.dot_general(w[0, :, cols], x[...], CONTRACT, preferred_element_type=jnp.float32)
        for w in (w_gate, w_up)
    ]


def first_kernel(own, next_block, next_swapped, *refs):
    far, (w_gate, w_up, gate, upper, x) = refs[:-5], refs[-5:]
    gate[...], upper[...] = gate_up(
        0, own, next_block, next_swapped, far, w_gate, w_up, x
    )


def second_kernel(parts, own, next_block, next_swapped, *refs):
    far, refs = refs[:-10], refs[-10:]
    w_gate, w_up, gate, upper, order, w_down, kept, sent, rest, x = refs
    more_gate, more_upper = gate_up(1, own, next_block, next_swapped, far, w_gate, w_up, x)
    gate = gate[...] + more_gate
    upper = upper[...] + more_upper
    hidden = (gate / (1.0 + jnp.exp(-gate)) * upper).astype(jnp.bfloat16)
    hidden = lax.dot_general(order[...], hidden, CONTRACT, preferred_element_type=jnp.float32)
    hidden = hidden.astype(jnp.bfloat16)
    now = rest.shape[0]
    rest[...] = hidden[now:]
    down(parts, hidden[:now], w_down, kept, sent)


def down(parts, hidden, w_down, kept, sent):
    side, width = kept.shape
    step = width // parts
    for c in range(parts):
        cols = slice(c * step, (c + 1) * step)
        out = jnp.dot(hidden, w_down[0, :, cols], preferred_element_type=jnp.float32)
        kept[:, cols] = out[:side]
        sent[:, cols] = out[side:].astype(jnp.bfloat16)


def down_kernel(parts, hidden, w_down, kept, sent):
    down(parts, hidden[...], w_down, kept, sent)


def add_kernel(kept, arrived, own, *pieces):
    span = own.shape[0]
    own[...] = kept[:span, :] + arrived[:span, :].astype(jnp.float32)
    for i, piece in enumerate(pieces):
        at = slice((i + 1) * span, (i + 2) * span)
        piece[...] = (kept[at, :] + arrived[at, :].astype(jnp.float32)).astype(jnp.bfloat16)


def fold_kernel(pairs, own, *refs):
    arrived, pieces = refs[: pairs - 1], refs[pairs - 1 :]
    total = own[...]
    for block in arrived:
        total = total + block[...].astype(jnp.float32)
    rows = pieces[0].shape[0]
    for k, piece in enumerate(pieces):
        piece[...] = total[k * rows : (k + 1) * rows].astype(piece.dtype)


def mix_kernel(n_expert, ids, weights, *refs):
    pieces, out = refs[:-1], refs[-1]
    rows = out.shape[0]
    me, expert = lax.axis_index("etp"), lax.axis_index("expert")
    top, tok = ids.shape

    def column(ref, start, i):
        lane = lax.broadcasted_iota(jnp.int32, (rows, ref.shape[1]), 1)
        row = lax.broadcasted_iota(jnp.int32, (rows, ref.shape[1]), 0)
        values = jnp.where(lane == start + row, ref[i : i + 1, :], 0)
        return jnp.sum(values, axis=1, keepdims=True)

    own_ids = [column(ids, me * rows, i) for i in range(top)]
    own_weights = [column(weights, 0, i) for i in range(top)]
    scale = sum(own_weights)
    total = None
    for k in range(n_expert):
        owner = lax.bitwise_xor(expert, k)
        factor = sum(jnp.where(own_ids[i] == owner, own_weights[i], 0.0) for i in range(top)) / scale
        term = pieces[k][...].astype(jnp.float32) * factor
        total = term if total is None else total + term
    out[...] = total.astype(out.dtype)


def on_device(n_expert, n_etp, tokens, expert_ids, route_weights, w_gate, w_up, w_down):
    tok, width = tokens.shape
    rows = tok // n_etp
    pairs = n_etp // 2
    side = n_expert * tok // 2

    column_half = jax.ShapeDtypeStruct((tok, width // 2), tokens.dtype)
    first, second, mine = pl.pallas_call(
        fetch_kernel,
        out_shape=[column_half] * 3,
        in_specs=[HBM],
        out_specs=[VMEM] * 3,
        scratch_shapes=[pltpu.SemaphoreType.DMA((3,))],
        compiler_params=GRANT,
        name="fetch",
    )(pltpu.with_memory_space_constraint(tokens, pltpu.HBM))
    order = pl.pallas_call(
        functools.partial(order_kernel, n_expert, pairs, rows),
        out_shape=jax.ShapeDtypeStruct((2 * side, 2 * side), jnp.bfloat16),
        in_specs=[VMEM],
        out_specs=VMEM,
        cost_estimate=AHEAD,
        compiler_params=GRANT,
        name="order",
    )(first)
    first, second, mine, order = lax.optimization_barrier((first, second, mine, order))

    swap = [(t, t ^ 1) for t in range(n_etp)]
    routes = [
        [
            (e * n_etp + t, (e ^ (k + t % 2)) * n_etp + t)
            for e in range(n_expert)
            for t in range(n_etp)
        ]
        for k in range(2, n_expert, 2)
    ]

    def exchange(block, axes, route):
        block = lax.ppermute(block, axes, route)
        return [block, lax.ppermute(block, "etp", swap)]

    far_first = [b for route in routes for b in exchange(first, ("expert", "etp"), route)]
    near = exchange(mine, "expert", [(e, e ^ 1) for e in range(n_expert)])
    far_second = [b for route in routes for b in exchange(second, ("expert", "etp"), route)]

    parts = 4
    hidden = w_gate.shape[1]
    scratch = [pltpu.VMEM((n_expert * tok, width // 2), jnp.bfloat16)]
    gate, upper = pl.pallas_call(
        first_kernel,
        out_shape=[jax.ShapeDtypeStruct((hidden, n_expert * tok), jnp.float32)] * 2,
        in_specs=[VMEM] * (n_expert + 3),
        out_specs=[VMEM] * 2,
        scratch_shapes=scratch,
        compiler_params=GRANT,
        name="first",
    )(first, *near, *far_first, w_gate, w_up)
    halves = [
        jax.ShapeDtypeStruct((side // 2, width), jnp.float32),
        jax.ShapeDtypeStruct((side // 2, width), jnp.bfloat16),
    ]
    far_kept, far_sent, rest = pl.pallas_call(
        functools.partial(second_kernel, parts),
        out_shape=halves + [jax.ShapeDtypeStruct((side, hidden), jnp.bfloat16)],
        in_specs=[VMEM] * (n_expert + 7),
        out_specs=[VMEM] * 3,
        scratch_shapes=scratch,
        compiler_params=GRANT,
        name="second",
    )(second, *near, *far_second, w_gate, w_up, gate, upper, order, w_down)
    near_kept, near_sent = pl.pallas_call(
        functools.partial(down_kernel, parts),
        out_shape=halves,
        in_specs=[VMEM] * 2,
        out_specs=[VMEM] * 2,
        compiler_params=GRANT,
        name="down",
    )(rest, w_down)

    block = n_expert // 2 * rows
    pieces = []
    for kept, sent in ((far_kept, far_sent), (near_kept, near_sent)):
        arrived = lax.ppermute(sent, "etp", swap)
        own, *others = pl.pallas_call(
            add_kernel,
            out_shape=[jax.ShapeDtypeStruct((block, width), jnp.float32)]
            + [jax.ShapeDtypeStruct((block, width), jnp.bfloat16)] * (pairs - 1),
            in_specs=[VMEM] * 2,
            out_specs=[VMEM] * pairs,
            compiler_params=GRANT,
            name="add",
        )(kept, arrived)
        landed = []
        for h, piece in enumerate(others, 1):
            route = [(t, 2 * ((t // 2 + h) % pairs) + t % 2) for t in range(n_etp)]
            landed.append(lax.ppermute(piece, "etp", route))
        folded = pl.pallas_call(
            functools.partial(fold_kernel, pairs),
            out_shape=[jax.ShapeDtypeStruct((rows, width), jnp.bfloat16)] * (n_expert // 2),
            in_specs=[VMEM] * pairs,
            out_specs=[VMEM] * (n_expert // 2),
            compiler_params=GRANT,
            name="fold",
        )(own, *landed)
        pieces = list(folded) + pieces
    landed = []
    for k in range(n_expert - 1, 0, -1):
        landed.insert(0, lax.ppermute(pieces[k], "expert", [(e, e ^ k) for e in range(n_expert)]))
    landed.insert(0, pieces[0])

    return pl.pallas_call(
        functools.partial(mix_kernel, n_expert),
        out_shape=jax.ShapeDtypeStruct((rows, width), jnp.bfloat16),
        in_specs=[VMEM] * (2 + n_expert),
        out_specs=VMEM,
        compiler_params=GRANT,
        name="mix",
    )(expert_ids.T, route_weights.T, *landed)


def solution(mesh):
    in_specs = (
        P(("group", "expert"), None),
        P(("group", "expert"), None),
        P(("group", "expert", "etp"), None),
        P("expert", "etp", None),
        P("expert", "etp", None),
        P("expert", "etp", None),
    )
    out_specs = P(("group", "expert", "etp"), None)
    return jax.shard_map(
        functools.partial(on_device, mesh.shape["expert"], mesh.shape["etp"]),
        mesh=mesh,
        in_specs=in_specs,
        out_specs=out_specs,
        check_vma=False,
    )
```

```python
import functools

import jax
import jax.numpy as jnp
from jax import lax
from jax.experimental import pallas as pl
from jax.experimental.pallas import tpu as pltpu
from jax.sharding import PartitionSpec as P

VMEM = pl.BlockSpec(memory_space=pltpu.VMEM)
GRANT = pltpu.CompilerParams(vmem_limit_bytes=16 * 1024 * 1024)
AHEAD = pl.CostEstimate(flops=10**10, bytes_accessed=0, transcendentals=0)
HBM = pl.BlockSpec(memory_space=pltpu.HBM)


def fetch_kernel(tokens, own, mine, sems):
    half = mine.shape[1]
    core = lax.rem(lax.axis_index("etp"), 2)
    cols = pl.ds(pl.multiple_of(core * half, half), half)
    copies = [
        pltpu.make_async_copy(tokens.at[:, cols], mine, sems.at[0]),
        pltpu.make_async_copy(tokens, own, sems.at[1]),
    ]
    for copy in copies:
        copy.start()
    for copy in copies:
        copy.wait()


def order_kernel(n_expert, pairs, rows, mine, out):
    del mine
    total = out.shape[0]
    me = lax.axis_index("etp")
    core, pair = lax.rem(me, 2), lax.div(me, 2)
    place = lax.broadcasted_iota(jnp.int32, (total, total), 0)
    source = lax.broadcasted_iota(jnp.int32, (total, total), 1)
    half = n_expert // 2
    row = lax.rem(place, rows)
    k = lax.rem(lax.div(place, rows), half)
    h = lax.rem(lax.div(place, rows * half), pairs)
    sent = lax.rem(lax.div(place, rows * half * pairs), 2)
    k = k + half * (1 - lax.div(place, rows * half * pairs * 2))
    block = 2 * lax.rem(pair + h, pairs) + lax.rem(core + sent, 2)
    wanted = (k * pairs * 2 + block) * rows + row
    out[...] = jnp.where(source == wanted, 1.0, 0.0).astype(jnp.bfloat16)


def ffn_kernel(n_expert, parts, own, next_block, next_swapped, order, *refs):
    far = refs[: n_expert - 2]
    w_gate, w_up, w_down, kept, sent, rest, x = refs[n_expert - 2 :]
    core = lax.rem(lax.axis_index("etp"), 2)
    tok = own.shape[0]
    x[0:tok, :] = own[...]
    half = next_block.shape[1]
    for block, side in ((next_block, core), (next_swapped, 1 - core)):
        x[tok : 2 * tok, pl.ds(pl.multiple_of(side * half, half), half)] = block[...]
    for i in range(0, n_expert - 2, 2):
        for block, k in ((far[i], i + 2 + core), (far[i + 1], i + 3 - core)):
            x[pl.ds(pl.multiple_of(k * tok, tok), tok), :] = block[...]
    contract = (((1,), (1,)), ((), ()))
    gate = lax.dot_general(w_gate[0], x[...], contract, preferred_element_type=jnp.float32)
    upper = lax.dot_general(w_up[0], x[...], contract, preferred_element_type=jnp.float32)
    hidden = (gate / (1.0 + jnp.exp(-gate)) * upper).astype(jnp.bfloat16)
    hidden = lax.dot_general(order[...], hidden, contract, preferred_element_type=jnp.float32)
    hidden = hidden.astype(jnp.bfloat16)
    now = rest.shape[0]
    rest[...] = hidden[now:]
    down(parts, hidden[:now], w_down, kept, sent)


def down(parts, hidden, w_down, kept, sent):
    side, width = kept.shape
    step = width // parts
    for c in range(parts):
        cols = slice(c * step, (c + 1) * step)
        out = jnp.dot(hidden, w_down[0, :, cols], preferred_element_type=jnp.float32)
        kept[:, cols] = out[:side]
        sent[:, cols] = out[side:].astype(jnp.bfloat16)


def down_kernel(parts, hidden, w_down, kept, sent):
    down(parts, hidden[...], w_down, kept, sent)


def add_kernel(kept, arrived, own, *pieces):
    span = own.shape[0]
    own[...] = kept[:span, :] + arrived[:span, :].astype(jnp.float32)
    for i, piece in enumerate(pieces):
        at = slice((i + 1) * span, (i + 2) * span)
        piece[...] = (kept[at, :] + arrived[at, :].astype(jnp.float32)).astype(jnp.bfloat16)


def fold_kernel(pairs, own, *refs):
    arrived, pieces = refs[: pairs - 1], refs[pairs - 1 :]
    total = own[...]
    for block in arrived:
        total = total + block[...].astype(jnp.float32)
    rows = pieces[0].shape[0]
    for k, piece in enumerate(pieces):
        piece[...] = total[k * rows : (k + 1) * rows].astype(piece.dtype)


def mix_kernel(n_expert, ids, weights, *refs):
    pieces, out = refs[:-1], refs[-1]
    rows = out.shape[0]
    me, expert = lax.axis_index("etp"), lax.axis_index("expert")
    top, tok = ids.shape

    def column(ref, start, i):
        lane = lax.broadcasted_iota(jnp.int32, (rows, ref.shape[1]), 1)
        row = lax.broadcasted_iota(jnp.int32, (rows, ref.shape[1]), 0)
        values = jnp.where(lane == start + row, ref[i : i + 1, :], 0)
        return jnp.sum(values, axis=1, keepdims=True)

    own_ids = [column(ids, me * rows, i) for i in range(top)]
    own_weights = [column(weights, 0, i) for i in range(top)]
    scale = sum(own_weights)
    total = None
    for k in range(n_expert):
        owner = lax.bitwise_xor(expert, k)
        factor = sum(jnp.where(own_ids[i] == owner, own_weights[i], 0.0) for i in range(top)) / scale
        term = pieces[k][...].astype(jnp.float32) * factor
        total = term if total is None else total + term
    out[...] = total.astype(out.dtype)


def on_device(n_expert, n_etp, tokens, expert_ids, route_weights, w_gate, w_up, w_down):
    tok, width = tokens.shape
    rows = tok // n_etp
    pairs = n_etp // 2
    side = n_expert * tok // 2

    own, mine = pl.pallas_call(
        fetch_kernel,
        out_shape=[
            jax.ShapeDtypeStruct((tok, width), tokens.dtype),
            jax.ShapeDtypeStruct((tok, width // 2), tokens.dtype),
        ],
        in_specs=[HBM],
        out_specs=[VMEM] * 2,
        scratch_shapes=[pltpu.SemaphoreType.DMA((2,))],
        compiler_params=GRANT,
        name="fetch",
    )(pltpu.with_memory_space_constraint(tokens, pltpu.HBM))
    order = pl.pallas_call(
        functools.partial(order_kernel, n_expert, pairs, rows),
        out_shape=jax.ShapeDtypeStruct((2 * side, 2 * side), jnp.bfloat16),
        in_specs=[VMEM],
        out_specs=VMEM,
        cost_estimate=AHEAD,
        compiler_params=GRANT,
        name="order",
    )(mine)
    mine, order = lax.optimization_barrier((mine, order))

    swap = [(t, t ^ 1) for t in range(n_etp)]
    far = []
    for k in range(2, n_expert, 2):
        route = [
            (e * n_etp + t, (e ^ (k + t % 2)) * n_etp + t)
            for e in range(n_expert)
            for t in range(n_etp)
        ]
        far.append(lax.ppermute(tokens, ("expert", "etp"), route))
    next_block = lax.ppermute(mine, "expert", [(e, e ^ 1) for e in range(n_expert)])
    near = [next_block, lax.ppermute(next_block, "etp", swap)]
    far = [b for block in far for b in (block, lax.ppermute(block, "etp", swap))]

    parts = 4
    halves = [
        jax.ShapeDtypeStruct((side // 2, width), jnp.float32),
        jax.ShapeDtypeStruct((side // 2, width), jnp.bfloat16),
    ]
    far_kept, far_sent, rest = pl.pallas_call(
        functools.partial(ffn_kernel, n_expert, parts),
        out_shape=halves + [jax.ShapeDtypeStruct((side, w_gate.shape[1]), jnp.bfloat16)],
        in_specs=[VMEM] * (n_expert + 5),
        out_specs=[VMEM] * 3,
        scratch_shapes=[pltpu.VMEM((n_expert * tok, width), jnp.bfloat16)],
        compiler_params=GRANT,
        name="ffn",
    )(own, *near, order, *far, w_gate, w_up, w_down)
    near_kept, near_sent = pl.pallas_call(
        functools.partial(down_kernel, parts),
        out_shape=halves,
        in_specs=[VMEM] * 2,
        out_specs=[VMEM] * 2,
        compiler_params=GRANT,
        name="down",
    )(rest, w_down)

    block = n_expert // 2 * rows
    pieces = []
    for kept, sent in ((far_kept, far_sent), (near_kept, near_sent)):
        arrived = lax.ppermute(sent, "etp", swap)
        own, *others = pl.pallas_call(
            add_kernel,
            out_shape=[jax.ShapeDtypeStruct((block, width), jnp.float32)]
            + [jax.ShapeDtypeStruct((block, width), jnp.bfloat16)] * (pairs - 1),
            in_specs=[VMEM] * 2,
            out_specs=[VMEM] * pairs,
            compiler_params=GRANT,
            name="add",
        )(kept, arrived)
        landed = []
        for h, piece in enumerate(others, 1):
            route = [(t, 2 * ((t // 2 + h) % pairs) + t % 2) for t in range(n_etp)]
            landed.append(lax.ppermute(piece, "etp", route))
        folded = pl.pallas_call(
            functools.partial(fold_kernel, pairs),
            out_shape=[jax.ShapeDtypeStruct((rows, width), jnp.bfloat16)] * (n_expert // 2),
            in_specs=[VMEM] * pairs,
            out_specs=[VMEM] * (n_expert // 2),
            compiler_params=GRANT,
            name="fold",
        )(own, *landed)
        pieces = list(folded) + pieces
    landed = []
    for k in range(n_expert - 1, 0, -1):
        landed.insert(0, lax.ppermute(pieces[k], "expert", [(e, e ^ k) for e in range(n_expert)]))
    landed.insert(0, pieces[0])

    return pl.pallas_call(
        functools.partial(mix_kernel, n_expert),
        out_shape=jax.ShapeDtypeStruct((rows, width), jnp.bfloat16),
        in_specs=[VMEM] * (2 + n_expert),
        out_specs=VMEM,
        compiler_params=GRANT,
        name="mix",
    )(expert_ids.T, route_weights.T, *landed)


def solution(mesh):
    in_specs = (
        P(("group", "expert"), None),
        P(("group", "expert"), None),
        P(("group", "expert", "etp"), None),
        P("expert", "etp", None),
        P("expert", "etp", None),
        P("expert", "etp", None),
    )
    out_specs = P(("group", "expert", "etp"), None)
    return jax.shard_map(
        functools.partial(on_device, mesh.shape["expert"], mesh.shape["etp"]),
        mesh=mesh,
        in_specs=in_specs,
        out_specs=out_specs,
        check_vma=False,
    )
```

```python
import functools

import jax
import jax.numpy as jnp
from jax import lax
from jax.experimental import pallas as pl
from jax.experimental.pallas import tpu as pltpu
from jax.sharding import PartitionSpec as P

VMEM = pl.BlockSpec(memory_space=pltpu.VMEM)
GRANT = pltpu.CompilerParams(vmem_limit_bytes=16 * 1024 * 1024)
AHEAD = pl.CostEstimate(flops=10**10, bytes_accessed=0, transcendentals=0)
HBM = pl.BlockSpec(memory_space=pltpu.HBM)


def fetch_kernel(tokens, share, first, *refs):
    quarters, sems = refs[:4], refs[4]
    half, part, wide = first.shape[1], share.shape[1], quarters[0].shape[1]
    me = lax.axis_index("etp")
    core, pair = lax.rem(me, 2), lax.div(me, 2)
    moves = [
        (share, pl.multiple_of(pair * part, part)),
        (quarters[0], half),
        (quarters[1], half + wide),
        (quarters[2], pl.multiple_of(core * half, wide)),
        (quarters[3], pl.multiple_of(core * half + wide, wide)),
        (first, 0),
    ]
    copies = [
        pltpu.make_async_copy(tokens.at[:, pl.ds(start, out.shape[1])], out, sems.at[i])
        for i, (out, start) in enumerate(moves)
    ]
    for copy in copies:
        copy.start()
    for copy in copies:
        copy.wait()


def order_kernel(n_expert, pairs, rows, first, out):
    del first
    total = out.shape[0]
    me = lax.axis_index("etp")
    core, pair = lax.rem(me, 2), lax.div(me, 2)
    place = lax.broadcasted_iota(jnp.int32, (total, total), 0)
    source = lax.broadcasted_iota(jnp.int32, (total, total), 1)
    half = n_expert // 2
    row = lax.rem(place, rows)
    k = lax.rem(lax.div(place, rows), half)
    h = lax.rem(lax.div(place, rows * half), pairs)
    sent = lax.rem(lax.div(place, rows * half * pairs), 2)
    k = k + half * (1 - lax.div(place, rows * half * pairs * 2))
    block = 2 * lax.rem(pair + h, pairs) + lax.rem(core + sent, 2)
    wanted = (k * pairs * 2 + block) * rows + row
    out[...] = jnp.where(source == wanted, 1.0, 0.0).astype(jnp.bfloat16)


CONTRACT = (((1,), (1,)), ((), ()))


def gate_up(part, own, near, far, w_gate, w_up, x):
    core = lax.rem(lax.axis_index("etp"), 2)
    tok, half = own[0].shape[0], x.shape[1]
    for i, block in enumerate(own):
        wide = block.shape[1]
        x[0:tok, i * wide : (i + 1) * wide] = block[...]
    wide = near[0].shape[1]
    for i in range(2):
        x[tok : 2 * tok, i * wide : (i + 1) * wide] = jnp.where(
            core == part, near[i][...], near[2 + i][...]
        )
    for block, swapped, two, start in far:
        wide = block.shape[1]
        cols = pl.ds(start if isinstance(start, int) else pl.multiple_of(start, wide), wide)
        for ref, k in ((block, 2 * two + 2 + core), (swapped, 2 * two + 3 - core)):
            x[pl.ds(pl.multiple_of(k * tok, tok), tok), cols] = ref[...]
    cols = slice(part * half, (part + 1) * half)
    return [
        lax.dot_general(w[0, :, cols], x[...], CONTRACT, preferred_element_type=jnp.float32)
        for w in (w_gate, w_up)
    ]


def first_kernel(pairs, own, *refs):
    near, far, (w_gate, w_up, gate, upper, x) = refs[:4], refs[4:-5], refs[-5:]
    pair = lax.div(lax.axis_index("etp"), 2)
    wide = far[0].shape[1]
    placed = []
    for i in range(0, len(far), 2):
        two, h = divmod(i // 2, pairs)
        placed.append((far[i], far[i + 1], two, lax.rem(pair - h + pairs, pairs) * wide))
    gate[...], upper[...] = gate_up(0, [own], near, placed, w_gate, w_up, x)


def second_kernel(parts, *refs):
    own, near, far, refs = refs[:2], refs[2:6], refs[6:-10], refs[-10:]
    w_gate, w_up, gate, upper, order, w_down, kept, sent, rest, x = refs
    wide = far[0].shape[1]
    placed = [(far[i], far[i + 1], i // 4, i // 2 % 2 * wide) for i in range(0, len(far), 2)]
    more_gate, more_upper = gate_up(1, own, near, placed, w_gate, w_up, x)
    gate = gate[...] + more_gate
    upper = upper[...] + more_upper
    hidden = (gate / (1.0 + jnp.exp(-gate)) * upper).astype(jnp.bfloat16)
    hidden = lax.dot_general(order[...], hidden, CONTRACT, preferred_element_type=jnp.float32)
    hidden = hidden.astype(jnp.bfloat16)
    now = rest.shape[0]
    rest[...] = hidden[now:]
    down(parts, hidden[:now], w_down, kept, sent)


def down(parts, hidden, w_down, kept, sent):
    side, width = kept.shape
    step = width // parts
    for c in range(parts):
        cols = slice(c * step, (c + 1) * step)
        out = jnp.dot(hidden, w_down[0, :, cols], preferred_element_type=jnp.float32)
        kept[:, cols] = out[:side]
        sent[:, cols] = out[side:].astype(jnp.bfloat16)


def down_kernel(parts, hidden, w_down, kept, sent):
    down(parts, hidden[...], w_down, kept, sent)


def add_kernel(kept, arrived, own, *pieces):
    span = own.shape[0]
    own[...] = kept[:span, :] + arrived[:span, :].astype(jnp.float32)
    for i, piece in enumerate(pieces):
        at = slice((i + 1) * span, (i + 2) * span)
        piece[...] = (kept[at, :] + arrived[at, :].astype(jnp.float32)).astype(jnp.bfloat16)


def fold_kernel(pairs, own, *refs):
    arrived, pieces = refs[: pairs - 1], refs[pairs - 1 :]
    total = own[...]
    for block in arrived:
        total = total + block[...].astype(jnp.float32)
    rows = pieces[0].shape[0]
    for k, piece in enumerate(pieces):
        piece[...] = total[k * rows : (k + 1) * rows].astype(piece.dtype)


def mix_kernel(n_expert, ids, weights, *refs):
    pieces, out = refs[:-1], refs[-1]
    rows = out.shape[0]
    me, expert = lax.axis_index("etp"), lax.axis_index("expert")
    top, tok = ids.shape

    def column(ref, start, i):
        lane = lax.broadcasted_iota(jnp.int32, (rows, ref.shape[1]), 1)
        row = lax.broadcasted_iota(jnp.int32, (rows, ref.shape[1]), 0)
        values = jnp.where(lane == start + row, ref[i : i + 1, :], 0)
        return jnp.sum(values, axis=1, keepdims=True)

    own_ids = [column(ids, me * rows, i) for i in range(top)]
    own_weights = [column(weights, 0, i) for i in range(top)]
    scale = sum(own_weights)
    total = None
    for k in range(n_expert):
        owner = lax.bitwise_xor(expert, k)
        factor = sum(jnp.where(own_ids[i] == owner, own_weights[i], 0.0) for i in range(top)) / scale
        term = pieces[k][...].astype(jnp.float32) * factor
        total = term if total is None else total + term
    out[...] = total.astype(out.dtype)


def on_device(n_expert, n_etp, tokens, expert_ids, route_weights, w_gate, w_up, w_down):
    tok, width = tokens.shape
    rows = tok // n_etp
    pairs = n_etp // 2
    side = n_expert * tok // 2

    def columns(count):
        return jax.ShapeDtypeStruct((tok, count), tokens.dtype)

    half, quarter = width // 2, width // 4
    share, first, *quarters = pl.pallas_call(
        fetch_kernel,
        out_shape=[columns(half // pairs), columns(half)] + [columns(quarter)] * 4,
        in_specs=[HBM],
        out_specs=[VMEM] * 6,
        scratch_shapes=[pltpu.SemaphoreType.DMA((6,))],
        compiler_params=GRANT,
        name="fetch",
    )(pltpu.with_memory_space_constraint(tokens, pltpu.HBM))
    order = pl.pallas_call(
        functools.partial(order_kernel, n_expert, pairs, rows),
        out_shape=jax.ShapeDtypeStruct((2 * side, 2 * side), jnp.bfloat16),
        in_specs=[VMEM],
        out_specs=VMEM,
        cost_estimate=AHEAD,
        compiler_params=GRANT,
        name="order",
    )(first)
    quarters, order = lax.optimization_barrier((quarters, order))

    swap = [(t, t ^ 1) for t in range(n_etp)]
    routes = [
        [
            (e * n_etp + t, (e ^ (k + t % 2)) * n_etp + t)
            for e in range(n_expert)
            for t in range(n_etp)
        ]
        for k in range(2, n_expert, 2)
    ]

    def exchange(block, axes, route):
        block = lax.ppermute(block, axes, route)
        return [block, lax.ppermute(block, "etp", swap)]

    turns = [
        [(t, 2 * ((t // 2 + h) % pairs) + t % 2) for t in range(n_etp)] for h in range(1, pairs)
    ]
    far_first, far_second = [], []
    for route in routes:
        block = lax.ppermute(share, ("expert", "etp"), route)
        for piece in [block] + [lax.ppermute(block, "etp", turn) for turn in turns]:
            far_first += [piece, lax.ppermute(piece, "etp", swap)]
        for piece in quarters[:2]:
            far_second += exchange(piece, ("expert", "etp"), route)
    next_route = [(e, e ^ 1) for e in range(n_expert)]
    near = [exchange(piece, "expert", next_route) for piece in quarters[2:]]
    near = [near[0][0], near[1][0], near[0][1], near[1][1]]

    parts = 4
    hidden = w_gate.shape[1]
    scratch = [pltpu.VMEM((n_expert * tok, width // 2), jnp.bfloat16)]
    gate, upper = pl.pallas_call(
        functools.partial(first_kernel, pairs),
        out_shape=[jax.ShapeDtypeStruct((hidden, n_expert * tok), jnp.float32)] * 2,
        in_specs=[VMEM] * (7 + len(far_first)),
        out_specs=[VMEM] * 2,
        scratch_shapes=scratch,
        compiler_params=GRANT,
        name="first",
    )(first, *near, *far_first, w_gate, w_up)
    halves = [
        jax.ShapeDtypeStruct((side // 2, width), jnp.float32),
        jax.ShapeDtypeStruct((side // 2, width), jnp.bfloat16),
    ]
    far_kept, far_sent, rest = pl.pallas_call(
        functools.partial(second_kernel, parts),
        out_shape=halves + [jax.ShapeDtypeStruct((side, hidden), jnp.bfloat16)],
        in_specs=[VMEM] * (12 + len(far_second)),
        out_specs=[VMEM] * 3,
        scratch_shapes=scratch,
        compiler_params=GRANT,
        name="second",
    )(*quarters[:2], *near, *far_second, w_gate, w_up, gate, upper, order, w_down)
    near_kept, near_sent = pl.pallas_call(
        functools.partial(down_kernel, parts),
        out_shape=halves,
        in_specs=[VMEM] * 2,
        out_specs=[VMEM] * 2,
        compiler_params=GRANT,
        name="down",
    )(rest, w_down)

    block = n_expert // 2 * rows
    pieces = []
    for kept, sent in ((far_kept, far_sent), (near_kept, near_sent)):
        arrived = lax.ppermute(sent, "etp", swap)
        own, *others = pl.pallas_call(
            add_kernel,
            out_shape=[jax.ShapeDtypeStruct((block, width), jnp.float32)]
            + [jax.ShapeDtypeStruct((block, width), jnp.bfloat16)] * (pairs - 1),
            in_specs=[VMEM] * 2,
            out_specs=[VMEM] * pairs,
            compiler_params=GRANT,
            name="add",
        )(kept, arrived)
        landed = [lax.ppermute(piece, "etp", turn) for piece, turn in zip(others, turns)]
        folded = pl.pallas_call(
            functools.partial(fold_kernel, pairs),
            out_shape=[jax.ShapeDtypeStruct((rows, width), jnp.bfloat16)] * (n_expert // 2),
            in_specs=[VMEM] * pairs,
            out_specs=[VMEM] * (n_expert // 2),
            compiler_params=GRANT,
            name="fold",
        )(own, *landed)
        pieces = list(folded) + pieces
    landed = []
    for k in range(n_expert - 1, 0, -1):
        landed.insert(0, lax.ppermute(pieces[k], "expert", [(e, e ^ k) for e in range(n_expert)]))
    landed.insert(0, pieces[0])

    return pl.pallas_call(
        functools.partial(mix_kernel, n_expert),
        out_shape=jax.ShapeDtypeStruct((rows, width), jnp.bfloat16),
        in_specs=[VMEM] * (2 + n_expert),
        out_specs=VMEM,
        compiler_params=GRANT,
        name="mix",
    )(expert_ids.T, route_weights.T, *landed)


def solution(mesh):
    in_specs = (
        P(("group", "expert"), None),
        P(("group", "expert"), None),
        P(("group", "expert", "etp"), None),
        P("expert", "etp", None),
        P("expert", "etp", None),
        P("expert", "etp", None),
    )
    out_specs = P(("group", "expert", "etp"), None)
    return jax.shard_map(
        functools.partial(on_device, mesh.shape["expert"], mesh.shape["etp"]),
        mesh=mesh,
        in_specs=in_specs,
        out_specs=out_specs,
        check_vma=False,
    )
```

```python
import functools

import jax
import jax.numpy as jnp
from jax import lax
from jax.experimental import pallas as pl
from jax.experimental.pallas import tpu as pltpu
from jax.sharding import PartitionSpec as P

VMEM = pl.BlockSpec(memory_space=pltpu.VMEM)
GRANT = pltpu.CompilerParams(vmem_limit_bytes=16 * 1024 * 1024)
AHEAD = pl.CostEstimate(flops=10**10, bytes_accessed=0, transcendentals=0)
HBM = pl.BlockSpec(memory_space=pltpu.HBM)


def fetch_kernel(tokens, own, mine, sems):
    half = mine.shape[1]
    core = lax.rem(lax.axis_index("etp"), 2)
    cols = pl.ds(pl.multiple_of(core * half, half), half)
    copies = [
        pltpu.make_async_copy(tokens.at[:, cols], mine, sems.at[0]),
        pltpu.make_async_copy(tokens, own, sems.at[1]),
    ]
    for copy in copies:
        copy.start()
    for copy in copies:
        copy.wait()


def order_kernel(n_expert, pairs, rows, mine, out):
    del mine
    total = out.shape[0]
    me = lax.axis_index("etp")
    core, pair = lax.rem(me, 2), lax.div(me, 2)
    place = lax.broadcasted_iota(jnp.int32, (total, total), 0)
    source = lax.broadcasted_iota(jnp.int32, (total, total), 1)
    far = total - 4 * pairs * rows
    is_near = place >= far
    place = jnp.where(is_near, place - far, place)
    count = jnp.where(is_near, 1, n_expert // 2 - 1)
    row = lax.rem(place, rows)
    side = lax.rem(lax.div(place, rows), 2)
    two = lax.rem(lax.div(place, rows * 2), count)
    h = lax.rem(lax.div(place, rows * 2 * count), pairs)
    sent = lax.div(place, rows * 2 * count * pairs)
    k = jnp.where(is_near, 0, 2 * two + 2) + lax.rem(core + sent, 2)
    block = 2 * lax.rem(pair + h, pairs) + lax.rem(core + sent + side, 2)
    wanted = (k * pairs * 2 + block) * rows + row
    out[...] = jnp.where(source == wanted, 1.0, 0.0).astype(jnp.bfloat16)


def ffn_kernel(n_expert, parts, own, next_block, next_swapped, order, *refs):
    far = refs[: n_expert - 2]
    w_gate, w_up, w_down, kept, sent, rest, x = refs[n_expert - 2 :]
    core = lax.rem(lax.axis_index("etp"), 2)
    tok = own.shape[0]
    x[0:tok, :] = own[...]
    half = next_block.shape[1]
    for block, side in ((next_block, core), (next_swapped, 1 - core)):
        x[tok : 2 * tok, pl.ds(pl.multiple_of(side * half, half), half)] = block[...]
    for i in range(0, n_expert - 2, 2):
        for block, k in ((far[i], i + 2 + core), (far[i + 1], i + 3 - core)):
            x[pl.ds(pl.multiple_of(k * tok, tok), tok), :] = block[...]
    contract = (((1,), (1,)), ((), ()))
    gate = lax.dot_general(w_gate[0], x[...], contract, preferred_element_type=jnp.float32)
    upper = lax.dot_general(w_up[0], x[...], contract, preferred_element_type=jnp.float32)
    hidden = (gate / (1.0 + jnp.exp(-gate)) * upper).astype(jnp.bfloat16)
    hidden = lax.dot_general(order[...], hidden, contract, preferred_element_type=jnp.float32)
    hidden = hidden.astype(jnp.bfloat16)
    now = hidden.shape[0] - rest.shape[0]
    rest[...] = hidden[now:]
    down(parts, hidden[:now], w_down, kept, sent)


def down(parts, hidden, w_down, kept, sent):
    side, width = kept.shape
    step = width // parts
    for c in range(parts):
        cols = slice(c * step, (c + 1) * step)
        out = jnp.dot(hidden, w_down[0, :, cols], preferred_element_type=jnp.float32)
        kept[:, cols] = out[:side]
        sent[:, cols] = out[side:].astype(jnp.bfloat16)


def down_kernel(parts, hidden, w_down, kept, sent):
    down(parts, hidden[...], w_down, kept, sent)


def add_kernel(kept, arrived, own, *pieces):
    span = own.shape[0]
    own[...] = kept[:span, :] + arrived[:span, :].astype(jnp.float32)
    for i, piece in enumerate(pieces):
        at = slice((i + 1) * span, (i + 2) * span)
        piece[...] = (kept[at, :] + arrived[at, :].astype(jnp.float32)).astype(jnp.bfloat16)


def fold_kernel(pairs, own, *refs):
    arrived, pieces = refs[: pairs - 1], refs[pairs - 1 :]
    total = own[...]
    for block in arrived:
        total = total + block[...].astype(jnp.float32)
    rows = pieces[0].shape[0]
    for k, piece in enumerate(pieces):
        piece[...] = total[k * rows : (k + 1) * rows].astype(piece.dtype)


def pack_kernel(near_kept, near_landed, *refs):
    far, out = refs[:-1], refs[-1]
    rows = near_kept.shape[0] // 2
    core = lax.rem(lax.axis_index("etp"), 2)
    out[:rows] = jnp.where(core == 0, near_kept[rows:], near_landed[rows:])
    for i, piece in enumerate(far, 1):
        out[i * rows : (i + 1) * rows] = piece[rows:]


def mix_kernel(ids, weights, swapped, near_kept, near_landed, *refs):
    far, out = refs[:-1], refs[-1]
    rows = out.shape[0]
    me, expert = lax.axis_index("etp"), lax.axis_index("expert")
    core = lax.rem(me, 2)
    top, tok = ids.shape

    def column(ref, start, i):
        lane = lax.broadcasted_iota(jnp.int32, (rows, ref.shape[1]), 1)
        row = lax.broadcasted_iota(jnp.int32, (rows, ref.shape[1]), 0)
        values = jnp.where(lane == start + row, ref[i : i + 1, :], 0)
        return jnp.sum(values, axis=1, keepdims=True)

    own_ids = [column(ids, me * rows, i) for i in range(top)]
    own_weights = [column(weights, 0, i) for i in range(top)]
    scale = sum(own_weights)
    total = None
    for i in range(len(far) + 1):
        if i == 0:
            mine = jnp.where(core == 0, near_kept[:rows], near_landed[:rows])
        else:
            mine = far[i - 1][:rows]
        for part, k in ((mine, 2 * i + core), (swapped[i * rows : (i + 1) * rows], 2 * i + 1 - core)):
            owner = lax.bitwise_xor(expert, k)
            factor = (
                sum(jnp.where(own_ids[j] == owner, own_weights[j], 0.0) for j in range(top)) / scale
            )
            term = part.astype(jnp.float32) * factor
            total = term if total is None else total + term
    out[...] = total.astype(out.dtype)


def on_device(n_expert, n_etp, tokens, expert_ids, route_weights, w_gate, w_up, w_down):
    tok, width = tokens.shape
    rows = tok // n_etp
    pairs = n_etp // 2
    side = n_expert * tok // 2

    own, mine = pl.pallas_call(
        fetch_kernel,
        out_shape=[
            jax.ShapeDtypeStruct((tok, width), tokens.dtype),
            jax.ShapeDtypeStruct((tok, width // 2), tokens.dtype),
        ],
        in_specs=[HBM],
        out_specs=[VMEM] * 2,
        scratch_shapes=[pltpu.SemaphoreType.DMA((2,))],
        compiler_params=GRANT,
        name="fetch",
    )(pltpu.with_memory_space_constraint(tokens, pltpu.HBM))
    order = pl.pallas_call(
        functools.partial(order_kernel, n_expert, pairs, rows),
        out_shape=jax.ShapeDtypeStruct((2 * side, 2 * side), jnp.bfloat16),
        in_specs=[VMEM],
        out_specs=VMEM,
        cost_estimate=AHEAD,
        compiler_params=GRANT,
        name="order",
    )(mine)
    mine, order = lax.optimization_barrier((mine, order))

    swap = [(t, t ^ 1) for t in range(n_etp)]
    routes = [
        [
            (e * n_etp + t, (e ^ (k + t % 2)) * n_etp + t)
            for e in range(n_expert)
            for t in range(n_etp)
        ]
        for k in range(2, n_expert, 2)
    ]
    far = [lax.ppermute(tokens, ("expert", "etp"), route) for route in routes]
    next_block = lax.ppermute(mine, "expert", [(e, e ^ 1) for e in range(n_expert)])
    near = [next_block, lax.ppermute(next_block, "etp", swap)]
    far = [b for block in far for b in (block, lax.ppermute(block, "etp", swap))]

    parts = 4
    def halves(experts):
        shape = (experts * tok // 2, width)
        return [jax.ShapeDtypeStruct(shape, dtype) for dtype in (jnp.float32, jnp.bfloat16)]

    far_kept, far_sent, rest = pl.pallas_call(
        functools.partial(ffn_kernel, n_expert, parts),
        out_shape=halves(n_expert - 2)
        + [jax.ShapeDtypeStruct((2 * tok, w_gate.shape[1]), jnp.bfloat16)],
        in_specs=[VMEM] * (n_expert + 5),
        out_specs=[VMEM] * 3,
        scratch_shapes=[pltpu.VMEM((n_expert * tok, width), jnp.bfloat16)],
        compiler_params=GRANT,
        name="ffn",
    )(own, *near, order, *far, w_gate, w_up, w_down)
    near_kept, near_sent = pl.pallas_call(
        functools.partial(down_kernel, parts),
        out_shape=halves(2),
        in_specs=[VMEM] * 2,
        out_specs=[VMEM] * 2,
        compiler_params=GRANT,
        name="down",
    )(rest, w_down)

    turns = [
        [(t, 2 * ((t // 2 + h) % pairs) + t % 2) for t in range(n_etp)] for h in range(1, pairs)
    ]

    def over_etp(kept, sent, twos):
        block = (kept.shape[0] // pairs, width)
        own, *others = pl.pallas_call(
            add_kernel,
            out_shape=[jax.ShapeDtypeStruct(block, jnp.float32)]
            + [jax.ShapeDtypeStruct(block, jnp.bfloat16)] * (pairs - 1),
            in_specs=[VMEM] * 2,
            out_specs=[VMEM] * pairs,
            compiler_params=GRANT,
            name="add",
        )(kept, lax.ppermute(sent, "etp", swap))
        landed = [lax.ppermute(piece, "etp", turn) for piece, turn in zip(others, turns)]
        return pl.pallas_call(
            functools.partial(fold_kernel, pairs),
            out_shape=[jax.ShapeDtypeStruct((2 * rows, width), jnp.bfloat16)] * twos,
            in_specs=[VMEM] * pairs,
            out_specs=[VMEM] * twos,
            compiler_params=GRANT,
            name="fold",
        )(own, *landed)

    twos = n_expert // 2
    far = [
        lax.ppermute(piece, ("expert", "etp"), route)
        for piece, route in zip(over_etp(far_kept, far_sent, twos - 1), routes)
    ]
    (near_kept,) = over_etp(near_kept, near_sent, 1)
    odd = [
        (e * n_etp + t, (e ^ 1) * n_etp + t) for e in range(n_expert) for t in range(1, n_etp, 2)
    ]
    near_landed = lax.ppermute(near_kept, ("expert", "etp"), odd)
    packed = pl.pallas_call(
        pack_kernel,
        out_shape=jax.ShapeDtypeStruct((twos * rows, width), jnp.bfloat16),
        in_specs=[VMEM] * (twos + 1),
        out_specs=VMEM,
        compiler_params=GRANT,
        name="pack",
    )(near_kept, near_landed, *far)
    swapped = lax.ppermute(packed, "etp", swap)

    return pl.pallas_call(
        mix_kernel,
        out_shape=jax.ShapeDtypeStruct((rows, width), jnp.bfloat16),
        in_specs=[VMEM] * (twos + 4),
        out_specs=VMEM,
        compiler_params=GRANT,
        name="mix",
    )(expert_ids.T, route_weights.T, swapped, near_kept, near_landed, *far)


def solution(mesh):
    in_specs = (
        P(("group", "expert"), None),
        P(("group", "expert"), None),
        P(("group", "expert", "etp"), None),
        P("expert", "etp", None),
        P("expert", "etp", None),
        P("expert", "etp", None),
    )
    out_specs = P(("group", "expert", "etp"), None)
    return jax.shard_map(
        functools.partial(on_device, mesh.shape["expert"], mesh.shape["etp"]),
        mesh=mesh,
        in_specs=in_specs,
        out_specs=out_specs,
        check_vma=False,
    )
```

```python
import functools

import jax
import jax.numpy as jnp
from jax import lax
from jax.experimental import pallas as pl
from jax.experimental.pallas import tpu as pltpu
from jax.sharding import PartitionSpec as P

VMEM = pl.BlockSpec(memory_space=pltpu.VMEM)
GRANT = pltpu.CompilerParams(vmem_limit_bytes=16 * 1024 * 1024)
AHEAD = pl.CostEstimate(flops=10**10, bytes_accessed=0, transcendentals=0)
HBM = pl.BlockSpec(memory_space=pltpu.HBM)


def fetch_kernel(tokens, own, sem):
    copy = pltpu.make_async_copy(tokens, own, sem)
    copy.start()
    copy.wait()


def order_kernel(n_expert, pairs, rows, own, out):
    del own
    total = out.shape[0]
    me = lax.axis_index("etp")
    core, pair = lax.rem(me, 2), lax.div(me, 2)
    place = lax.broadcasted_iota(jnp.int32, (total, total), 0)
    source = lax.broadcasted_iota(jnp.int32, (total, total), 1)
    half = n_expert // 2
    row = lax.rem(place, rows)
    k = lax.rem(lax.div(place, rows), half)
    h = lax.rem(lax.div(place, rows * half), pairs)
    sent = lax.rem(lax.div(place, rows * half * pairs), 2)
    k = k + half * (1 - lax.div(place, rows * half * pairs * 2))
    block = 2 * lax.rem(pair + h, pairs) + lax.rem(core + sent, 2)
    wanted = (k * pairs * 2 + block) * rows + row
    out[...] = jnp.where(source == wanted, 1.0, 0.0).astype(jnp.bfloat16)


def ffn_kernel(n_expert, parts, own, next_block, order, *refs):
    far = refs[: n_expert - 2]
    w_gate, w_up, w_down, kept, sent, rest, x = refs[n_expert - 2 :]
    core = lax.rem(lax.axis_index("etp"), 2)
    tok = own.shape[0]
    x[0:tok, :] = own[...]
    x[tok : 2 * tok, :] = next_block[...]
    for i in range(0, n_expert - 2, 2):
        for block, k in ((far[i], i + 2 + core), (far[i + 1], i + 3 - core)):
            x[pl.ds(pl.multiple_of(k * tok, tok), tok), :] = block[...]
    contract = (((1,), (1,)), ((), ()))
    gate = lax.dot_general(w_gate[0], x[...], contract, preferred_element_type=jnp.float32)
    upper = lax.dot_general(w_up[0], x[...], contract, preferred_element_type=jnp.float32)
    hidden = (gate / (1.0 + jnp.exp(-gate)) * upper).astype(jnp.bfloat16)
    hidden = lax.dot_general(order[...], hidden, contract, preferred_element_type=jnp.float32)
    hidden = hidden.astype(jnp.bfloat16)
    now = rest.shape[0]
    rest[...] = hidden[now:]
    down(parts, hidden[:now], w_down, kept, sent)


def down(parts, hidden, w_down, kept, sent):
    side, width = kept.shape
    step = width // parts
    for c in range(parts):
        cols = slice(c * step, (c + 1) * step)
        out = jnp.dot(hidden, w_down[0, :, cols], preferred_element_type=jnp.float32)
        kept[:, cols] = out[:side]
        sent[:, cols] = out[side:].astype(jnp.bfloat16)


def down_kernel(parts, hidden, w_down, kept, sent):
    down(parts, hidden[...], w_down, kept, sent)


def add_kernel(kept, arrived, own, *pieces):
    span = own.shape[0]
    own[...] = kept[:span, :] + arrived[:span, :].astype(jnp.float32)
    for i, piece in enumerate(pieces):
        at = slice((i + 1) * span, (i + 2) * span)
        piece[...] = (kept[at, :] + arrived[at, :].astype(jnp.float32)).astype(jnp.bfloat16)


def fold_kernel(pairs, own, *refs):
    arrived, pieces = refs[: pairs - 1], refs[pairs - 1 :]
    total = own[...]
    for block in arrived:
        total = total + block[...].astype(jnp.float32)
    rows = pieces[0].shape[0]
    for k, piece in enumerate(pieces):
        piece[...] = total[k * rows : (k + 1) * rows].astype(piece.dtype)


def mix_kernel(n_expert, ids, weights, *refs):
    pieces, out = refs[:-1], refs[-1]
    rows = out.shape[0]
    me, expert = lax.axis_index("etp"), lax.axis_index("expert")
    top, tok = ids.shape

    def column(ref, start, i):
        lane = lax.broadcasted_iota(jnp.int32, (rows, ref.shape[1]), 1)
        row = lax.broadcasted_iota(jnp.int32, (rows, ref.shape[1]), 0)
        values = jnp.where(lane == start + row, ref[i : i + 1, :], 0)
        return jnp.sum(values, axis=1, keepdims=True)

    own_ids = [column(ids, me * rows, i) for i in range(top)]
    own_weights = [column(weights, 0, i) for i in range(top)]
    scale = sum(own_weights)
    total = None
    for k in range(n_expert):
        owner = lax.bitwise_xor(expert, k)
        factor = sum(jnp.where(own_ids[i] == owner, own_weights[i], 0.0) for i in range(top)) / scale
        term = pieces[k][...].astype(jnp.float32) * factor
        total = term if total is None else total + term
    out[...] = total.astype(out.dtype)


def on_device(n_expert, n_etp, tokens, expert_ids, route_weights, w_gate, w_up, w_down):
    tok, width = tokens.shape
    rows = tok // n_etp
    pairs = n_etp // 2
    side = n_expert * tok // 2

    own = pl.pallas_call(
        fetch_kernel,
        out_shape=jax.ShapeDtypeStruct((tok, width), tokens.dtype),
        in_specs=[HBM],
        out_specs=VMEM,
        scratch_shapes=[pltpu.SemaphoreType.DMA],
        compiler_params=GRANT,
        name="fetch",
    )(pltpu.with_memory_space_constraint(tokens, pltpu.HBM))
    order = pl.pallas_call(
        functools.partial(order_kernel, n_expert, pairs, rows),
        out_shape=jax.ShapeDtypeStruct((2 * side, 2 * side), jnp.bfloat16),
        in_specs=[VMEM],
        out_specs=VMEM,
        cost_estimate=AHEAD,
        compiler_params=GRANT,
        name="order",
    )(own)
    own, order = lax.optimization_barrier((own, order))

    swap = [(t, t ^ 1) for t in range(n_etp)]
    far = []
    for k in range(2, n_expert, 2):
        route = [
            (e * n_etp + t, (e ^ (k + t % 2)) * n_etp + t)
            for e in range(n_expert)
            for t in range(n_etp)
        ]
        far.append(lax.ppermute(tokens, ("expert", "etp"), route))
    next_block = lax.ppermute(own, "expert", [(e, e ^ 1) for e in range(n_expert)])
    far = [b for block in far for b in (block, lax.ppermute(block, "etp", swap))]

    parts = 4
    halves = [
        jax.ShapeDtypeStruct((side // 2, width), jnp.float32),
        jax.ShapeDtypeStruct((side // 2, width), jnp.bfloat16),
    ]
    far_kept, far_sent, rest = pl.pallas_call(
        functools.partial(ffn_kernel, n_expert, parts),
        out_shape=halves + [jax.ShapeDtypeStruct((side, w_gate.shape[1]), jnp.bfloat16)],
        in_specs=[VMEM] * (n_expert + 4),
        out_specs=[VMEM] * 3,
        scratch_shapes=[pltpu.VMEM((n_expert * tok, width), jnp.bfloat16)],
        compiler_params=GRANT,
        name="ffn",
    )(own, next_block, order, *far, w_gate, w_up, w_down)
    near_kept, near_sent = pl.pallas_call(
        functools.partial(down_kernel, parts),
        out_shape=halves,
        in_specs=[VMEM] * 2,
        out_specs=[VMEM] * 2,
        compiler_params=GRANT,
        name="down",
    )(rest, w_down)

    block = n_expert // 2 * rows
    pieces = []
    for kept, sent in ((far_kept, far_sent), (near_kept, near_sent)):
        arrived = lax.ppermute(sent, "etp", swap)
        own, *others = pl.pallas_call(
            add_kernel,
            out_shape=[jax.ShapeDtypeStruct((block, width), jnp.float32)]
            + [jax.ShapeDtypeStruct((block, width), jnp.bfloat16)] * (pairs - 1),
            in_specs=[VMEM] * 2,
            out_specs=[VMEM] * pairs,
            compiler_params=GRANT,
            name="add",
        )(kept, arrived)
        landed = []
        for h, piece in enumerate(others, 1):
            route = [(t, 2 * ((t // 2 + h) % pairs) + t % 2) for t in range(n_etp)]
            landed.append(lax.ppermute(piece, "etp", route))
        folded = pl.pallas_call(
            functools.partial(fold_kernel, pairs),
            out_shape=[jax.ShapeDtypeStruct((rows, width), jnp.bfloat16)] * (n_expert // 2),
            in_specs=[VMEM] * pairs,
            out_specs=[VMEM] * (n_expert // 2),
            compiler_params=GRANT,
            name="fold",
        )(own, *landed)
        pieces = list(folded) + pieces
    landed = []
    for k in range(n_expert - 1, 0, -1):
        landed.insert(0, lax.ppermute(pieces[k], "expert", [(e, e ^ k) for e in range(n_expert)]))
    landed.insert(0, pieces[0])

    return pl.pallas_call(
        functools.partial(mix_kernel, n_expert),
        out_shape=jax.ShapeDtypeStruct((rows, width), jnp.bfloat16),
        in_specs=[VMEM] * (2 + n_expert),
        out_specs=VMEM,
        compiler_params=GRANT,
        name="mix",
    )(expert_ids.T, route_weights.T, *landed)


def solution(mesh):
    in_specs = (
        P(("group", "expert"), None),
        P(("group", "expert"), None),
        P(("group", "expert", "etp"), None),
        P("expert", "etp", None),
        P("expert", "etp", None),
        P("expert", "etp", None),
    )
    out_specs = P(("group", "expert", "etp"), None)
    return jax.shard_map(
        functools.partial(on_device, mesh.shape["expert"], mesh.shape["etp"]),
        mesh=mesh,
        in_specs=in_specs,
        out_specs=out_specs,
        check_vma=False,
    )
```

```python
import functools

import jax
import jax.numpy as jnp
from jax import lax
from jax.experimental import pallas as pl
from jax.experimental.pallas import tpu as pltpu
from jax.sharding import PartitionSpec as P

VMEM = pl.BlockSpec(memory_space=pltpu.VMEM)
GRANT = pltpu.CompilerParams(vmem_limit_bytes=16 * 1024 * 1024)
AHEAD = pl.CostEstimate(flops=10**10, bytes_accessed=0, transcendentals=0)
HBM = pl.BlockSpec(memory_space=pltpu.HBM)


def fetch_kernel(tokens, own, sem):
    copy = pltpu.make_async_copy(tokens, own, sem)
    copy.start()
    copy.wait()


def order_kernel(n_expert, pairs, rows, own, out):
    del own
    total = out.shape[0]
    me = lax.axis_index("etp")
    core, pair = lax.rem(me, 2), lax.div(me, 2)
    place = lax.broadcasted_iota(jnp.int32, (total, total), 0)
    source = lax.broadcasted_iota(jnp.int32, (total, total), 1)
    half = n_expert // 2
    row = lax.rem(place, rows)
    k = lax.rem(lax.div(place, rows), half)
    h = lax.rem(lax.div(place, rows * half), pairs)
    sent = lax.rem(lax.div(place, rows * half * pairs), 2)
    k = k + half * (1 - lax.div(place, rows * half * pairs * 2))
    block = 2 * lax.rem(pair + h, pairs) + lax.rem(core + sent, 2)
    wanted = (k * pairs * 2 + block) * rows + row
    out[...] = jnp.where(source == wanted, 1.0, 0.0).astype(jnp.bfloat16)


def ffn_kernel(n_expert, parts, own, next_block, order, *refs):
    far = refs[: n_expert - 2]
    w_gate, w_up, w_down, kept, sent, rest, x = refs[n_expert - 2 :]
    core = lax.rem(lax.axis_index("etp"), 2)
    tok = own.shape[0]
    x[0:tok, :] = own[...]
    x[tok : 2 * tok, :] = next_block[...]
    for i in range(0, n_expert - 2, 2):
        for block, k in ((far[i], i + 2 + core), (far[i + 1], i + 3 - core)):
            x[pl.ds(pl.multiple_of(k * tok, tok), tok), :] = block[...]
    contract = (((1,), (1,)), ((), ()))
    gate = lax.dot_general(w_gate[0], x[...], contract, preferred_element_type=jnp.float32)
    upper = lax.dot_general(w_up[0], x[...], contract, preferred_element_type=jnp.float32)
    hidden = (gate / (1.0 + jnp.exp(-gate)) * upper).astype(jnp.bfloat16)
    hidden = lax.dot_general(order[...], hidden, contract, preferred_element_type=jnp.float32)
    hidden = hidden.astype(jnp.bfloat16)
    now = rest.shape[0]
    rest[...] = hidden[now:]
    down(parts, hidden[:now], w_down, kept, sent)


def down(parts, hidden, w_down, kept, sent):
    side, width = kept.shape
    step = width // parts
    for c in range(parts):
        cols = slice(c * step, (c + 1) * step)
        out = jnp.dot(hidden, w_down[0, :, cols], preferred_element_type=jnp.float32)
        kept[:, cols] = out[:side]
        sent[:, cols] = out[side:].astype(jnp.bfloat16)


def down_kernel(parts, hidden, w_down, kept, sent):
    down(parts, hidden[...], w_down, kept, sent)


def add_kernel(kept, arrived, own, *pieces):
    span = own.shape[0]
    own[...] = kept[:span, :] + arrived[:span, :].astype(jnp.float32)
    for i, piece in enumerate(pieces):
        at = slice((i + 1) * span, (i + 2) * span)
        piece[...] = (kept[at, :] + arrived[at, :].astype(jnp.float32)).astype(jnp.bfloat16)


def fold_kernel(pairs, own, *refs):
    arrived, pieces = refs[: pairs - 1], refs[pairs - 1 :]
    total = own[...]
    for block in arrived:
        total = total + block[...].astype(jnp.float32)
    rows, half = pieces[0].shape[0] // 2, pieces[0].shape[1]
    for k, piece in enumerate(pieces):
        block = total[k * rows : (k + 1) * rows].astype(piece.dtype)
        piece[:rows] = block[:, :half]
        piece[rows:] = block[:, half:]


def mix_kernel(n_expert, ids, weights, *refs):
    pieces, out = refs[:-1], refs[-1]
    rows = out.shape[0]
    me, expert = lax.axis_index("etp"), lax.axis_index("expert")
    top, tok = ids.shape

    def column(ref, start, i):
        lane = lax.broadcasted_iota(jnp.int32, (rows, ref.shape[1]), 1)
        row = lax.broadcasted_iota(jnp.int32, (rows, ref.shape[1]), 0)
        values = jnp.where(lane == start + row, ref[i : i + 1, :], 0)
        return jnp.sum(values, axis=1, keepdims=True)

    own_ids = [column(ids, me * rows, i) for i in range(top)]
    own_weights = [column(weights, 0, i) for i in range(top)]
    scale = sum(own_weights)
    left, right = None, None
    for k in range(n_expert):
        owner = lax.bitwise_xor(expert, k)
        factor = sum(jnp.where(own_ids[i] == owner, own_weights[i], 0.0) for i in range(top)) / scale
        term = pieces[k][:rows].astype(jnp.float32) * factor
        left = term if left is None else left + term
        term = pieces[k][rows:].astype(jnp.float32) * factor
        right = term if right is None else right + term
    half = out.shape[1] // 2
    out[:, :half] = left.astype(out.dtype)
    out[:, half:] = right.astype(out.dtype)


def on_device(n_expert, n_etp, tokens, expert_ids, route_weights, w_gate, w_up, w_down):
    tok, width = tokens.shape
    rows = tok // n_etp
    pairs = n_etp // 2
    side = n_expert * tok // 2

    own = pl.pallas_call(
        fetch_kernel,
        out_shape=jax.ShapeDtypeStruct((tok, width), tokens.dtype),
        in_specs=[HBM],
        out_specs=VMEM,
        scratch_shapes=[pltpu.SemaphoreType.DMA],
        compiler_params=GRANT,
        name="fetch",
    )(pltpu.with_memory_space_constraint(tokens, pltpu.HBM))
    order = pl.pallas_call(
        functools.partial(order_kernel, n_expert, pairs, rows),
        out_shape=jax.ShapeDtypeStruct((2 * side, 2 * side), jnp.bfloat16),
        in_specs=[VMEM],
        out_specs=VMEM,
        cost_estimate=AHEAD,
        compiler_params=GRANT,
        name="order",
    )(own)
    own, order = lax.optimization_barrier((own, order))

    swap = [(t, t ^ 1) for t in range(n_etp)]
    far = []
    for k in range(2, n_expert, 2):
        route = [
            (e * n_etp + t, (e ^ (k + t % 2)) * n_etp + t)
            for e in range(n_expert)
            for t in range(n_etp)
        ]
        far.append(lax.ppermute(tokens, ("expert", "etp"), route))
    next_block = lax.ppermute(own, "expert", [(e, e ^ 1) for e in range(n_expert)])
    far = [b for block in far for b in (block, lax.ppermute(block, "etp", swap))]

    parts = 4
    halves = [
        jax.ShapeDtypeStruct((side // 2, width), jnp.float32),
        jax.ShapeDtypeStruct((side // 2, width), jnp.bfloat16),
    ]
    far_kept, far_sent, rest = pl.pallas_call(
        functools.partial(ffn_kernel, n_expert, parts),
        out_shape=halves + [jax.ShapeDtypeStruct((side, w_gate.shape[1]), jnp.bfloat16)],
        in_specs=[VMEM] * (n_expert + 4),
        out_specs=[VMEM] * 3,
        scratch_shapes=[pltpu.VMEM((n_expert * tok, width), jnp.bfloat16)],
        compiler_params=GRANT,
        name="ffn",
    )(own, next_block, order, *far, w_gate, w_up, w_down)
    near_kept, near_sent = pl.pallas_call(
        functools.partial(down_kernel, parts),
        out_shape=halves,
        in_specs=[VMEM] * 2,
        out_specs=[VMEM] * 2,
        compiler_params=GRANT,
        name="down",
    )(rest, w_down)

    block = n_expert // 2 * rows
    pieces = []
    for kept, sent in ((far_kept, far_sent), (near_kept, near_sent)):
        arrived = lax.ppermute(sent, "etp", swap)
        own, *others = pl.pallas_call(
            add_kernel,
            out_shape=[jax.ShapeDtypeStruct((block, width), jnp.float32)]
            + [jax.ShapeDtypeStruct((block, width), jnp.bfloat16)] * (pairs - 1),
            in_specs=[VMEM] * 2,
            out_specs=[VMEM] * pairs,
            compiler_params=GRANT,
            name="add",
        )(kept, arrived)
        landed = []
        for h, piece in enumerate(others, 1):
            route = [(t, 2 * ((t // 2 + h) % pairs) + t % 2) for t in range(n_etp)]
            landed.append(lax.ppermute(piece, "etp", route))
        folded = pl.pallas_call(
            functools.partial(fold_kernel, pairs),
            out_shape=[jax.ShapeDtypeStruct((2 * rows, width // 2), jnp.bfloat16)]
            * (n_expert // 2),
            in_specs=[VMEM] * pairs,
            out_specs=[VMEM] * (n_expert // 2),
            compiler_params=GRANT,
            name="fold",
        )(own, *landed)
        pieces = list(folded) + pieces
    landed = []
    for k in range(n_expert - 1, 0, -1):
        landed.insert(0, lax.ppermute(pieces[k], "expert", [(e, e ^ k) for e in range(n_expert)]))
    landed.insert(0, pieces[0])

    return pl.pallas_call(
        functools.partial(mix_kernel, n_expert),
        out_shape=jax.ShapeDtypeStruct((rows, width), jnp.bfloat16),
        in_specs=[VMEM] * (2 + n_expert),
        out_specs=VMEM,
        compiler_params=GRANT,
        name="mix",
    )(expert_ids.T, route_weights.T, *landed)


def solution(mesh):
    in_specs = (
        P(("group", "expert"), None),
        P(("group", "expert"), None),
        P(("group", "expert", "etp"), None),
        P("expert", "etp", None),
        P("expert", "etp", None),
        P("expert", "etp", None),
    )
    out_specs = P(("group", "expert", "etp"), None)
    return jax.shard_map(
        functools.partial(on_device, mesh.shape["expert"], mesh.shape["etp"]),
        mesh=mesh,
        in_specs=in_specs,
        out_specs=out_specs,
        check_vma=False,
    )
```

```python
import functools

import jax
import jax.numpy as jnp
from jax import lax
from jax.experimental import pallas as pl
from jax.experimental.pallas import tpu as pltpu
from jax.sharding import PartitionSpec as P

VMEM = pl.BlockSpec(memory_space=pltpu.VMEM)
GRANT = pltpu.CompilerParams(vmem_limit_bytes=16 * 1024 * 1024)
AHEAD = pl.CostEstimate(flops=10**10, bytes_accessed=0, transcendentals=0)
HBM = pl.BlockSpec(memory_space=pltpu.HBM)


def fetch_kernel(tokens, own, sem):
    copy = pltpu.make_async_copy(tokens, own, sem)
    copy.start()
    copy.wait()


def order_kernel(n_expert, pairs, rows, own, out):
    del own
    total = out.shape[0]
    me = lax.axis_index("etp")
    core, pair = lax.rem(me, 2), lax.div(me, 2)
    place = lax.broadcasted_iota(jnp.int32, (total, total), 0)
    source = lax.broadcasted_iota(jnp.int32, (total, total), 1)
    half = n_expert // 2
    row = lax.rem(place, rows)
    k = lax.rem(lax.div(place, rows), half)
    h = lax.rem(lax.div(place, rows * half), pairs)
    sent = lax.rem(lax.div(place, rows * half * pairs), 2)
    k = k + half * (1 - lax.div(place, rows * half * pairs * 2))
    block = 2 * lax.rem(pair + h, pairs) + lax.rem(core + sent, 2)
    wanted = (k * pairs * 2 + block) * rows + row
    out[...] = jnp.where(source == wanted, 1.0, 0.0).astype(jnp.bfloat16)


def ffn_kernel(n_expert, parts, own, next_block, order, *refs):
    far = refs[: n_expert - 2]
    w_gate, w_up, w_down, kept, sent, rest, x = refs[n_expert - 2 :]
    core = lax.rem(lax.axis_index("etp"), 2)
    tok = own.shape[0]
    x[0:tok, :] = own[...]
    x[tok : 2 * tok, :] = next_block[...]
    for i in range(0, n_expert - 2, 2):
        for block, k in ((far[i], i + 2 + core), (far[i + 1], i + 3 - core)):
            x[pl.ds(pl.multiple_of(k * tok, tok), tok), :] = block[...]
    contract = (((1,), (1,)), ((), ()))
    gate = lax.dot_general(x[...], w_gate[0], contract, preferred_element_type=jnp.float32)
    upper = lax.dot_general(x[...], w_up[0], contract, preferred_element_type=jnp.float32)
    hidden = (gate / (1.0 + jnp.exp(-gate)) * upper).astype(jnp.bfloat16)
    hidden = jnp.dot(order[...], hidden, preferred_element_type=jnp.float32)
    hidden = hidden.astype(jnp.bfloat16)
    now = rest.shape[0]
    rest[...] = hidden[now:]
    down(parts, hidden[:now], w_down, kept, sent)


def down(parts, hidden, w_down, kept, sent):
    side, width = kept.shape
    step = width // parts
    for c in range(parts):
        cols = slice(c * step, (c + 1) * step)
        out = jnp.dot(hidden, w_down[0, :, cols], preferred_element_type=jnp.float32)
        kept[:, cols] = out[:side]
        sent[:, cols] = out[side:].astype(jnp.bfloat16)


def down_kernel(parts, hidden, w_down, kept, sent):
    down(parts, hidden[...], w_down, kept, sent)


def add_kernel(kept, arrived, own, *pieces):
    span = own.shape[0]
    own[...] = kept[:span, :] + arrived[:span, :].astype(jnp.float32)
    for i, piece in enumerate(pieces):
        at = slice((i + 1) * span, (i + 2) * span)
        piece[...] = (kept[at, :] + arrived[at, :].astype(jnp.float32)).astype(jnp.bfloat16)


def fold_kernel(pairs, own, *refs):
    arrived, pieces = refs[: pairs - 1], refs[pairs - 1 :]
    total = own[...]
    for block in arrived:
        total = total + block[...].astype(jnp.float32)
    rows = pieces[0].shape[0]
    for k, piece in enumerate(pieces):
        piece[...] = total[k * rows : (k + 1) * rows].astype(piece.dtype)


def mix_kernel(n_expert, ids, weights, *refs):
    pieces, out = refs[:-1], refs[-1]
    rows = out.shape[0]
    me, expert = lax.axis_index("etp"), lax.axis_index("expert")
    top, tok = ids.shape

    def column(ref, start, i):
        lane = lax.broadcasted_iota(jnp.int32, (rows, ref.shape[1]), 1)
        row = lax.broadcasted_iota(jnp.int32, (rows, ref.shape[1]), 0)
        values = jnp.where(lane == start + row, ref[i : i + 1, :], 0)
        return jnp.sum(values, axis=1, keepdims=True)

    own_ids = [column(ids, me * rows, i) for i in range(top)]
    own_weights = [column(weights, 0, i) for i in range(top)]
    scale = sum(own_weights)
    total = None
    for k in range(n_expert):
        owner = lax.bitwise_xor(expert, k)
        factor = sum(jnp.where(own_ids[i] == owner, own_weights[i], 0.0) for i in range(top)) / scale
        term = pieces[k][...].astype(jnp.float32) * factor
        total = term if total is None else total + term
    out[...] = total.astype(out.dtype)


def on_device(n_expert, n_etp, tokens, expert_ids, route_weights, w_gate, w_up, w_down):
    tok, width = tokens.shape
    rows = tok // n_etp
    pairs = n_etp // 2
    side = n_expert * tok // 2

    own = pl.pallas_call(
        fetch_kernel,
        out_shape=jax.ShapeDtypeStruct((tok, width), tokens.dtype),
        in_specs=[HBM],
        out_specs=VMEM,
        scratch_shapes=[pltpu.SemaphoreType.DMA],
        compiler_params=GRANT,
        name="fetch",
    )(pltpu.with_memory_space_constraint(tokens, pltpu.HBM))
    order = pl.pallas_call(
        functools.partial(order_kernel, n_expert, pairs, rows),
        out_shape=jax.ShapeDtypeStruct((2 * side, 2 * side), jnp.bfloat16),
        in_specs=[VMEM],
        out_specs=VMEM,
        cost_estimate=AHEAD,
        compiler_params=GRANT,
        name="order",
    )(own)
    own, order = lax.optimization_barrier((own, order))

    swap = [(t, t ^ 1) for t in range(n_etp)]
    far = []
    for k in range(2, n_expert, 2):
        route = [
            (e * n_etp + t, (e ^ (k + t % 2)) * n_etp + t)
            for e in range(n_expert)
            for t in range(n_etp)
        ]
        far.append(lax.ppermute(tokens, ("expert", "etp"), route))
    next_block = lax.ppermute(own, "expert", [(e, e ^ 1) for e in range(n_expert)])
    far = [b for block in far for b in (block, lax.ppermute(block, "etp", swap))]

    parts = 4
    halves = [
        jax.ShapeDtypeStruct((side // 2, width), jnp.float32),
        jax.ShapeDtypeStruct((side // 2, width), jnp.bfloat16),
    ]
    far_kept, far_sent, rest = pl.pallas_call(
        functools.partial(ffn_kernel, n_expert, parts),
        out_shape=halves + [jax.ShapeDtypeStruct((side, w_gate.shape[1]), jnp.bfloat16)],
        in_specs=[VMEM] * (n_expert + 4),
        out_specs=[VMEM] * 3,
        scratch_shapes=[pltpu.VMEM((n_expert * tok, width), jnp.bfloat16)],
        compiler_params=GRANT,
        name="ffn",
    )(own, next_block, order, *far, w_gate, w_up, w_down)
    near_kept, near_sent = pl.pallas_call(
        functools.partial(down_kernel, parts),
        out_shape=halves,
        in_specs=[VMEM] * 2,
        out_specs=[VMEM] * 2,
        compiler_params=GRANT,
        name="down",
    )(rest, w_down)

    block = n_expert // 2 * rows
    pieces = []
    for kept, sent in ((far_kept, far_sent), (near_kept, near_sent)):
        arrived = lax.ppermute(sent, "etp", swap)
        own, *others = pl.pallas_call(
            add_kernel,
            out_shape=[jax.ShapeDtypeStruct((block, width), jnp.float32)]
            + [jax.ShapeDtypeStruct((block, width), jnp.bfloat16)] * (pairs - 1),
            in_specs=[VMEM] * 2,
            out_specs=[VMEM] * pairs,
            compiler_params=GRANT,
            name="add",
        )(kept, arrived)
        landed = []
        for h, piece in enumerate(others, 1):
            route = [(t, 2 * ((t // 2 + h) % pairs) + t % 2) for t in range(n_etp)]
            landed.append(lax.ppermute(piece, "etp", route))
        folded = pl.pallas_call(
            functools.partial(fold_kernel, pairs),
            out_shape=[jax.ShapeDtypeStruct((rows, width), jnp.bfloat16)] * (n_expert // 2),
            in_specs=[VMEM] * pairs,
            out_specs=[VMEM] * (n_expert // 2),
            compiler_params=GRANT,
            name="fold",
        )(own, *landed)
        pieces = list(folded) + pieces
    landed = []
    for k in range(n_expert - 1, 0, -1):
        landed.insert(0, lax.ppermute(pieces[k], "expert", [(e, e ^ k) for e in range(n_expert)]))
    landed.insert(0, pieces[0])

    return pl.pallas_call(
        functools.partial(mix_kernel, n_expert),
        out_shape=jax.ShapeDtypeStruct((rows, width), jnp.bfloat16),
        in_specs=[VMEM] * (2 + n_expert),
        out_specs=VMEM,
        compiler_params=GRANT,
        name="mix",
    )(expert_ids.T, route_weights.T, *landed)


def solution(mesh):
    in_specs = (
        P(("group", "expert"), None),
        P(("group", "expert"), None),
        P(("group", "expert", "etp"), None),
        P("expert", "etp", None),
        P("expert", "etp", None),
        P("expert", "etp", None),
    )
    out_specs = P(("group", "expert", "etp"), None)
    return jax.shard_map(
        functools.partial(on_device, mesh.shape["expert"], mesh.shape["etp"]),
        mesh=mesh,
        in_specs=in_specs,
        out_specs=out_specs,
        check_vma=False,
    )
```

```python
import functools

import jax
import jax.numpy as jnp
from jax import lax
from jax.experimental import pallas as pl
from jax.experimental.pallas import tpu as pltpu
from jax.sharding import PartitionSpec as P

VMEM = pl.BlockSpec(memory_space=pltpu.VMEM)
GRANT = pltpu.CompilerParams(vmem_limit_bytes=16 * 1024 * 1024)
AHEAD = pl.CostEstimate(flops=10**10, bytes_accessed=0, transcendentals=0)
HBM = pl.BlockSpec(memory_space=pltpu.HBM)


def fetch_kernel(tokens, own, sem):
    copy = pltpu.make_async_copy(tokens, own, sem)
    copy.start()
    copy.wait()


def order_kernel(n_expert, pairs, rows, own, out):
    del own
    total = out.shape[0]
    me = lax.axis_index("etp")
    core, pair = lax.rem(me, 2), lax.div(me, 2)
    place = lax.broadcasted_iota(jnp.int32, (total, total), 0)
    source = lax.broadcasted_iota(jnp.int32, (total, total), 1)
    half = n_expert // 2
    row = lax.rem(place, rows)
    k = lax.rem(lax.div(place, rows), half)
    h = lax.rem(lax.div(place, rows * half), pairs)
    sent = lax.rem(lax.div(place, rows * half * pairs), 2)
    k = k + half * (1 - lax.div(place, rows * half * pairs * 2))
    block = 2 * lax.rem(pair + h, pairs) + lax.rem(core + sent, 2)
    wanted = (k * pairs * 2 + block) * rows + row
    out[...] = jnp.where(source == wanted, 1.0, 0.0).astype(jnp.bfloat16)


def ffn_kernel(n_expert, parts, own, next_block, order, *refs):
    far = refs[: n_expert - 2]
    w_gate, w_up, w_down, kept, sent, rest, x = refs[n_expert - 2 :]
    core = lax.rem(lax.axis_index("etp"), 2)
    tok = own.shape[0]
    x[0:tok, :] = own[...]
    x[tok : 2 * tok, :] = next_block[...]
    for i in range(0, n_expert - 2, 2):
        for block, k in ((far[i], i + 2 + core), (far[i + 1], i + 3 - core)):
            x[pl.ds(pl.multiple_of(k * tok, tok), tok), :] = block[...]
    contract = (((1,), (1,)), ((), ()))
    gate = lax.dot_general(w_gate[0], x[...], contract, preferred_element_type=jnp.float32)
    upper = lax.dot_general(w_up[0], x[...], contract, preferred_element_type=jnp.float32)
    hidden = (gate / (1.0 + jnp.exp(-gate)) * upper).astype(jnp.bfloat16)
    hidden = lax.dot_general(order[...], hidden, contract, preferred_element_type=jnp.float32)
    hidden = hidden.astype(jnp.bfloat16)
    now = rest.shape[0]
    rest[...] = hidden[now:]
    down(parts, hidden[:now], w_down, kept, sent)


def down(parts, hidden, w_down, kept, sent):
    side, width = kept.shape
    step = width // parts
    for c in range(parts):
        cols = slice(c * step, (c + 1) * step)
        out = jnp.dot(hidden, w_down[0, :, cols], preferred_element_type=jnp.float32)
        kept[:, cols] = out[:side]
        sent[:, cols] = out[side:].astype(jnp.bfloat16)


def down_kernel(parts, hidden, w_down, kept, sent):
    down(parts, hidden[...], w_down, kept, sent)


def add_kernel(kept, arrived, own, *pieces):
    span = own.shape[0]
    own[...] = kept[:span, :] + arrived[:span, :].astype(jnp.float32)
    for i, piece in enumerate(pieces):
        at = slice((i + 1) * span, (i + 2) * span)
        piece[...] = (kept[at, :] + arrived[at, :].astype(jnp.float32)).astype(jnp.bfloat16)


def fold_kernel(pairs, own, *refs):
    arrived, pieces = refs[: pairs - 1], refs[pairs - 1 :]
    total = own[...]
    for block in arrived:
        total = total + block[...].astype(jnp.float32)
    rows = pieces[0].shape[0]
    for k, piece in enumerate(pieces):
        piece[...] = total[k * rows : (k + 1) * rows].astype(piece.dtype)


def mix_kernel(n_expert, ids, weights, *refs):
    pieces, out = refs[:-1], refs[-1]
    rows = out.shape[0]
    me, expert = lax.axis_index("etp"), lax.axis_index("expert")
    top, tok = ids.shape

    def column(ref, start, i):
        lane = lax.broadcasted_iota(jnp.int32, (rows, ref.shape[1]), 1)
        row = lax.broadcasted_iota(jnp.int32, (rows, ref.shape[1]), 0)
        values = jnp.where(lane == start + row, ref[i : i + 1, :], 0)
        return jnp.sum(values, axis=1, keepdims=True)

    own_ids = [column(ids, me * rows, i) for i in range(top)]
    own_weights = [column(weights, 0, i) for i in range(top)]
    scale = sum(own_weights)
    total = None
    for k in range(n_expert):
        owner = lax.bitwise_xor(expert, k)
        factor = sum(jnp.where(own_ids[i] == owner, own_weights[i], 0.0) for i in range(top)) / scale
        term = pieces[k][...].astype(jnp.float32) * factor
        total = term if total is None else total + term
    out[...] = total.astype(out.dtype)


def on_device(n_expert, n_etp, tokens, expert_ids, route_weights, w_gate, w_up, w_down):
    tok, width = tokens.shape
    rows = tok // n_etp
    pairs = n_etp // 2
    side = n_expert * tok // 2

    own = pl.pallas_call(
        fetch_kernel,
        out_shape=jax.ShapeDtypeStruct((tok, width), tokens.dtype),
        in_specs=[HBM],
        out_specs=VMEM,
        scratch_shapes=[pltpu.SemaphoreType.DMA],
        compiler_params=GRANT,
        name="fetch",
    )(pltpu.with_memory_space_constraint(tokens, pltpu.HBM))
    order = pl.pallas_call(
        functools.partial(order_kernel, n_expert, pairs, rows),
        out_shape=jax.ShapeDtypeStruct((2 * side, 2 * side), jnp.bfloat16),
        in_specs=[VMEM],
        out_specs=VMEM,
        cost_estimate=AHEAD,
        compiler_params=GRANT,
        name="order",
    )(own)

    swap = [(t, t ^ 1) for t in range(n_etp)]
    far = []
    for k in range(2, n_expert, 2):
        route = [
            (e * n_etp + t, (e ^ (k + t % 2)) * n_etp + t)
            for e in range(n_expert)
            for t in range(n_etp)
        ]
        far.append(lax.ppermute(tokens, ("expert", "etp"), route))
    next_block = lax.ppermute(tokens, "expert", [(e, e ^ 1) for e in range(n_expert)])
    far = [b for block in far for b in (block, lax.ppermute(block, "etp", swap))]

    parts = 4
    halves = [
        jax.ShapeDtypeStruct((side // 2, width), jnp.float32),
        jax.ShapeDtypeStruct((side // 2, width), jnp.bfloat16),
    ]
    far_kept, far_sent, rest = pl.pallas_call(
        functools.partial(ffn_kernel, n_expert, parts),
        out_shape=halves + [jax.ShapeDtypeStruct((side, w_gate.shape[1]), jnp.bfloat16)],
        in_specs=[VMEM] * (n_expert + 4),
        out_specs=[VMEM] * 3,
        scratch_shapes=[pltpu.VMEM((n_expert * tok, width), jnp.bfloat16)],
        compiler_params=GRANT,
        name="ffn",
    )(own, next_block, order, *far, w_gate, w_up, w_down)
    near_kept, near_sent = pl.pallas_call(
        functools.partial(down_kernel, parts),
        out_shape=halves,
        in_specs=[VMEM] * 2,
        out_specs=[VMEM] * 2,
        compiler_params=GRANT,
        name="down",
    )(rest, w_down)

    block = n_expert // 2 * rows
    pieces = []
    for kept, sent in ((far_kept, far_sent), (near_kept, near_sent)):
        arrived = lax.ppermute(sent, "etp", swap)
        own, *others = pl.pallas_call(
            add_kernel,
            out_shape=[jax.ShapeDtypeStruct((block, width), jnp.float32)]
            + [jax.ShapeDtypeStruct((block, width), jnp.bfloat16)] * (pairs - 1),
            in_specs=[VMEM] * 2,
            out_specs=[VMEM] * pairs,
            compiler_params=GRANT,
            name="add",
        )(kept, arrived)
        landed = []
        for h, piece in enumerate(others, 1):
            route = [(t, 2 * ((t // 2 + h) % pairs) + t % 2) for t in range(n_etp)]
            landed.append(lax.ppermute(piece, "etp", route))
        folded = pl.pallas_call(
            functools.partial(fold_kernel, pairs),
            out_shape=[jax.ShapeDtypeStruct((rows, width), jnp.bfloat16)] * (n_expert // 2),
            in_specs=[VMEM] * pairs,
            out_specs=[VMEM] * (n_expert // 2),
            compiler_params=GRANT,
            name="fold",
        )(own, *landed)
        pieces = list(folded) + pieces
    landed = []
    for k in range(n_expert - 1, 0, -1):
        landed.insert(0, lax.ppermute(pieces[k], "expert", [(e, e ^ k) for e in range(n_expert)]))
    landed.insert(0, pieces[0])

    return pl.pallas_call(
        functools.partial(mix_kernel, n_expert),
        out_shape=jax.ShapeDtypeStruct((rows, width), jnp.bfloat16),
        in_specs=[VMEM] * (2 + n_expert),
        out_specs=VMEM,
        compiler_params=GRANT,
        name="mix",
    )(expert_ids.T, route_weights.T, *landed)


def solution(mesh):
    in_specs = (
        P(("group", "expert"), None),
        P(("group", "expert"), None),
        P(("group", "expert", "etp"), None),
        P("expert", "etp", None),
        P("expert", "etp", None),
        P("expert", "etp", None),
    )
    out_specs = P(("group", "expert", "etp"), None)
    return jax.shard_map(
        functools.partial(on_device, mesh.shape["expert"], mesh.shape["etp"]),
        mesh=mesh,
        in_specs=in_specs,
        out_specs=out_specs,
        check_vma=False,
    )
```

```python
import functools

import jax
import jax.numpy as jnp
from jax import lax
from jax.experimental import pallas as pl
from jax.experimental.pallas import tpu as pltpu
from jax.sharding import PartitionSpec as P

VMEM = pl.BlockSpec(memory_space=pltpu.VMEM)
GRANT = pltpu.CompilerParams(vmem_limit_bytes=16 * 1024 * 1024)
AHEAD = pl.CostEstimate(flops=10**10, bytes_accessed=0, transcendentals=0)
HBM = pl.BlockSpec(memory_space=pltpu.HBM)


def fetch_kernel(tokens, own, sem):
    copy = pltpu.make_async_copy(tokens, own, sem)
    copy.start()
    copy.wait()


def order_kernel(n_expert, pairs, rows, own, out):
    del own
    total = out.shape[0]
    me = lax.axis_index("etp")
    core, pair = lax.rem(me, 2), lax.div(me, 2)
    place = lax.broadcasted_iota(jnp.int32, (total, total), 0)
    source = lax.broadcasted_iota(jnp.int32, (total, total), 1)
    half = n_expert // 2
    row = lax.rem(place, rows)
    k = lax.rem(lax.div(place, rows), half)
    h = lax.rem(lax.div(place, rows * half), pairs)
    sent = lax.rem(lax.div(place, rows * half * pairs), 2)
    k = k + half * (1 - lax.div(place, rows * half * pairs * 2))
    block = 2 * lax.rem(pair + h, pairs) + lax.rem(core + sent, 2)
    wanted = (k * pairs * 2 + block) * rows + row
    out[...] = jnp.where(source == wanted, 1.0, 0.0).astype(jnp.bfloat16)


def ffn_kernel(n_expert, parts, own, next_block, order, *refs):
    far = refs[: n_expert - 2]
    w_gate, w_up, w_down, kept, sent, rest, x = refs[n_expert - 2 :]
    core = lax.rem(lax.axis_index("etp"), 2)
    tok = own.shape[0]
    x[0:tok, :] = own[...]
    x[tok : 2 * tok, :] = next_block[...]
    for i in range(0, n_expert - 2, 2):
        for block, k in ((far[i], i + 2 + core), (far[i + 1], i + 3 - core)):
            x[pl.ds(pl.multiple_of(k * tok, tok), tok), :] = block[...]
    contract = (((1,), (1,)), ((), ()))
    step = x.shape[1] // parts
    sums = [None, None]
    for c in range(parts):
        cols = slice(c * step, (c + 1) * step)
        for i, w in enumerate((w_gate, w_up)):
            part = lax.dot_general(
                w[0, :, cols], x[:, cols], contract, preferred_element_type=jnp.float32
            )
            sums[i] = part if c == 0 else sums[i] + part
    gate, upper = sums
    hidden = (gate / (1.0 + jnp.exp(-gate)) * upper).astype(jnp.bfloat16)
    hidden = lax.dot_general(order[...], hidden, contract, preferred_element_type=jnp.float32)
    hidden = hidden.astype(jnp.bfloat16)
    now = rest.shape[0]
    rest[...] = hidden[now:]
    down(parts, hidden[:now], w_down, kept, sent)


def down(parts, hidden, w_down, kept, sent):
    side, width = kept.shape
    step = width // parts
    for c in range(parts):
        cols = slice(c * step, (c + 1) * step)
        out = jnp.dot(hidden, w_down[0, :, cols], preferred_element_type=jnp.float32)
        kept[:, cols] = out[:side]
        sent[:, cols] = out[side:].astype(jnp.bfloat16)


def down_kernel(parts, hidden, w_down, kept, sent):
    down(parts, hidden[...], w_down, kept, sent)


def add_kernel(kept, arrived, own, *pieces):
    span = own.shape[0]
    own[...] = kept[:span, :] + arrived[:span, :].astype(jnp.float32)
    for i, piece in enumerate(pieces):
        at = slice((i + 1) * span, (i + 2) * span)
        piece[...] = (kept[at, :] + arrived[at, :].astype(jnp.float32)).astype(jnp.bfloat16)


def fold_kernel(pairs, own, *refs):
    arrived, pieces = refs[: pairs - 1], refs[pairs - 1 :]
    total = own[...]
    for block in arrived:
        total = total + block[...].astype(jnp.float32)
    rows = pieces[0].shape[0]
    for k, piece in enumerate(pieces):
        piece[...] = total[k * rows : (k + 1) * rows].astype(piece.dtype)


def mix_kernel(n_expert, ids, weights, *refs):
    pieces, out = refs[:-1], refs[-1]
    rows = out.shape[0]
    me, expert = lax.axis_index("etp"), lax.axis_index("expert")
    top, tok = ids.shape

    def column(ref, start, i):
        lane = lax.broadcasted_iota(jnp.int32, (rows, ref.shape[1]), 1)
        row = lax.broadcasted_iota(jnp.int32, (rows, ref.shape[1]), 0)
        values = jnp.where(lane == start + row, ref[i : i + 1, :], 0)
        return jnp.sum(values, axis=1, keepdims=True)

    own_ids = [column(ids, me * rows, i) for i in range(top)]
    own_weights = [column(weights, 0, i) for i in range(top)]
    scale = sum(own_weights)
    total = None
    for k in range(n_expert):
        owner = lax.bitwise_xor(expert, k)
        factor = sum(jnp.where(own_ids[i] == owner, own_weights[i], 0.0) for i in range(top)) / scale
        term = pieces[k][...].astype(jnp.float32) * factor
        total = term if total is None else total + term
    out[...] = total.astype(out.dtype)


def on_device(n_expert, n_etp, tokens, expert_ids, route_weights, w_gate, w_up, w_down):
    tok, width = tokens.shape
    rows = tok // n_etp
    pairs = n_etp // 2
    side = n_expert * tok // 2

    own = pl.pallas_call(
        fetch_kernel,
        out_shape=jax.ShapeDtypeStruct((tok, width), tokens.dtype),
        in_specs=[HBM],
        out_specs=VMEM,
        scratch_shapes=[pltpu.SemaphoreType.DMA],
        compiler_params=GRANT,
        name="fetch",
    )(pltpu.with_memory_space_constraint(tokens, pltpu.HBM))
    order = pl.pallas_call(
        functools.partial(order_kernel, n_expert, pairs, rows),
        out_shape=jax.ShapeDtypeStruct((2 * side, 2 * side), jnp.bfloat16),
        in_specs=[VMEM],
        out_specs=VMEM,
        cost_estimate=AHEAD,
        compiler_params=GRANT,
        name="order",
    )(own)

    swap = [(t, t ^ 1) for t in range(n_etp)]
    far = []
    for k in range(2, n_expert, 2):
        route = [
            (e * n_etp + t, (e ^ (k + t % 2)) * n_etp + t)
            for e in range(n_expert)
            for t in range(n_etp)
        ]
        far.append(lax.ppermute(tokens, ("expert", "etp"), route))
    next_block = lax.ppermute(tokens, "expert", [(e, e ^ 1) for e in range(n_expert)])
    far = [b for block in far for b in (block, lax.ppermute(block, "etp", swap))]

    parts = 4
    halves = [
        jax.ShapeDtypeStruct((side // 2, width), jnp.float32),
        jax.ShapeDtypeStruct((side // 2, width), jnp.bfloat16),
    ]
    far_kept, far_sent, rest = pl.pallas_call(
        functools.partial(ffn_kernel, n_expert, parts),
        out_shape=halves + [jax.ShapeDtypeStruct((side, w_gate.shape[1]), jnp.bfloat16)],
        in_specs=[VMEM] * (n_expert + 4),
        out_specs=[VMEM] * 3,
        scratch_shapes=[pltpu.VMEM((n_expert * tok, width), jnp.bfloat16)],
        compiler_params=GRANT,
        name="ffn",
    )(own, next_block, order, *far, w_gate, w_up, w_down)
    near_kept, near_sent = pl.pallas_call(
        functools.partial(down_kernel, parts),
        out_shape=halves,
        in_specs=[VMEM] * 2,
        out_specs=[VMEM] * 2,
        compiler_params=GRANT,
        name="down",
    )(rest, w_down)

    block = n_expert // 2 * rows
    pieces = []
    for kept, sent in ((far_kept, far_sent), (near_kept, near_sent)):
        arrived = lax.ppermute(sent, "etp", swap)
        own, *others = pl.pallas_call(
            add_kernel,
            out_shape=[jax.ShapeDtypeStruct((block, width), jnp.float32)]
            + [jax.ShapeDtypeStruct((block, width), jnp.bfloat16)] * (pairs - 1),
            in_specs=[VMEM] * 2,
            out_specs=[VMEM] * pairs,
            compiler_params=GRANT,
            name="add",
        )(kept, arrived)
        landed = []
        for h, piece in enumerate(others, 1):
            route = [(t, 2 * ((t // 2 + h) % pairs) + t % 2) for t in range(n_etp)]
            landed.append(lax.ppermute(piece, "etp", route))
        folded = pl.pallas_call(
            functools.partial(fold_kernel, pairs),
            out_shape=[jax.ShapeDtypeStruct((rows, width), jnp.bfloat16)] * (n_expert // 2),
            in_specs=[VMEM] * pairs,
            out_specs=[VMEM] * (n_expert // 2),
            compiler_params=GRANT,
            name="fold",
        )(own, *landed)
        pieces = list(folded) + pieces
    landed = []
    for k in range(n_expert - 1, 0, -1):
        landed.insert(0, lax.ppermute(pieces[k], "expert", [(e, e ^ k) for e in range(n_expert)]))
    landed.insert(0, pieces[0])

    return pl.pallas_call(
        functools.partial(mix_kernel, n_expert),
        out_shape=jax.ShapeDtypeStruct((rows, width), jnp.bfloat16),
        in_specs=[VMEM] * (2 + n_expert),
        out_specs=VMEM,
        compiler_params=GRANT,
        name="mix",
    )(expert_ids.T, route_weights.T, *landed)


def solution(mesh):
    in_specs = (
        P(("group", "expert"), None),
        P(("group", "expert"), None),
        P(("group", "expert", "etp"), None),
        P("expert", "etp", None),
        P("expert", "etp", None),
        P("expert", "etp", None),
    )
    out_specs = P(("group", "expert", "etp"), None)
    return jax.shard_map(
        functools.partial(on_device, mesh.shape["expert"], mesh.shape["etp"]),
        mesh=mesh,
        in_specs=in_specs,
        out_specs=out_specs,
        check_vma=False,
    )
```

```python
import functools

import jax
import jax.numpy as jnp
from jax import lax
from jax.experimental import pallas as pl
from jax.experimental.pallas import tpu as pltpu
from jax.sharding import PartitionSpec as P

VMEM = pl.BlockSpec(memory_space=pltpu.VMEM)
GRANT = pltpu.CompilerParams(vmem_limit_bytes=16 * 1024 * 1024)
AHEAD = pl.CostEstimate(flops=10**10, bytes_accessed=0, transcendentals=0)
HBM = pl.BlockSpec(memory_space=pltpu.HBM)


def fetch_kernel(tokens, own, sem):
    copy = pltpu.make_async_copy(tokens, own, sem)
    copy.start()
    copy.wait()


def order_kernel(n_expert, pairs, rows, own, out):
    del own
    total = out.shape[0]
    me = lax.axis_index("etp")
    core, pair = lax.rem(me, 2), lax.div(me, 2)
    place = lax.broadcasted_iota(jnp.int32, (total, total), 0)
    source = lax.broadcasted_iota(jnp.int32, (total, total), 1)
    half = n_expert // 2
    row = lax.rem(place, rows)
    k = lax.rem(lax.div(place, rows), half)
    h = lax.rem(lax.div(place, rows * half), pairs)
    sent = lax.rem(lax.div(place, rows * half * pairs), 2)
    second = lax.div(place, rows * half * pairs * 2)
    shift = jnp.where(second == 0, k + 1, jnp.where(k == 0, 0, k + half))
    expert = lax.axis_index("expert")
    k = lax.bitwise_xor(expert, lax.rem(expert + shift, n_expert))
    block = 2 * lax.rem(pair + h, pairs) + lax.rem(core + sent, 2)
    wanted = (k * pairs * 2 + block) * rows + row
    out[...] = jnp.where(source == wanted, 1.0, 0.0).astype(jnp.bfloat16)


def ffn_kernel(n_expert, parts, own, next_block, order, *refs):
    far = refs[: n_expert - 2]
    w_gate, w_up, w_down, kept, sent, rest, x = refs[n_expert - 2 :]
    core = lax.rem(lax.axis_index("etp"), 2)
    tok = own.shape[0]
    x[0:tok, :] = own[...]
    x[tok : 2 * tok, :] = next_block[...]
    for i in range(0, n_expert - 2, 2):
        for block, k in ((far[i], i + 2 + core), (far[i + 1], i + 3 - core)):
            x[pl.ds(pl.multiple_of(k * tok, tok), tok), :] = block[...]
    contract = (((1,), (1,)), ((), ()))
    gate = lax.dot_general(w_gate[0], x[...], contract, preferred_element_type=jnp.float32)
    upper = lax.dot_general(w_up[0], x[...], contract, preferred_element_type=jnp.float32)
    hidden = (gate / (1.0 + jnp.exp(-gate)) * upper).astype(jnp.bfloat16)
    hidden = lax.dot_general(order[...], hidden, contract, preferred_element_type=jnp.float32)
    hidden = hidden.astype(jnp.bfloat16)
    now = rest.shape[0]
    rest[...] = hidden[now:]
    down(parts, hidden[:now], w_down, kept, sent)


def down(parts, hidden, w_down, kept, sent):
    side, width = kept.shape
    step = width // parts
    for c in range(parts):
        cols = slice(c * step, (c + 1) * step)
        out = jnp.dot(hidden, w_down[0, :, cols], preferred_element_type=jnp.float32)
        kept[:, cols] = out[:side]
        sent[:, cols] = out[side:].astype(jnp.bfloat16)


def down_kernel(parts, hidden, w_down, kept, sent):
    down(parts, hidden[...], w_down, kept, sent)


def add_kernel(kept, arrived, own, *pieces):
    span = own.shape[0]
    own[...] = kept[:span, :] + arrived[:span, :].astype(jnp.float32)
    for i, piece in enumerate(pieces):
        at = slice((i + 1) * span, (i + 2) * span)
        piece[...] = (kept[at, :] + arrived[at, :].astype(jnp.float32)).astype(jnp.bfloat16)


def fold_kernel(pairs, own, *refs):
    arrived, pieces = refs[: pairs - 1], refs[pairs - 1 :]
    total = own[...]
    for block in arrived:
        total = total + block[...].astype(jnp.float32)
    rows = pieces[0].shape[0]
    for k, piece in enumerate(pieces):
        piece[...] = total[k * rows : (k + 1) * rows].astype(piece.dtype)


def mix_kernel(n_expert, ids, weights, *refs):
    pieces, out = refs[:-1], refs[-1]
    rows = out.shape[0]
    me, expert = lax.axis_index("etp"), lax.axis_index("expert")
    top, tok = ids.shape

    def column(ref, start, i):
        lane = lax.broadcasted_iota(jnp.int32, (rows, ref.shape[1]), 1)
        row = lax.broadcasted_iota(jnp.int32, (rows, ref.shape[1]), 0)
        values = jnp.where(lane == start + row, ref[i : i + 1, :], 0)
        return jnp.sum(values, axis=1, keepdims=True)

    own_ids = [column(ids, me * rows, i) for i in range(top)]
    own_weights = [column(weights, 0, i) for i in range(top)]
    scale = sum(own_weights)
    total = None
    for k in range(n_expert):
        owner = lax.rem(expert - k + n_expert, n_expert)
        factor = sum(jnp.where(own_ids[i] == owner, own_weights[i], 0.0) for i in range(top)) / scale
        term = pieces[k][...].astype(jnp.float32) * factor
        total = term if total is None else total + term
    out[...] = total.astype(out.dtype)


def on_device(n_expert, n_etp, tokens, expert_ids, route_weights, w_gate, w_up, w_down):
    tok, width = tokens.shape
    rows = tok // n_etp
    pairs = n_etp // 2
    side = n_expert * tok // 2

    own = pl.pallas_call(
        fetch_kernel,
        out_shape=jax.ShapeDtypeStruct((tok, width), tokens.dtype),
        in_specs=[HBM],
        out_specs=VMEM,
        scratch_shapes=[pltpu.SemaphoreType.DMA],
        compiler_params=GRANT,
        name="fetch",
    )(pltpu.with_memory_space_constraint(tokens, pltpu.HBM))
    order = pl.pallas_call(
        functools.partial(order_kernel, n_expert, pairs, rows),
        out_shape=jax.ShapeDtypeStruct((2 * side, 2 * side), jnp.bfloat16),
        in_specs=[VMEM],
        out_specs=VMEM,
        cost_estimate=AHEAD,
        compiler_params=GRANT,
        name="order",
    )(own)

    swap = [(t, t ^ 1) for t in range(n_etp)]
    far = []
    for k in range(2, n_expert, 2):
        route = [
            (e * n_etp + t, (e ^ (k + t % 2)) * n_etp + t)
            for e in range(n_expert)
            for t in range(n_etp)
        ]
        far.append(lax.ppermute(tokens, ("expert", "etp"), route))
    next_block = lax.ppermute(tokens, "expert", [(e, e ^ 1) for e in range(n_expert)])
    far = [b for block in far for b in (block, lax.ppermute(block, "etp", swap))]

    parts = 4
    halves = [
        jax.ShapeDtypeStruct((side // 2, width), jnp.float32),
        jax.ShapeDtypeStruct((side // 2, width), jnp.bfloat16),
    ]
    far_kept, far_sent, rest = pl.pallas_call(
        functools.partial(ffn_kernel, n_expert, parts),
        out_shape=halves + [jax.ShapeDtypeStruct((side, w_gate.shape[1]), jnp.bfloat16)],
        in_specs=[VMEM] * (n_expert + 4),
        out_specs=[VMEM] * 3,
        scratch_shapes=[pltpu.VMEM((n_expert * tok, width), jnp.bfloat16)],
        compiler_params=GRANT,
        name="ffn",
    )(own, next_block, order, *far, w_gate, w_up, w_down)
    near_kept, near_sent = pl.pallas_call(
        functools.partial(down_kernel, parts),
        out_shape=halves,
        in_specs=[VMEM] * 2,
        out_specs=[VMEM] * 2,
        compiler_params=GRANT,
        name="down",
    )(rest, w_down)

    block = n_expert // 2 * rows
    pieces = []
    for kept, sent in ((far_kept, far_sent), (near_kept, near_sent)):
        arrived = lax.ppermute(sent, "etp", swap)
        own, *others = pl.pallas_call(
            add_kernel,
            out_shape=[jax.ShapeDtypeStruct((block, width), jnp.float32)]
            + [jax.ShapeDtypeStruct((block, width), jnp.bfloat16)] * (pairs - 1),
            in_specs=[VMEM] * 2,
            out_specs=[VMEM] * pairs,
            compiler_params=GRANT,
            name="add",
        )(kept, arrived)
        landed = []
        for h, piece in enumerate(others, 1):
            route = [(t, 2 * ((t // 2 + h) % pairs) + t % 2) for t in range(n_etp)]
            landed.append(lax.ppermute(piece, "etp", route))
        folded = pl.pallas_call(
            functools.partial(fold_kernel, pairs),
            out_shape=[jax.ShapeDtypeStruct((rows, width), jnp.bfloat16)] * (n_expert // 2),
            in_specs=[VMEM] * pairs,
            out_specs=[VMEM] * (n_expert // 2),
            compiler_params=GRANT,
            name="fold",
        )(own, *landed)
        pieces.append(list(folded))
    half = n_expert // 2
    pieces = pieces[1][:1] + pieces[0] + pieces[1][1:]
    landed = pieces[:1]
    for k in range(1, n_expert):
        route = [(e, (e + k) % n_expert) for e in range(n_expert)]
        landed.append(lax.ppermute(pieces[k], "expert", route))

    return pl.pallas_call(
        functools.partial(mix_kernel, n_expert),
        out_shape=jax.ShapeDtypeStruct((rows, width), jnp.bfloat16),
        in_specs=[VMEM] * (2 + n_expert),
        out_specs=VMEM,
        compiler_params=GRANT,
        name="mix",
    )(expert_ids.T, route_weights.T, *landed)


def solution(mesh):
    in_specs = (
        P(("group", "expert"), None),
        P(("group", "expert"), None),
        P(("group", "expert", "etp"), None),
        P("expert", "etp", None),
        P("expert", "etp", None),
        P("expert", "etp", None),
    )
    out_specs = P(("group", "expert", "etp"), None)
    return jax.shard_map(
        functools.partial(on_device, mesh.shape["expert"], mesh.shape["etp"]),
        mesh=mesh,
        in_specs=in_specs,
        out_specs=out_specs,
        check_vma=False,
    )
```

```python
import functools

import jax
import jax.numpy as jnp
from jax import lax
from jax.experimental import pallas as pl
from jax.experimental.pallas import tpu as pltpu
from jax.sharding import PartitionSpec as P

VMEM = pl.BlockSpec(memory_space=pltpu.VMEM)
GRANT = pltpu.CompilerParams(vmem_limit_bytes=16 * 1024 * 1024)
AHEAD = pl.CostEstimate(flops=10**10, bytes_accessed=0, transcendentals=0)
HBM = pl.BlockSpec(memory_space=pltpu.HBM)


def fetch_kernel(tokens, own, sem):
    copy = pltpu.make_async_copy(tokens, own, sem)
    copy.start()
    copy.wait()


def order_kernel(n_expert, pairs, rows, own, out):
    del own
    total = out.shape[0]
    me = lax.axis_index("etp")
    core, pair = lax.rem(me, 2), lax.div(me, 2)
    place = lax.broadcasted_iota(jnp.int32, (total, total), 0)
    source = lax.broadcasted_iota(jnp.int32, (total, total), 1)
    half = n_expert // 2
    row = lax.rem(place, rows)
    k = lax.rem(lax.div(place, rows), half)
    h = lax.rem(lax.div(place, rows * half), pairs)
    sent = lax.rem(lax.div(place, rows * half * pairs), 2)
    second = lax.div(place, rows * half * pairs * 2)
    shift = jnp.where(second == 0, k + 1, jnp.where(k == 0, 0, k + half))
    expert = lax.axis_index("expert")
    k = lax.bitwise_xor(expert, lax.rem(expert + shift, n_expert))
    block = 2 * lax.rem(pair + h, pairs) + lax.rem(core + sent, 2)
    wanted = (k * pairs * 2 + block) * rows + row
    out[...] = jnp.where(source == wanted, 1.0, 0.0).astype(jnp.bfloat16)


def ffn_kernel(n_expert, parts, own, next_block, order, *refs):
    far = refs[: n_expert - 2]
    w_gate, w_up, w_down, kept, sent, rest, x = refs[n_expert - 2 :]
    core = lax.rem(lax.axis_index("etp"), 2)
    tok = own.shape[0]
    x[0:tok, :] = own[...]
    x[tok : 2 * tok, :] = next_block[...]
    for i in range(0, n_expert - 2, 2):
        for block, k in ((far[i], i + 2 + core), (far[i + 1], i + 3 - core)):
            x[pl.ds(pl.multiple_of(k * tok, tok), tok), :] = block[...]
    contract = (((1,), (1,)), ((), ()))
    gate = lax.dot_general(w_gate[0], x[...], contract, preferred_element_type=jnp.float32)
    upper = lax.dot_general(w_up[0], x[...], contract, preferred_element_type=jnp.float32)
    hidden = (gate / (1.0 + jnp.exp(-gate)) * upper).astype(jnp.bfloat16)
    hidden = lax.dot_general(order[...], hidden, contract, preferred_element_type=jnp.float32)
    hidden = hidden.astype(jnp.bfloat16)
    now = rest.shape[0]
    rest[...] = hidden[now:]
    down(parts, hidden[:now], w_down, kept, sent)


def down(parts, hidden, w_down, kept, sent):
    side, width = kept.shape
    step = width // parts
    for c in range(parts):
        cols = slice(c * step, (c + 1) * step)
        out = jnp.dot(hidden, w_down[0, :, cols], preferred_element_type=jnp.float32)
        kept[:, cols] = out[:side]
        sent[:, cols] = out[side:].astype(jnp.bfloat16)


def down_kernel(parts, hidden, w_down, kept, sent):
    down(parts, hidden[...], w_down, kept, sent)


def add_kernel(pairs, kept, arrived, *refs):
    start = 0
    for h in range(pairs):
        for out in refs[h::pairs]:
            at = slice(start, start + out.shape[0])
            out[...] = (kept[at, :] + arrived[at, :].astype(jnp.float32)).astype(out.dtype)
            start += out.shape[0]


def fold_kernel(pairs, own, *refs):
    arrived, pieces = refs[: pairs - 1], refs[pairs - 1 :]
    total = own[...]
    for block in arrived:
        total = total + block[...].astype(jnp.float32)
    rows = pieces[0].shape[0]
    for k, piece in enumerate(pieces):
        piece[...] = total[k * rows : (k + 1) * rows].astype(piece.dtype)


def mix_kernel(n_expert, ids, weights, *refs):
    pieces, (out, own_factor) = refs[:-2], refs[-2:]
    rows = out.shape[0]
    me, expert = lax.axis_index("etp"), lax.axis_index("expert")
    top, tok = ids.shape

    def column(ref, start, i):
        lane = lax.broadcasted_iota(jnp.int32, (rows, ref.shape[1]), 1)
        row = lax.broadcasted_iota(jnp.int32, (rows, ref.shape[1]), 0)
        values = jnp.where(lane == start + row, ref[i : i + 1, :], 0)
        return jnp.sum(values, axis=1, keepdims=True)

    own_ids = [column(ids, me * rows, i) for i in range(top)]
    own_weights = [column(weights, 0, i) for i in range(top)]
    scale = sum(own_weights)
    total = None
    for k in range(n_expert):
        owner = lax.rem(expert - k + n_expert, n_expert)
        factor = sum(jnp.where(own_ids[i] == owner, own_weights[i], 0.0) for i in range(top)) / scale
        if k == 0:
            own_factor[...] = jnp.broadcast_to(factor, own_factor.shape)
        else:
            term = pieces[k - 1][...].astype(jnp.float32) * factor
            total = term if total is None else total + term
    out[...] = total


def finish_kernel(partial, own_factor, *refs):
    own, out = refs[:-1], refs[-1]
    total = sum(block[...].astype(jnp.float32) for block in own)
    out[...] = (partial[...] + total * own_factor[:, :1]).astype(out.dtype)


def on_device(n_expert, n_etp, tokens, expert_ids, route_weights, w_gate, w_up, w_down):
    tok, width = tokens.shape
    rows = tok // n_etp
    pairs = n_etp // 2
    side = n_expert * tok // 2

    own = pl.pallas_call(
        fetch_kernel,
        out_shape=jax.ShapeDtypeStruct((tok, width), tokens.dtype),
        in_specs=[HBM],
        out_specs=VMEM,
        scratch_shapes=[pltpu.SemaphoreType.DMA],
        compiler_params=GRANT,
        name="fetch",
    )(pltpu.with_memory_space_constraint(tokens, pltpu.HBM))
    order = pl.pallas_call(
        functools.partial(order_kernel, n_expert, pairs, rows),
        out_shape=jax.ShapeDtypeStruct((2 * side, 2 * side), jnp.bfloat16),
        in_specs=[VMEM],
        out_specs=VMEM,
        cost_estimate=AHEAD,
        compiler_params=GRANT,
        name="order",
    )(own)

    swap = [(t, t ^ 1) for t in range(n_etp)]
    far = []
    for k in range(2, n_expert, 2):
        route = [
            (e * n_etp + t, (e ^ (k + t % 2)) * n_etp + t)
            for e in range(n_expert)
            for t in range(n_etp)
        ]
        far.append(lax.ppermute(tokens, ("expert", "etp"), route))
    next_block = lax.ppermute(tokens, "expert", [(e, e ^ 1) for e in range(n_expert)])
    far = [b for block in far for b in (block, lax.ppermute(block, "etp", swap))]

    parts = 4
    halves = [
        jax.ShapeDtypeStruct((side // 2, width), jnp.float32),
        jax.ShapeDtypeStruct((side // 2, width), jnp.bfloat16),
    ]
    far_kept, far_sent, rest = pl.pallas_call(
        functools.partial(ffn_kernel, n_expert, parts),
        out_shape=halves + [jax.ShapeDtypeStruct((side, w_gate.shape[1]), jnp.bfloat16)],
        in_specs=[VMEM] * (n_expert + 4),
        out_specs=[VMEM] * 3,
        scratch_shapes=[pltpu.VMEM((n_expert * tok, width), jnp.bfloat16)],
        compiler_params=GRANT,
        name="ffn",
    )(own, next_block, order, *far, w_gate, w_up, w_down)
    near_kept, near_sent = pl.pallas_call(
        functools.partial(down_kernel, parts),
        out_shape=halves,
        in_specs=[VMEM] * 2,
        out_specs=[VMEM] * 2,
        compiler_params=GRANT,
        name="down",
    )(rest, w_down)

    turns = [
        [(t, 2 * ((t // 2 + h) % pairs) + t % 2) for t in range(n_etp)] for h in range(1, pairs)
    ]

    def add(kept, sent, counts):
        shapes = [
            jax.ShapeDtypeStruct((count * rows, width), jnp.bfloat16 if h else jnp.float32)
            for count in counts
            for h in range(pairs)
        ]
        sums = pl.pallas_call(
            functools.partial(add_kernel, pairs),
            out_shape=shapes,
            in_specs=[VMEM] * 2,
            out_specs=[VMEM] * len(shapes),
            compiler_params=GRANT,
            name="add",
        )(kept, lax.ppermute(sent, "etp", swap))
        return [sums[i * pairs : (i + 1) * pairs] for i in range(len(counts))]

    def over_pairs(own, *others):
        take = own.shape[0] // rows
        landed = [lax.ppermute(piece, "etp", turn) for piece, turn in zip(others, turns)]
        return list(
            pl.pallas_call(
                functools.partial(fold_kernel, pairs),
                out_shape=[jax.ShapeDtypeStruct((rows, width), jnp.bfloat16)] * take,
                in_specs=[VMEM] * pairs,
                out_specs=[VMEM] * take,
                compiler_params=GRANT,
                name="fold",
            )(own, *landed)
        )

    half = n_expert // 2
    first, second = add(far_kept, far_sent, (half // 2, half - half // 2))
    pieces = over_pairs(*first) + over_pairs(*second)
    own, last = add(near_kept, near_sent, (1, half - 1))
    last = over_pairs(*last)
    pieces += last
    own, *others = own
    others, _ = lax.optimization_barrier((others, last))
    landed = []
    for k, piece in enumerate(pieces, 1):
        route = [(e, (e + k) % n_expert) for e in range(n_expert)]
        landed.append(lax.ppermute(piece, "expert", route))
    own = [own] + [lax.ppermute(piece, "etp", turn) for piece, turn in zip(others, turns)]

    partial, own_factor = pl.pallas_call(
        functools.partial(mix_kernel, n_expert),
        out_shape=[
            jax.ShapeDtypeStruct((rows, width), jnp.float32),
            jax.ShapeDtypeStruct((rows, 128), jnp.float32),
        ],
        in_specs=[VMEM] * (1 + n_expert),
        out_specs=[VMEM] * 2,
        compiler_params=GRANT,
        name="mix",
    )(expert_ids.T, route_weights.T, *landed)
    return pl.pallas_call(
        finish_kernel,
        out_shape=jax.ShapeDtypeStruct((rows, width), jnp.bfloat16),
        in_specs=[VMEM] * (2 + pairs),
        out_specs=VMEM,
        compiler_params=GRANT,
        name="finish",
    )(partial, own_factor, *own)


def solution(mesh):
    in_specs = (
        P(("group", "expert"), None),
        P(("group", "expert"), None),
        P(("group", "expert", "etp"), None),
        P("expert", "etp", None),
        P("expert", "etp", None),
        P("expert", "etp", None),
    )
    out_specs = P(("group", "expert", "etp"), None)
    return jax.shard_map(
        functools.partial(on_device, mesh.shape["expert"], mesh.shape["etp"]),
        mesh=mesh,
        in_specs=in_specs,
        out_specs=out_specs,
        check_vma=False,
    )
```

```python
import functools

import jax
import jax.numpy as jnp
from jax import lax
from jax.experimental import pallas as pl
from jax.experimental.pallas import tpu as pltpu
from jax.sharding import PartitionSpec as P

VMEM = pl.BlockSpec(memory_space=pltpu.VMEM)
GRANT = pltpu.CompilerParams(vmem_limit_bytes=16 * 1024 * 1024)
AHEAD = pl.CostEstimate(flops=10**10, bytes_accessed=0, transcendentals=0)
HBM = pl.BlockSpec(memory_space=pltpu.HBM)


def fetch_kernel(tokens, own, sem):
    copy = pltpu.make_async_copy(tokens, own, sem)
    copy.start()
    copy.wait()


def order_kernel(n_expert, pairs, rows, own, out):
    del own
    total = out.shape[0]
    me = lax.axis_index("etp")
    core, pair = lax.rem(me, 2), lax.div(me, 2)
    place = lax.broadcasted_iota(jnp.int32, (total, total), 0)
    source = lax.broadcasted_iota(jnp.int32, (total, total), 1)
    half = n_expert // 2
    row = lax.rem(place, rows)
    k = lax.rem(lax.div(place, rows), half)
    h = lax.rem(lax.div(place, rows * half), pairs)
    sent = lax.rem(lax.div(place, rows * half * pairs), 2)
    second = lax.div(place, rows * half * pairs * 2)
    shift = jnp.where(second == 0, k + 1, jnp.where(k == 0, 0, k + half))
    expert = lax.axis_index("expert")
    k = lax.bitwise_xor(expert, lax.rem(expert + shift, n_expert))
    block = 2 * lax.rem(pair + h, pairs) + lax.rem(core + sent, 2)
    wanted = (k * pairs * 2 + block) * rows + row
    out[...] = jnp.where(source == wanted, 1.0, 0.0).astype(jnp.bfloat16)


def ffn_kernel(n_expert, parts, own, next_block, order, *refs):
    far = refs[: n_expert - 2]
    w_gate, w_up, w_down, kept, sent, rest, x = refs[n_expert - 2 :]
    core = lax.rem(lax.axis_index("etp"), 2)
    tok = own.shape[0]
    x[0:tok, :] = own[...]
    x[tok : 2 * tok, :] = next_block[...]
    for i in range(0, n_expert - 2, 2):
        for block, k in ((far[i], i + 2 + core), (far[i + 1], i + 3 - core)):
            x[pl.ds(pl.multiple_of(k * tok, tok), tok), :] = block[...]
    contract = (((1,), (1,)), ((), ()))
    gate = lax.dot_general(w_gate[0], x[...], contract, preferred_element_type=jnp.float32)
    upper = lax.dot_general(w_up[0], x[...], contract, preferred_element_type=jnp.float32)
    hidden = (gate / (1.0 + jnp.exp(-gate)) * upper).astype(jnp.bfloat16)
    hidden = lax.dot_general(order[...], hidden, contract, preferred_element_type=jnp.float32)
    hidden = hidden.astype(jnp.bfloat16)
    now = rest.shape[0]
    rest[...] = hidden[now:]
    down(parts, hidden[:now], w_down, kept, sent)


def down(parts, hidden, w_down, kept, sent):
    side, width = kept.shape
    step = width // parts
    for c in range(parts):
        cols = slice(c * step, (c + 1) * step)
        out = jnp.dot(hidden, w_down[0, :, cols], preferred_element_type=jnp.float32)
        kept[:, cols] = out[:side]
        sent[:, cols] = out[side:].astype(jnp.bfloat16)


def down_kernel(parts, hidden, w_down, kept, sent):
    down(parts, hidden[...], w_down, kept, sent)


def add_kernel(pairs, kept, arrived, *refs):
    start = 0
    for h in range(pairs):
        for out in refs[h::pairs]:
            at = slice(start, start + out.shape[0])
            out[...] = (kept[at, :] + arrived[at, :].astype(jnp.float32)).astype(out.dtype)
            start += out.shape[0]


def fold_kernel(pairs, own, *refs):
    arrived, pieces = refs[: pairs - 1], refs[pairs - 1 :]
    total = own[...]
    for block in arrived:
        total = total + block[...].astype(jnp.float32)
    rows = pieces[0].shape[0]
    for k, piece in enumerate(pieces):
        piece[...] = total[k * rows : (k + 1) * rows].astype(piece.dtype)


def mix_kernel(n_expert, pairs, ids, weights, *refs):
    own, pieces, out = refs[:pairs], refs[pairs:-1], refs[-1]
    rows = out.shape[0]
    me, expert = lax.axis_index("etp"), lax.axis_index("expert")
    top, tok = ids.shape

    def column(ref, start, i):
        lane = lax.broadcasted_iota(jnp.int32, (rows, ref.shape[1]), 1)
        row = lax.broadcasted_iota(jnp.int32, (rows, ref.shape[1]), 0)
        values = jnp.where(lane == start + row, ref[i : i + 1, :], 0)
        return jnp.sum(values, axis=1, keepdims=True)

    own_ids = [column(ids, me * rows, i) for i in range(top)]
    own_weights = [column(weights, 0, i) for i in range(top)]
    scale = sum(own_weights)
    for k in range(n_expert):
        owner = lax.rem(expert - k + n_expert, n_expert)
        factor = sum(jnp.where(own_ids[i] == owner, own_weights[i], 0.0) for i in range(top)) / scale
        if k == 0:
            total = sum(block[...].astype(jnp.float32) for block in own) * factor
        else:
            total = total + pieces[k - 1][...].astype(jnp.float32) * factor
    out[...] = total.astype(out.dtype)


def on_device(n_expert, n_etp, tokens, expert_ids, route_weights, w_gate, w_up, w_down):
    tok, width = tokens.shape
    rows = tok // n_etp
    pairs = n_etp // 2
    side = n_expert * tok // 2

    own = pl.pallas_call(
        fetch_kernel,
        out_shape=jax.ShapeDtypeStruct((tok, width), tokens.dtype),
        in_specs=[HBM],
        out_specs=VMEM,
        scratch_shapes=[pltpu.SemaphoreType.DMA],
        compiler_params=GRANT,
        name="fetch",
    )(pltpu.with_memory_space_constraint(tokens, pltpu.HBM))
    order = pl.pallas_call(
        functools.partial(order_kernel, n_expert, pairs, rows),
        out_shape=jax.ShapeDtypeStruct((2 * side, 2 * side), jnp.bfloat16),
        in_specs=[VMEM],
        out_specs=VMEM,
        cost_estimate=AHEAD,
        compiler_params=GRANT,
        name="order",
    )(own)

    swap = [(t, t ^ 1) for t in range(n_etp)]
    far = []
    for k in range(2, n_expert, 2):
        route = [
            (e * n_etp + t, (e ^ (k + t % 2)) * n_etp + t)
            for e in range(n_expert)
            for t in range(n_etp)
        ]
        far.append(lax.ppermute(tokens, ("expert", "etp"), route))
    next_block = lax.ppermute(tokens, "expert", [(e, e ^ 1) for e in range(n_expert)])
    far = [b for block in far for b in (block, lax.ppermute(block, "etp", swap))]

    parts = 4
    halves = [
        jax.ShapeDtypeStruct((side // 2, width), jnp.float32),
        jax.ShapeDtypeStruct((side // 2, width), jnp.bfloat16),
    ]
    far_kept, far_sent, rest = pl.pallas_call(
        functools.partial(ffn_kernel, n_expert, parts),
        out_shape=halves + [jax.ShapeDtypeStruct((side, w_gate.shape[1]), jnp.bfloat16)],
        in_specs=[VMEM] * (n_expert + 4),
        out_specs=[VMEM] * 3,
        scratch_shapes=[pltpu.VMEM((n_expert * tok, width), jnp.bfloat16)],
        compiler_params=GRANT,
        name="ffn",
    )(own, next_block, order, *far, w_gate, w_up, w_down)
    near_kept, near_sent = pl.pallas_call(
        functools.partial(down_kernel, parts),
        out_shape=halves,
        in_specs=[VMEM] * 2,
        out_specs=[VMEM] * 2,
        compiler_params=GRANT,
        name="down",
    )(rest, w_down)

    turns = [
        [(t, 2 * ((t // 2 + h) % pairs) + t % 2) for t in range(n_etp)] for h in range(1, pairs)
    ]

    def add(kept, sent, counts):
        shapes = [
            jax.ShapeDtypeStruct((count * rows, width), jnp.bfloat16 if h else jnp.float32)
            for count in counts
            for h in range(pairs)
        ]
        sums = pl.pallas_call(
            functools.partial(add_kernel, pairs),
            out_shape=shapes,
            in_specs=[VMEM] * 2,
            out_specs=[VMEM] * len(shapes),
            compiler_params=GRANT,
            name="add",
        )(kept, lax.ppermute(sent, "etp", swap))
        return [sums[i * pairs : (i + 1) * pairs] for i in range(len(counts))]

    def over_pairs(own, *others):
        take = own.shape[0] // rows
        landed = [lax.ppermute(piece, "etp", turn) for piece, turn in zip(others, turns)]
        return list(
            pl.pallas_call(
                functools.partial(fold_kernel, pairs),
                out_shape=[jax.ShapeDtypeStruct((rows, width), jnp.bfloat16)] * take,
                in_specs=[VMEM] * pairs,
                out_specs=[VMEM] * take,
                compiler_params=GRANT,
                name="fold",
            )(own, *landed)
        )

    half = n_expert // 2
    first, second = add(far_kept, far_sent, (half // 2, half - half // 2))
    pieces = over_pairs(*first) + over_pairs(*second)
    own, last = add(near_kept, near_sent, (1, half - 1))
    last = over_pairs(*last)
    pieces += last
    own, *others = own
    own = [own] + [lax.ppermute(piece, "etp", turn) for piece, turn in zip(others, turns)]
    landed = []
    for k, piece in enumerate(pieces, 1):
        route = [(e, (e + k) % n_expert) for e in range(n_expert)]
        landed.append(lax.ppermute(piece, "expert", route))

    return pl.pallas_call(
        functools.partial(mix_kernel, n_expert, pairs),
        out_shape=jax.ShapeDtypeStruct((rows, width), jnp.bfloat16),
        in_specs=[VMEM] * (1 + n_expert + pairs),
        out_specs=VMEM,
        compiler_params=GRANT,
        name="mix",
    )(expert_ids.T, route_weights.T, *own, *landed)


def solution(mesh):
    in_specs = (
        P(("group", "expert"), None),
        P(("group", "expert"), None),
        P(("group", "expert", "etp"), None),
        P("expert", "etp", None),
        P("expert", "etp", None),
        P("expert", "etp", None),
    )
    out_specs = P(("group", "expert", "etp"), None)
    return jax.shard_map(
        functools.partial(on_device, mesh.shape["expert"], mesh.shape["etp"]),
        mesh=mesh,
        in_specs=in_specs,
        out_specs=out_specs,
        check_vma=False,
    )
```

```python
import functools

import jax
import jax.numpy as jnp
from jax import lax
from jax.experimental import pallas as pl
from jax.experimental.pallas import tpu as pltpu
from jax.sharding import PartitionSpec as P

VMEM = pl.BlockSpec(memory_space=pltpu.VMEM)
GRANT = pltpu.CompilerParams(vmem_limit_bytes=16 * 1024 * 1024)
AHEAD = pl.CostEstimate(flops=10**10, bytes_accessed=0, transcendentals=0)
HBM = pl.BlockSpec(memory_space=pltpu.HBM)


def ring(place, n_expert):
    place = (place + n_expert) % n_expert if isinstance(place, int) else lax.rem(place + n_expert, n_expert)
    return place ^ (place >> 1)


def ring_place(n_expert):
    expert = lax.axis_index("expert")
    place = expert
    for shift in range(1, n_expert.bit_length() - 1):
        place = place ^ (expert >> shift)
    return place


def fetch_kernel(tokens, own, sem):
    copy = pltpu.make_async_copy(tokens, own, sem)
    copy.start()
    copy.wait()


def order_kernel(n_expert, pairs, rows, own, out):
    del own
    total = out.shape[0]
    me = lax.axis_index("etp")
    core, pair = lax.rem(me, 2), lax.div(me, 2)
    place = lax.broadcasted_iota(jnp.int32, (total, total), 0)
    source = lax.broadcasted_iota(jnp.int32, (total, total), 1)
    half = n_expert // 2
    row = lax.rem(place, rows)
    k = lax.rem(lax.div(place, rows), half)
    h = lax.rem(lax.div(place, rows * half), pairs)
    sent = lax.rem(lax.div(place, rows * half * pairs), 2)
    second = lax.div(place, rows * half * pairs * 2)
    shift = jnp.where(second == 0, k + 1, jnp.where(k == 0, 0, k + half))
    expert = lax.axis_index("expert")
    k = lax.bitwise_xor(expert, ring(ring_place(n_expert) + shift, n_expert))
    block = 2 * lax.rem(pair + h, pairs) + lax.rem(core + sent, 2)
    wanted = (k * pairs * 2 + block) * rows + row
    out[...] = jnp.where(source == wanted, 1.0, 0.0).astype(jnp.bfloat16)


def ffn_kernel(n_expert, parts, own, next_block, order, *refs):
    far = refs[: n_expert - 2]
    w_gate, w_up, w_down, kept, sent, rest, x = refs[n_expert - 2 :]
    core = lax.rem(lax.axis_index("etp"), 2)
    tok = own.shape[0]
    x[0:tok, :] = own[...]
    x[tok : 2 * tok, :] = next_block[...]
    for i in range(0, n_expert - 2, 2):
        for block, k in ((far[i], i + 2 + core), (far[i + 1], i + 3 - core)):
            x[pl.ds(pl.multiple_of(k * tok, tok), tok), :] = block[...]
    contract = (((1,), (1,)), ((), ()))
    gate = lax.dot_general(w_gate[0], x[...], contract, preferred_element_type=jnp.float32)
    upper = lax.dot_general(w_up[0], x[...], contract, preferred_element_type=jnp.float32)
    hidden = (gate / (1.0 + jnp.exp(-gate)) * upper).astype(jnp.bfloat16)
    hidden = lax.dot_general(order[...], hidden, contract, preferred_element_type=jnp.float32)
    hidden = hidden.astype(jnp.bfloat16)
    now = rest.shape[0]
    rest[...] = hidden[now:]
    down(parts, hidden[:now], w_down, kept, sent)


def down(parts, hidden, w_down, kept, sent):
    side, width = kept.shape
    step = width // parts
    for c in range(parts):
        cols = slice(c * step, (c + 1) * step)
        out = jnp.dot(hidden, w_down[0, :, cols], preferred_element_type=jnp.float32)
        kept[:, cols] = out[:side]
        sent[:, cols] = out[side:].astype(jnp.bfloat16)


def down_kernel(parts, hidden, w_down, kept, sent):
    down(parts, hidden[...], w_down, kept, sent)


def add_kernel(pairs, kept, arrived, *refs):
    start = 0
    for h in range(pairs):
        for out in refs[h::pairs]:
            at = slice(start, start + out.shape[0])
            out[...] = (kept[at, :] + arrived[at, :].astype(jnp.float32)).astype(out.dtype)
            start += out.shape[0]


def fold_kernel(pairs, own, *refs):
    arrived, pieces = refs[: pairs - 1], refs[pairs - 1 :]
    total = own[...]
    for block in arrived:
        total = total + block[...].astype(jnp.float32)
    rows = pieces[0].shape[0]
    for k, piece in enumerate(pieces):
        piece[...] = total[k * rows : (k + 1) * rows].astype(piece.dtype)


def mix_kernel(n_expert, pairs, ids, weights, *refs):
    own, pieces, out = refs[:pairs], refs[pairs:-1], refs[-1]
    rows = out.shape[0]
    me, place = lax.axis_index("etp"), ring_place(n_expert)
    top, tok = ids.shape

    def column(ref, start, i):
        lane = lax.broadcasted_iota(jnp.int32, (rows, ref.shape[1]), 1)
        row = lax.broadcasted_iota(jnp.int32, (rows, ref.shape[1]), 0)
        values = jnp.where(lane == start + row, ref[i : i + 1, :], 0)
        return jnp.sum(values, axis=1, keepdims=True)

    own_ids = [column(ids, me * rows, i) for i in range(top)]
    own_weights = [column(weights, 0, i) for i in range(top)]
    scale = sum(own_weights)
    for k in range(n_expert):
        owner = ring(place - k, n_expert)
        factor = sum(jnp.where(own_ids[i] == owner, own_weights[i], 0.0) for i in range(top)) / scale
        if k == 0:
            total = sum(block[...].astype(jnp.float32) for block in own) * factor
        else:
            total = total + pieces[k - 1][...].astype(jnp.float32) * factor
    out[...] = total.astype(out.dtype)


def on_device(n_expert, n_etp, tokens, expert_ids, route_weights, w_gate, w_up, w_down):
    tok, width = tokens.shape
    rows = tok // n_etp
    pairs = n_etp // 2
    side = n_expert * tok // 2

    own = pl.pallas_call(
        fetch_kernel,
        out_shape=jax.ShapeDtypeStruct((tok, width), tokens.dtype),
        in_specs=[HBM],
        out_specs=VMEM,
        scratch_shapes=[pltpu.SemaphoreType.DMA],
        compiler_params=GRANT,
        name="fetch",
    )(pltpu.with_memory_space_constraint(tokens, pltpu.HBM))
    order = pl.pallas_call(
        functools.partial(order_kernel, n_expert, pairs, rows),
        out_shape=jax.ShapeDtypeStruct((2 * side, 2 * side), jnp.bfloat16),
        in_specs=[VMEM],
        out_specs=VMEM,
        cost_estimate=AHEAD,
        compiler_params=GRANT,
        name="order",
    )(own)

    swap = [(t, t ^ 1) for t in range(n_etp)]
    far = []
    for k in range(2, n_expert, 2):
        route = [
            (e * n_etp + t, (e ^ (k + t % 2)) * n_etp + t)
            for e in range(n_expert)
            for t in range(n_etp)
        ]
        far.append(lax.ppermute(tokens, ("expert", "etp"), route))
    next_block = lax.ppermute(tokens, "expert", [(e, e ^ 1) for e in range(n_expert)])
    far = [b for block in far for b in (block, lax.ppermute(block, "etp", swap))]

    parts = 4
    halves = [
        jax.ShapeDtypeStruct((side // 2, width), jnp.float32),
        jax.ShapeDtypeStruct((side // 2, width), jnp.bfloat16),
    ]
    far_kept, far_sent, rest = pl.pallas_call(
        functools.partial(ffn_kernel, n_expert, parts),
        out_shape=halves + [jax.ShapeDtypeStruct((side, w_gate.shape[1]), jnp.bfloat16)],
        in_specs=[VMEM] * (n_expert + 4),
        out_specs=[VMEM] * 3,
        scratch_shapes=[pltpu.VMEM((n_expert * tok, width), jnp.bfloat16)],
        compiler_params=GRANT,
        name="ffn",
    )(own, next_block, order, *far, w_gate, w_up, w_down)
    near_kept, near_sent = pl.pallas_call(
        functools.partial(down_kernel, parts),
        out_shape=halves,
        in_specs=[VMEM] * 2,
        out_specs=[VMEM] * 2,
        compiler_params=GRANT,
        name="down",
    )(rest, w_down)

    turns = [
        [(t, 2 * ((t // 2 + h) % pairs) + t % 2) for t in range(n_etp)] for h in range(1, pairs)
    ]

    def add(kept, sent, counts):
        shapes = [
            jax.ShapeDtypeStruct((count * rows, width), jnp.bfloat16 if h else jnp.float32)
            for count in counts
            for h in range(pairs)
        ]
        sums = pl.pallas_call(
            functools.partial(add_kernel, pairs),
            out_shape=shapes,
            in_specs=[VMEM] * 2,
            out_specs=[VMEM] * len(shapes),
            compiler_params=GRANT,
            name="add",
        )(kept, lax.ppermute(sent, "etp", swap))
        return [sums[i * pairs : (i + 1) * pairs] for i in range(len(counts))]

    def over_pairs(own, *others):
        take = own.shape[0] // rows
        landed = [lax.ppermute(piece, "etp", turn) for piece, turn in zip(others, turns)]
        return list(
            pl.pallas_call(
                functools.partial(fold_kernel, pairs),
                out_shape=[jax.ShapeDtypeStruct((rows, width), jnp.bfloat16)] * take,
                in_specs=[VMEM] * pairs,
                out_specs=[VMEM] * take,
                compiler_params=GRANT,
                name="fold",
            )(own, *landed)
        )

    half = n_expert // 2
    first, second = add(far_kept, far_sent, (half // 2, half - half // 2))
    pieces = over_pairs(*first) + over_pairs(*second)
    own, last = add(near_kept, near_sent, (1, half - 1))
    last = over_pairs(*last)
    pieces += last
    own, *others = own
    own = [own] + [lax.ppermute(piece, "etp", turn) for piece, turn in zip(others, turns)]
    landed = []
    for k, piece in enumerate(pieces, 1):
        route = [(ring(i, n_expert), ring(i + k, n_expert)) for i in range(n_expert)]
        landed.append(lax.ppermute(piece, "expert", route))

    return pl.pallas_call(
        functools.partial(mix_kernel, n_expert, pairs),
        out_shape=jax.ShapeDtypeStruct((rows, width), jnp.bfloat16),
        in_specs=[VMEM] * (1 + n_expert + pairs),
        out_specs=VMEM,
        compiler_params=GRANT,
        name="mix",
    )(expert_ids.T, route_weights.T, *own, *landed)


def solution(mesh):
    in_specs = (
        P(("group", "expert"), None),
        P(("group", "expert"), None),
        P(("group", "expert", "etp"), None),
        P("expert", "etp", None),
        P("expert", "etp", None),
        P("expert", "etp", None),
    )
    out_specs = P(("group", "expert", "etp"), None)
    return jax.shard_map(
        functools.partial(on_device, mesh.shape["expert"], mesh.shape["etp"]),
        mesh=mesh,
        in_specs=in_specs,
        out_specs=out_specs,
        check_vma=False,
    )
```

```python
import functools

import jax
import jax.numpy as jnp
from jax import lax
from jax.experimental import pallas as pl
from jax.experimental.pallas import tpu as pltpu
from jax.sharding import PartitionSpec as P

VMEM = pl.BlockSpec(memory_space=pltpu.VMEM)
GRANT = pltpu.CompilerParams(vmem_limit_bytes=16 * 1024 * 1024)
AHEAD = pl.CostEstimate(flops=10**10, bytes_accessed=0, transcendentals=0)
HBM = pl.BlockSpec(memory_space=pltpu.HBM)


def fetch_kernel(tokens, own, sem):
    copy = pltpu.make_async_copy(tokens, own, sem)
    copy.start()
    copy.wait()


def order_kernel(n_expert, pairs, rows, own, out):
    del own
    total = out.shape[0]
    me = lax.axis_index("etp")
    core, pair = lax.rem(me, 2), lax.div(me, 2)
    place = lax.broadcasted_iota(jnp.int32, (total, total), 0)
    source = lax.broadcasted_iota(jnp.int32, (total, total), 1)
    half = n_expert // 2
    row = lax.rem(place, rows)
    k = lax.rem(lax.div(place, rows), half)
    h = lax.rem(lax.div(place, rows * half), pairs)
    sent = lax.rem(lax.div(place, rows * half * pairs), 2)
    second = lax.div(place, rows * half * pairs * 2)
    shift = jnp.where(second == 0, k + 1, jnp.where(k == 0, 0, k + half))
    expert = lax.axis_index("expert")
    k = lax.bitwise_xor(expert, lax.rem(expert + shift, n_expert))
    block = 2 * lax.rem(pair + h, pairs) + lax.rem(core + sent, 2)
    wanted = (k * pairs * 2 + block) * rows + row
    out[...] = jnp.where(source == wanted, 1.0, 0.0).astype(jnp.bfloat16)


TILE = 256


def tiles_of(unit, count):
    return [t for t in range(count) if 2 * t + 1 == count or (2 * t < count) == (unit == 0)]


def staged(unit, x, weights, accs):
    hidden, width = weights[0].shape[1:]
    count = len(weights) * hidden // TILE

    def rows_of(tile, cols):
        parts, start = [], tile * TILE
        while start < (tile + 1) * TILE:
            i, at = divmod(start, hidden)
            size = min(hidden - at, (tile + 1) * TILE - start)
            parts.append(weights[i][0, at : at + size, cols])
            start += size
        return parts[0] if len(parts) == 1 else jnp.concatenate(parts, axis=0)

    steps = []
    for slot, tile in enumerate(tiles_of(unit, count)):
        shared = 2 * tile + 1 == count
        for i in range(width // TILE):
            if not shared or i % 2 == unit:
                steps.append((slot, tile, slice(i * TILE, (i + 1) * TILE)))
    for i, (slot, tile, cols) in enumerate(steps):
        pltpu.matmul_push_rhs(rows_of(tile, cols), i % 2, unit, transpose=True)
        yield
        if i:
            last, _, before = steps[i - 1]
            pltpu.matmul_acc_lhs(accs[last], x[:, before], load_staged_rhs=(i - 1) % 2)
        yield
    last, _, before = steps[-1]
    pltpu.matmul_acc_lhs(accs[last], x[:, before], load_staged_rhs=(len(steps) - 1) % 2)


def stacked_product(x, weights, accs):
    count = len(weights) * weights[0].shape[1] // TILE
    running = [staged(unit, x, weights, accs[unit]) for unit in range(2)]
    while running:
        running = [steps for steps in running if next(steps, running) is None]
    columns = [None] * count
    for unit in range(2):
        for slot, tile in enumerate(tiles_of(unit, count)):
            part = pltpu.matmul_pop(accs[unit][slot])
            columns[tile] = part if columns[tile] is None else columns[tile] + part
    return jnp.concatenate(columns, axis=1)


def hidden_kernel(n_expert, own, next_block, *refs):
    far = refs[: n_expert - 2]
    w_gate, w_up, out, x = refs[n_expert - 2 :]
    core = lax.rem(lax.axis_index("etp"), 2)
    tok = own.shape[0]
    x[0:tok, :] = own[...]
    x[tok : 2 * tok, :] = next_block[...]
    for i in range(0, n_expert - 2, 2):
        for block, k in ((far[i], i + 2 + core), (far[i + 1], i + 3 - core)):
            x[pl.ds(pl.multiple_of(k * tok, tok), tok), :] = block[...]
    size = w_gate.shape[1]
    if x.shape[0] <= TILE and 2 * size % TILE == 0 and size % 128 == 0:
        columns = 2 * size // TILE
        first = len(tiles_of(0, columns))
        both = pl.run_scoped(
            lambda *accs: stacked_product(x, (w_gate, w_up), (accs[:first], accs[first:])),
            *(
                pltpu.ACC(unit)((x.shape[0], TILE), jnp.float32)
                for unit in range(2)
                for _ in tiles_of(unit, columns)
            ),
        )
        gate, upper = both[:, :size], both[:, size:]
    else:
        contract = (((1,), (1,)), ((), ()))
        gate = lax.dot_general(x[...], w_gate[0], contract, preferred_element_type=jnp.float32)
        upper = lax.dot_general(x[...], w_up[0], contract, preferred_element_type=jnp.float32)
    out[...] = (gate / (1.0 + jnp.exp(-gate)) * upper).astype(out.dtype)


def ffn_kernel(parts, order, hidden, w_down, kept, sent, rest):
    hidden = jnp.dot(order[...], hidden[...], preferred_element_type=jnp.float32)
    hidden = hidden.astype(jnp.bfloat16)
    now = rest.shape[0]
    rest[...] = hidden[now:]
    down(parts, hidden[:now], w_down, kept, sent)


def down(parts, hidden, w_down, kept, sent):
    side, width = kept.shape
    step = width // parts
    for c in range(parts):
        cols = slice(c * step, (c + 1) * step)
        out = jnp.dot(hidden, w_down[0, :, cols], preferred_element_type=jnp.float32)
        kept[:, cols] = out[:side]
        sent[:, cols] = out[side:].astype(jnp.bfloat16)


def down_kernel(parts, hidden, w_down, kept, sent):
    down(parts, hidden[...], w_down, kept, sent)


def add_kernel(pairs, kept, arrived, *refs):
    start = 0
    for h in range(pairs):
        for out in refs[h::pairs]:
            at = slice(start, start + out.shape[0])
            out[...] = (kept[at, :] + arrived[at, :].astype(jnp.float32)).astype(out.dtype)
            start += out.shape[0]


def fold_kernel(pairs, own, *refs):
    arrived, pieces = refs[: pairs - 1], refs[pairs - 1 :]
    total = own[...]
    for block in arrived:
        total = total + block[...].astype(jnp.float32)
    rows = pieces[0].shape[0]
    for k, piece in enumerate(pieces):
        piece[...] = total[k * rows : (k + 1) * rows].astype(piece.dtype)


def mix_kernel(n_expert, pairs, ids, weights, *refs):
    own, pieces, out = refs[:pairs], refs[pairs:-1], refs[-1]
    rows = out.shape[0]
    me, expert = lax.axis_index("etp"), lax.axis_index("expert")
    top, tok = ids.shape

    def column(ref, start, i):
        lane = lax.broadcasted_iota(jnp.int32, (rows, ref.shape[1]), 1)
        row = lax.broadcasted_iota(jnp.int32, (rows, ref.shape[1]), 0)
        values = jnp.where(lane == start + row, ref[i : i + 1, :], 0)
        return jnp.sum(values, axis=1, keepdims=True)

    own_ids = [column(ids, me * rows, i) for i in range(top)]
    own_weights = [column(weights, 0, i) for i in range(top)]
    scale = sum(own_weights)
    for k in range(n_expert):
        owner = lax.rem(expert - k + n_expert, n_expert)
        factor = sum(jnp.where(own_ids[i] == owner, own_weights[i], 0.0) for i in range(top)) / scale
        if k == 0:
            total = sum(block[...].astype(jnp.float32) for block in own) * factor
        else:
            total = total + pieces[k - 1][...].astype(jnp.float32) * factor
    out[...] = total.astype(out.dtype)


def on_device(n_expert, n_etp, tokens, expert_ids, route_weights, w_gate, w_up, w_down):
    tok, width = tokens.shape
    rows = tok // n_etp
    pairs = n_etp // 2
    side = n_expert * tok // 2

    own = pl.pallas_call(
        fetch_kernel,
        out_shape=jax.ShapeDtypeStruct((tok, width), tokens.dtype),
        in_specs=[HBM],
        out_specs=VMEM,
        scratch_shapes=[pltpu.SemaphoreType.DMA],
        compiler_params=GRANT,
        name="fetch",
    )(pltpu.with_memory_space_constraint(tokens, pltpu.HBM))
    order = pl.pallas_call(
        functools.partial(order_kernel, n_expert, pairs, rows),
        out_shape=jax.ShapeDtypeStruct((2 * side, 2 * side), jnp.bfloat16),
        in_specs=[VMEM],
        out_specs=VMEM,
        cost_estimate=AHEAD,
        compiler_params=GRANT,
        name="order",
    )(own)

    swap = [(t, t ^ 1) for t in range(n_etp)]
    far = []
    for k in range(2, n_expert, 2):
        route = [
            (e * n_etp + t, (e ^ (k + t % 2)) * n_etp + t)
            for e in range(n_expert)
            for t in range(n_etp)
        ]
        far.append(lax.ppermute(tokens, ("expert", "etp"), route))
    next_block = lax.ppermute(tokens, "expert", [(e, e ^ 1) for e in range(n_expert)])
    far = [b for block in far for b in (block, lax.ppermute(block, "etp", swap))]

    parts = 4
    halves = [
        jax.ShapeDtypeStruct((side // 2, width), jnp.float32),
        jax.ShapeDtypeStruct((side // 2, width), jnp.bfloat16),
    ]
    hidden = pl.pallas_call(
        functools.partial(hidden_kernel, n_expert),
        out_shape=jax.ShapeDtypeStruct((n_expert * tok, w_gate.shape[1]), jnp.bfloat16),
        in_specs=[VMEM] * (n_expert + 2),
        out_specs=VMEM,
        scratch_shapes=[pltpu.VMEM((n_expert * tok, width), jnp.bfloat16)],
        compiler_params=GRANT,
        name="hidden",
    )(own, next_block, *far, w_gate, w_up)
    far_kept, far_sent, rest = pl.pallas_call(
        functools.partial(ffn_kernel, parts),
        out_shape=halves + [jax.ShapeDtypeStruct((side, w_gate.shape[1]), jnp.bfloat16)],
        in_specs=[VMEM] * 3,
        out_specs=[VMEM] * 3,
        compiler_params=GRANT,
        name="ffn",
    )(order, hidden, w_down)
    near_kept, near_sent = pl.pallas_call(
        functools.partial(down_kernel, parts),
        out_shape=halves,
        in_specs=[VMEM] * 2,
        out_specs=[VMEM] * 2,
        compiler_params=GRANT,
        name="down",
    )(rest, w_down)

    turns = [
        [(t, 2 * ((t // 2 + h) % pairs) + t % 2) for t in range(n_etp)] for h in range(1, pairs)
    ]

    def add(kept, sent, counts):
        shapes = [
            jax.ShapeDtypeStruct((count * rows, width), jnp.bfloat16 if h else jnp.float32)
            for count in counts
            for h in range(pairs)
        ]
        sums = pl.pallas_call(
            functools.partial(add_kernel, pairs),
            out_shape=shapes,
            in_specs=[VMEM] * 2,
            out_specs=[VMEM] * len(shapes),
            compiler_params=GRANT,
            name="add",
        )(kept, lax.ppermute(sent, "etp", swap))
        return [sums[i * pairs : (i + 1) * pairs] for i in range(len(counts))]

    def over_pairs(own, *others):
        take = own.shape[0] // rows
        landed = [lax.ppermute(piece, "etp", turn) for piece, turn in zip(others, turns)]
        return list(
            pl.pallas_call(
                functools.partial(fold_kernel, pairs),
                out_shape=[jax.ShapeDtypeStruct((rows, width), jnp.bfloat16)] * take,
                in_specs=[VMEM] * pairs,
                out_specs=[VMEM] * take,
                compiler_params=GRANT,
                name="fold",
            )(own, *landed)
        )

    half = n_expert // 2
    first, second = add(far_kept, far_sent, (half // 2, half - half // 2))
    pieces = over_pairs(*first) + over_pairs(*second)
    own, last = add(near_kept, near_sent, (1, half - 1))
    last = over_pairs(*last)
    pieces += last
    own, *others = own
    own = [own] + [lax.ppermute(piece, "etp", turn) for piece, turn in zip(others, turns)]
    landed = []
    for k, piece in enumerate(pieces, 1):
        route = [(e, (e + k) % n_expert) for e in range(n_expert)]
        landed.append(lax.ppermute(piece, "expert", route))

    return pl.pallas_call(
        functools.partial(mix_kernel, n_expert, pairs),
        out_shape=jax.ShapeDtypeStruct((rows, width), jnp.bfloat16),
        in_specs=[VMEM] * (1 + n_expert + pairs),
        out_specs=VMEM,
        compiler_params=GRANT,
        name="mix",
    )(expert_ids.T, route_weights.T, *own, *landed)


def solution(mesh):
    in_specs = (
        P(("group", "expert"), None),
        P(("group", "expert"), None),
        P(("group", "expert", "etp"), None),
        P("expert", "etp", None),
        P("expert", "etp", None),
        P("expert", "etp", None),
    )
    out_specs = P(("group", "expert", "etp"), None)
    return jax.shard_map(
        functools.partial(on_device, mesh.shape["expert"], mesh.shape["etp"]),
        mesh=mesh,
        in_specs=in_specs,
        out_specs=out_specs,
        check_vma=False,
    )
```

```python
import functools

import jax
import jax.numpy as jnp
from jax import lax
from jax.experimental import pallas as pl
from jax.experimental.pallas import tpu as pltpu
from jax.sharding import PartitionSpec as P

VMEM = pl.BlockSpec(memory_space=pltpu.VMEM)
GRANT = pltpu.CompilerParams(vmem_limit_bytes=16 * 1024 * 1024)
AHEAD = pl.CostEstimate(flops=10**10, bytes_accessed=0, transcendentals=0)
HBM = pl.BlockSpec(memory_space=pltpu.HBM)


def fetch_kernel(tokens, own, sem):
    copy = pltpu.make_async_copy(tokens, own, sem)
    copy.start()
    copy.wait()


def order_kernel(n_expert, pairs, rows, own, out):
    del own
    total = out.shape[0]
    me = lax.axis_index("etp")
    core, pair = lax.rem(me, 2), lax.div(me, 2)
    place = lax.broadcasted_iota(jnp.int32, (total, total), 0)
    source = lax.broadcasted_iota(jnp.int32, (total, total), 1)
    half = n_expert // 2
    row = lax.rem(place, rows)
    k = lax.rem(lax.div(place, rows), half)
    h = lax.rem(lax.div(place, rows * half), pairs)
    sent = lax.rem(lax.div(place, rows * half * pairs), 2)
    second = lax.div(place, rows * half * pairs * 2)
    shift = jnp.where(second == 0, k + 1, jnp.where(k == 0, 0, k + half))
    expert = lax.axis_index("expert")
    k = lax.bitwise_xor(expert, lax.rem(expert + shift, n_expert))
    block = 2 * lax.rem(pair + h, pairs) + lax.rem(core + sent, 2)
    wanted = (k * pairs * 2 + block) * rows + row
    out[...] = jnp.where(source == wanted, 1.0, 0.0).astype(jnp.bfloat16)


TILE = 256


CHUNK = 128


def streamed_products(x, weights, accs):
    columns = x.shape[1] // TILE

    def stage(i):
        rows = x[:, i * TILE : (i + 1) * TILE]
        for unit in range(len(weights)):
            pltpu.matmul_push_rhs(rows, i % 2, unit, transpose=True)

    stage(0)
    for i in range(columns):
        cols = slice(i * TILE, (i + 1) * TILE)
        for c in range(len(accs[0])):
            span = slice(c * CHUNK, (c + 1) * CHUNK)
            for unit, w in enumerate(weights):
                pltpu.matmul_acc_lhs(
                    accs[unit][c], w[0, span, cols], load_staged_rhs=None if c else i % 2
                )
            if c == 0 and i + 1 < columns:
                stage(i + 1)


def hidden_kernel(n_expert, own, next_block, *refs):
    far = refs[: n_expert - 2]
    w_gate, w_up, out, x = refs[n_expert - 2 :]
    core = lax.rem(lax.axis_index("etp"), 2)
    tok = own.shape[0]
    x[0:tok, :] = own[...]
    x[tok : 2 * tok, :] = next_block[...]
    for i in range(0, n_expert - 2, 2):
        for block, k in ((far[i], i + 2 + core), (far[i + 1], i + 3 - core)):
            x[pl.ds(pl.multiple_of(k * tok, tok), tok), :] = block[...]
    size, count = out.shape

    def silu(gate, upper):
        return (gate / (1.0 + jnp.exp(-gate)) * upper).astype(out.dtype)

    def by_units(*accs):
        half = len(accs) // 2
        streamed_products(x, (w_gate, w_up), (accs[:half], accs[half:]))
        for c in range(half):
            gate, upper = pltpu.matmul_pop(accs[c]), pltpu.matmul_pop(accs[half + c])
            out[c * CHUNK : (c + 1) * CHUNK] = silu(gate[:, :count], upper[:, :count])

    if x.shape[0] == TILE:
        chunk = [pltpu.ACC(unit)((CHUNK, TILE), jnp.float32) for unit in range(2)]
        pl.run_scoped(by_units, *([chunk[0]] * (size // CHUNK) + [chunk[1]] * (size // CHUNK)))
    else:
        contract = (((1,), (1,)), ((), ()))
        gate = lax.dot_general(w_gate[0], x[...], contract, preferred_element_type=jnp.float32)
        upper = lax.dot_general(w_up[0], x[...], contract, preferred_element_type=jnp.float32)
        out[...] = silu(gate, upper)


def ffn_kernel(parts, order, hidden, w_down, kept, sent, rest):
    contract = (((1,), (1,)), ((), ()))
    hidden = lax.dot_general(
        order[...], hidden[...], contract, preferred_element_type=jnp.float32
    )
    hidden = hidden.astype(jnp.bfloat16)
    now = rest.shape[0]
    rest[...] = hidden[now:]
    down(parts, hidden[:now], w_down, kept, sent)


def down(parts, hidden, w_down, kept, sent):
    side, width = kept.shape
    step = width // parts
    for c in range(parts):
        cols = slice(c * step, (c + 1) * step)
        out = jnp.dot(hidden, w_down[0, :, cols], preferred_element_type=jnp.float32)
        kept[:, cols] = out[:side]
        sent[:, cols] = out[side:].astype(jnp.bfloat16)


def down_kernel(parts, hidden, w_down, kept, sent):
    down(parts, hidden[...], w_down, kept, sent)


def add_kernel(pairs, kept, arrived, *refs):
    start = 0
    for h in range(pairs):
        for out in refs[h::pairs]:
            at = slice(start, start + out.shape[0])
            out[...] = (kept[at, :] + arrived[at, :].astype(jnp.float32)).astype(out.dtype)
            start += out.shape[0]


def fold_kernel(pairs, own, *refs):
    arrived, pieces = refs[: pairs - 1], refs[pairs - 1 :]
    total = own[...]
    for block in arrived:
        total = total + block[...].astype(jnp.float32)
    rows = pieces[0].shape[0]
    for k, piece in enumerate(pieces):
        piece[...] = total[k * rows : (k + 1) * rows].astype(piece.dtype)


def mix_kernel(n_expert, pairs, ids, weights, *refs):
    own, pieces, out = refs[:pairs], refs[pairs:-1], refs[-1]
    rows = out.shape[0]
    me, expert = lax.axis_index("etp"), lax.axis_index("expert")
    top, tok = ids.shape

    def column(ref, start, i):
        lane = lax.broadcasted_iota(jnp.int32, (rows, ref.shape[1]), 1)
        row = lax.broadcasted_iota(jnp.int32, (rows, ref.shape[1]), 0)
        values = jnp.where(lane == start + row, ref[i : i + 1, :], 0)
        return jnp.sum(values, axis=1, keepdims=True)

    own_ids = [column(ids, me * rows, i) for i in range(top)]
    own_weights = [column(weights, 0, i) for i in range(top)]
    scale = sum(own_weights)
    for k in range(n_expert):
        owner = lax.rem(expert - k + n_expert, n_expert)
        factor = sum(jnp.where(own_ids[i] == owner, own_weights[i], 0.0) for i in range(top)) / scale
        if k == 0:
            total = sum(block[...].astype(jnp.float32) for block in own) * factor
        else:
            total = total + pieces[k - 1][...].astype(jnp.float32) * factor
    out[...] = total.astype(out.dtype)


def on_device(n_expert, n_etp, tokens, expert_ids, route_weights, w_gate, w_up, w_down):
    tok, width = tokens.shape
    rows = tok // n_etp
    pairs = n_etp // 2
    side = n_expert * tok // 2

    own = pl.pallas_call(
        fetch_kernel,
        out_shape=jax.ShapeDtypeStruct((tok, width), tokens.dtype),
        in_specs=[HBM],
        out_specs=VMEM,
        scratch_shapes=[pltpu.SemaphoreType.DMA],
        compiler_params=GRANT,
        name="fetch",
    )(pltpu.with_memory_space_constraint(tokens, pltpu.HBM))
    order = pl.pallas_call(
        functools.partial(order_kernel, n_expert, pairs, rows),
        out_shape=jax.ShapeDtypeStruct((2 * side, 2 * side), jnp.bfloat16),
        in_specs=[VMEM],
        out_specs=VMEM,
        cost_estimate=AHEAD,
        compiler_params=GRANT,
        name="order",
    )(own)

    swap = [(t, t ^ 1) for t in range(n_etp)]
    far = []
    for k in range(2, n_expert, 2):
        route = [
            (e * n_etp + t, (e ^ (k + t % 2)) * n_etp + t)
            for e in range(n_expert)
            for t in range(n_etp)
        ]
        far.append(lax.ppermute(tokens, ("expert", "etp"), route))
    next_block = lax.ppermute(tokens, "expert", [(e, e ^ 1) for e in range(n_expert)])
    far = [b for block in far for b in (block, lax.ppermute(block, "etp", swap))]

    parts = 4
    halves = [
        jax.ShapeDtypeStruct((side // 2, width), jnp.float32),
        jax.ShapeDtypeStruct((side // 2, width), jnp.bfloat16),
    ]
    by_units = n_expert * tok <= TILE and w_gate.shape[1] % CHUNK == 0 and width % TILE == 0
    hidden = pl.pallas_call(
        functools.partial(hidden_kernel, n_expert),
        out_shape=jax.ShapeDtypeStruct((w_gate.shape[1], n_expert * tok), jnp.bfloat16),
        in_specs=[VMEM] * (n_expert + 2),
        out_specs=VMEM,
        scratch_shapes=[
            pltpu.VMEM((TILE if by_units else n_expert * tok, width), jnp.bfloat16)
        ],
        compiler_params=GRANT,
        name="hidden",
    )(own, next_block, *far, w_gate, w_up)
    far_kept, far_sent, rest = pl.pallas_call(
        functools.partial(ffn_kernel, parts),
        out_shape=halves + [jax.ShapeDtypeStruct((side, w_gate.shape[1]), jnp.bfloat16)],
        in_specs=[VMEM] * 3,
        out_specs=[VMEM] * 3,
        compiler_params=GRANT,
        name="ffn",
    )(order, hidden, w_down)
    near_kept, near_sent = pl.pallas_call(
        functools.partial(down_kernel, parts),
        out_shape=halves,
        in_specs=[VMEM] * 2,
        out_specs=[VMEM] * 2,
        compiler_params=GRANT,
        name="down",
    )(rest, w_down)

    turns = [
        [(t, 2 * ((t // 2 + h) % pairs) + t % 2) for t in range(n_etp)] for h in range(1, pairs)
    ]

    def add(kept, sent, counts):
        shapes = [
            jax.ShapeDtypeStruct((count * rows, width), jnp.bfloat16 if h else jnp.float32)
            for count in counts
            for h in range(pairs)
        ]
        sums = pl.pallas_call(
            functools.partial(add_kernel, pairs),
            out_shape=shapes,
            in_specs=[VMEM] * 2,
            out_specs=[VMEM] * len(shapes),
            compiler_params=GRANT,
            name="add",
        )(kept, lax.ppermute(sent, "etp", swap))
        return [sums[i * pairs : (i + 1) * pairs] for i in range(len(counts))]

    def over_pairs(own, *others):
        take = own.shape[0] // rows
        landed = [lax.ppermute(piece, "etp", turn) for piece, turn in zip(others, turns)]
        return list(
            pl.pallas_call(
                functools.partial(fold_kernel, pairs),
                out_shape=[jax.ShapeDtypeStruct((rows, width), jnp.bfloat16)] * take,
                in_specs=[VMEM] * pairs,
                out_specs=[VMEM] * take,
                compiler_params=GRANT,
                name="fold",
            )(own, *landed)
        )

    half = n_expert // 2
    first, second = add(far_kept, far_sent, (half // 2, half - half // 2))
    pieces = over_pairs(*first) + over_pairs(*second)
    own, last = add(near_kept, near_sent, (1, half - 1))
    last = over_pairs(*last)
    pieces += last
    own, *others = own
    own = [own] + [lax.ppermute(piece, "etp", turn) for piece, turn in zip(others, turns)]
    landed = []
    for k, piece in enumerate(pieces, 1):
        route = [(e, (e + k) % n_expert) for e in range(n_expert)]
        landed.append(lax.ppermute(piece, "expert", route))

    return pl.pallas_call(
        functools.partial(mix_kernel, n_expert, pairs),
        out_shape=jax.ShapeDtypeStruct((rows, width), jnp.bfloat16),
        in_specs=[VMEM] * (1 + n_expert + pairs),
        out_specs=VMEM,
        compiler_params=GRANT,
        name="mix",
    )(expert_ids.T, route_weights.T, *own, *landed)


def solution(mesh):
    in_specs = (
        P(("group", "expert"), None),
        P(("group", "expert"), None),
        P(("group", "expert", "etp"), None),
        P("expert", "etp", None),
        P("expert", "etp", None),
        P("expert", "etp", None),
    )
    out_specs = P(("group", "expert", "etp"), None)
    return jax.shard_map(
        functools.partial(on_device, mesh.shape["expert"], mesh.shape["etp"]),
        mesh=mesh,
        in_specs=in_specs,
        out_specs=out_specs,
        check_vma=False,
    )
```

```python
import functools

import jax
import jax.numpy as jnp
from jax import lax
from jax.experimental import pallas as pl
from jax.experimental.pallas import tpu as pltpu
from jax.sharding import PartitionSpec as P

VMEM = pl.BlockSpec(memory_space=pltpu.VMEM)
GRANT = pltpu.CompilerParams(vmem_limit_bytes=16 * 1024 * 1024)
AHEAD = pl.CostEstimate(flops=10**10, bytes_accessed=0, transcendentals=0)
HBM = pl.BlockSpec(memory_space=pltpu.HBM)


def fetch_kernel(tokens, own, sem):
    copy = pltpu.make_async_copy(tokens, own, sem)
    copy.start()
    copy.wait()


def order_kernel(n_expert, pairs, rows, own, out):
    del own
    total = out.shape[0]
    me = lax.axis_index("etp")
    core, pair = lax.rem(me, 2), lax.div(me, 2)
    place = lax.broadcasted_iota(jnp.int32, (total, total), 0)
    source = lax.broadcasted_iota(jnp.int32, (total, total), 1)
    half = n_expert // 2
    row = lax.rem(place, rows)
    k = lax.rem(lax.div(place, rows), half)
    h = lax.rem(lax.div(place, rows * half), pairs)
    sent = lax.rem(lax.div(place, rows * half * pairs), 2)
    second = lax.div(place, rows * half * pairs * 2)
    shift = jnp.where(second == 0, k + 1, jnp.where(k == 0, 0, k + half))
    expert = lax.axis_index("expert")
    k = lax.bitwise_xor(expert, lax.rem(expert + shift, n_expert))
    block = 2 * lax.rem(pair + h, pairs) + lax.rem(core + sent, 2)
    wanted = (k * pairs * 2 + block) * rows + row
    out[...] = jnp.where(source == wanted, 1.0, 0.0).astype(jnp.bfloat16)


def ffn_kernel(n_expert, parts, own, next_block, order, *refs):
    far = refs[: n_expert - 2]
    w_gate, w_up, w_down, kept, sent, rest, x = refs[n_expert - 2 :]
    core = lax.rem(lax.axis_index("etp"), 2)
    tok = own.shape[0]
    x[0:tok, :] = own[...]
    x[tok : 2 * tok, :] = next_block[...]
    for i in range(0, n_expert - 2, 2):
        for block, k in ((far[i], i + 2 + core), (far[i + 1], i + 3 - core)):
            x[pl.ds(pl.multiple_of(k * tok, tok), tok), :] = block[...]
    contract = (((1,), (1,)), ((), ()))
    gate = lax.dot_general(w_gate[0], x[...], contract, preferred_element_type=jnp.float32)
    upper = lax.dot_general(w_up[0], x[...], contract, preferred_element_type=jnp.float32)
    hidden = (gate / (1.0 + jnp.exp(-gate)) * upper).astype(jnp.bfloat16)
    hidden = lax.dot_general(order[...], hidden, contract, preferred_element_type=jnp.float32)
    hidden = hidden.astype(jnp.bfloat16)
    now = rest.shape[0]
    rest[...] = hidden[now:]
    down(parts, hidden[:now], w_down, kept, sent)


def down(parts, hidden, w_down, kept, sent):
    side, width = kept.shape
    step = width // parts
    for c in range(parts):
        cols = slice(c * step, (c + 1) * step)
        out = jnp.dot(hidden, w_down[0, :, cols], preferred_element_type=jnp.float32)
        kept[:, cols] = out[:side]
        sent[:, cols] = out[side:].astype(jnp.bfloat16)


def down_kernel(parts, hidden, w_down, kept, sent):
    down(parts, hidden[...], w_down, kept, sent)


def add_kernel(pairs, kept, arrived, *refs):
    total = kept[...] + arrived[...].astype(jnp.float32)
    start = 0
    for h in range(pairs):
        for out in refs[h::pairs]:
            out[...] = total[start : start + out.shape[0]].astype(out.dtype)
            start += out.shape[0]


def fold_kernel(pairs, own, *refs):
    arrived, pieces = refs[: pairs - 1], refs[pairs - 1 :]
    total = own[...]
    for block in arrived:
        total = total + block[...].astype(jnp.float32)
    rows = pieces[0].shape[0]
    for k, piece in enumerate(pieces):
        piece[...] = total[k * rows : (k + 1) * rows].astype(piece.dtype)


def mix_kernel(n_expert, pairs, ids, weights, *refs):
    own, pieces, out = refs[:pairs], refs[pairs:-1], refs[-1]
    rows = out.shape[0]
    me, expert = lax.axis_index("etp"), lax.axis_index("expert")
    top, tok = ids.shape

    def column(ref, start, i):
        lane = lax.broadcasted_iota(jnp.int32, (rows, ref.shape[1]), 1)
        row = lax.broadcasted_iota(jnp.int32, (rows, ref.shape[1]), 0)
        values = jnp.where(lane == start + row, ref[i : i + 1, :], 0)
        return jnp.sum(values, axis=1, keepdims=True)

    own_ids = [column(ids, me * rows, i) for i in range(top)]
    own_weights = [column(weights, 0, i) for i in range(top)]
    scale = sum(own_weights)
    for k in range(n_expert):
        owner = lax.rem(expert - k + n_expert, n_expert)
        factor = sum(jnp.where(own_ids[i] == owner, own_weights[i], 0.0) for i in range(top)) / scale
        if k == 0:
            total = sum(block[...].astype(jnp.float32) for block in own) * factor
        else:
            total = total + pieces[k - 1][...].astype(jnp.float32) * factor
    out[...] = total.astype(out.dtype)


def on_device(n_expert, n_etp, tokens, expert_ids, route_weights, w_gate, w_up, w_down):
    tok, width = tokens.shape
    rows = tok // n_etp
    pairs = n_etp // 2
    side = n_expert * tok // 2

    own = pl.pallas_call(
        fetch_kernel,
        out_shape=jax.ShapeDtypeStruct((tok, width), tokens.dtype),
        in_specs=[HBM],
        out_specs=VMEM,
        scratch_shapes=[pltpu.SemaphoreType.DMA],
        compiler_params=GRANT,
        name="fetch",
    )(pltpu.with_memory_space_constraint(tokens, pltpu.HBM))
    order = pl.pallas_call(
        functools.partial(order_kernel, n_expert, pairs, rows),
        out_shape=jax.ShapeDtypeStruct((2 * side, 2 * side), jnp.bfloat16),
        in_specs=[VMEM],
        out_specs=VMEM,
        cost_estimate=AHEAD,
        compiler_params=GRANT,
        name="order",
    )(own)

    swap = [(t, t ^ 1) for t in range(n_etp)]
    far = []
    for k in range(2, n_expert, 2):
        route = [
            (e * n_etp + t, (e ^ (k + t % 2)) * n_etp + t)
            for e in range(n_expert)
            for t in range(n_etp)
        ]
        far.append(lax.ppermute(tokens, ("expert", "etp"), route))
    next_block = lax.ppermute(tokens, "expert", [(e, e ^ 1) for e in range(n_expert)])
    far = [b for block in far for b in (block, lax.ppermute(block, "etp", swap))]

    parts = 4
    halves = [
        jax.ShapeDtypeStruct((side // 2, width), jnp.float32),
        jax.ShapeDtypeStruct((side // 2, width), jnp.bfloat16),
    ]
    far_kept, far_sent, rest = pl.pallas_call(
        functools.partial(ffn_kernel, n_expert, parts),
        out_shape=halves + [jax.ShapeDtypeStruct((side, w_gate.shape[1]), jnp.bfloat16)],
        in_specs=[VMEM] * (n_expert + 4),
        out_specs=[VMEM] * 3,
        scratch_shapes=[pltpu.VMEM((n_expert * tok, width), jnp.bfloat16)],
        compiler_params=GRANT,
        name="ffn",
    )(own, next_block, order, *far, w_gate, w_up, w_down)
    near_kept, near_sent = pl.pallas_call(
        functools.partial(down_kernel, parts),
        out_shape=halves,
        in_specs=[VMEM] * 2,
        out_specs=[VMEM] * 2,
        compiler_params=GRANT,
        name="down",
    )(rest, w_down)

    turns = [
        [(t, 2 * ((t // 2 + h) % pairs) + t % 2) for t in range(n_etp)] for h in range(1, pairs)
    ]

    def add(kept, sent, counts):
        shapes = [
            jax.ShapeDtypeStruct((count * rows, width), jnp.bfloat16 if h else jnp.float32)
            for count in counts
            for h in range(pairs)
        ]
        sums = pl.pallas_call(
            functools.partial(add_kernel, pairs),
            out_shape=shapes,
            in_specs=[VMEM] * 2,
            out_specs=[VMEM] * len(shapes),
            compiler_params=GRANT,
            name="add",
        )(kept, lax.ppermute(sent, "etp", swap))
        return [sums[i * pairs : (i + 1) * pairs] for i in range(len(counts))]

    def over_pairs(own, *others):
        take = own.shape[0] // rows
        landed = [lax.ppermute(piece, "etp", turn) for piece, turn in zip(others, turns)]
        return list(
            pl.pallas_call(
                functools.partial(fold_kernel, pairs),
                out_shape=[jax.ShapeDtypeStruct((rows, width), jnp.bfloat16)] * take,
                in_specs=[VMEM] * pairs,
                out_specs=[VMEM] * take,
                compiler_params=GRANT,
                name="fold",
            )(own, *landed)
        )

    half = n_expert // 2
    first, second = add(far_kept, far_sent, (half // 2, half - half // 2))
    pieces = over_pairs(*first) + over_pairs(*second)
    own, last = add(near_kept, near_sent, (1, half - 1))
    last = over_pairs(*last)
    pieces += last
    own, *others = own
    own = [own] + [lax.ppermute(piece, "etp", turn) for piece, turn in zip(others, turns)]
    landed = []
    for k, piece in enumerate(pieces, 1):
        route = [(e, (e + k) % n_expert) for e in range(n_expert)]
        landed.append(lax.ppermute(piece, "expert", route))

    return pl.pallas_call(
        functools.partial(mix_kernel, n_expert, pairs),
        out_shape=jax.ShapeDtypeStruct((rows, width), jnp.bfloat16),
        in_specs=[VMEM] * (1 + n_expert + pairs),
        out_specs=VMEM,
        compiler_params=GRANT,
        name="mix",
    )(expert_ids.T, route_weights.T, *own, *landed)


def solution(mesh):
    in_specs = (
        P(("group", "expert"), None),
        P(("group", "expert"), None),
        P(("group", "expert", "etp"), None),
        P("expert", "etp", None),
        P("expert", "etp", None),
        P("expert", "etp", None),
    )
    out_specs = P(("group", "expert", "etp"), None)
    return jax.shard_map(
        functools.partial(on_device, mesh.shape["expert"], mesh.shape["etp"]),
        mesh=mesh,
        in_specs=in_specs,
        out_specs=out_specs,
        check_vma=False,
    )
```

```python
import functools

import jax
import jax.numpy as jnp
from jax import lax
from jax.experimental import pallas as pl
from jax.experimental.pallas import tpu as pltpu
from jax.sharding import PartitionSpec as P

VMEM = pl.BlockSpec(memory_space=pltpu.VMEM)
GRANT = pltpu.CompilerParams(vmem_limit_bytes=16 * 1024 * 1024)
AHEAD = pl.CostEstimate(flops=10**10, bytes_accessed=0, transcendentals=0)
HBM = pl.BlockSpec(memory_space=pltpu.HBM)


def fetch_kernel(tokens, own, sem):
    copy = pltpu.make_async_copy(tokens, own, sem)
    copy.start()
    copy.wait()


def order_kernel(n_expert, pairs, rows, own, out):
    del own
    total = out.shape[0]
    me = lax.axis_index("etp")
    core, pair = lax.rem(me, 2), lax.div(me, 2)
    place = lax.broadcasted_iota(jnp.int32, (total, total), 0)
    source = lax.broadcasted_iota(jnp.int32, (total, total), 1)
    half = n_expert // 2
    row = lax.rem(place, rows)
    k = lax.rem(lax.div(place, rows), half)
    h = lax.rem(lax.div(place, rows * half), pairs)
    sent = lax.rem(lax.div(place, rows * half * pairs), 2)
    second = lax.div(place, rows * half * pairs * 2)
    shift = jnp.where(second == 0, k + 1, jnp.where(k == 0, 0, k + half))
    expert = lax.axis_index("expert")
    k = lax.bitwise_xor(expert, lax.rem(expert + shift, n_expert))
    block = 2 * lax.rem(pair + h, pairs) + lax.rem(core + sent, 2)
    wanted = (k * pairs * 2 + block) * rows + row
    out[...] = jnp.where(source == wanted, 1.0, 0.0).astype(jnp.bfloat16)


def ffn_kernel(n_expert, parts, own, next_block, order, *refs):
    far = refs[: n_expert - 2]
    w_gate, w_up, w_down, *outs, x = refs[n_expert - 2 :]
    core = lax.rem(lax.axis_index("etp"), 2)
    tok = own.shape[0]
    x[0:tok, :] = own[...]
    x[tok : 2 * tok, :] = next_block[...]
    for i in range(0, n_expert - 2, 2):
        for block, k in ((far[i], i + 2 + core), (far[i + 1], i + 3 - core)):
            x[pl.ds(pl.multiple_of(k * tok, tok), tok), :] = block[...]
    contract = (((1,), (1,)), ((), ()))
    gate = lax.dot_general(w_gate[0], x[...], contract, preferred_element_type=jnp.float32)
    upper = lax.dot_general(w_up[0], x[...], contract, preferred_element_type=jnp.float32)
    hidden = (gate / (1.0 + jnp.exp(-gate)) * upper).astype(jnp.bfloat16)
    hidden = lax.dot_general(order[...], hidden, contract, preferred_element_type=jnp.float32)
    hidden = hidden.astype(jnp.bfloat16)
    side, width = outs[0].shape
    step = width // parts
    for c in range(parts):
        cols = slice(c * step, (c + 1) * step)
        rows = jnp.dot(hidden, w_down[0, :, cols], preferred_element_type=jnp.float32)
        for i, out in enumerate(outs):
            out[:, cols] = rows[i * side : (i + 1) * side].astype(out.dtype)


def add_kernel(pairs, kept, arrived, *refs):
    total = kept[...] + arrived[...].astype(jnp.float32)
    start = 0
    for h in range(pairs):
        for out in refs[h::pairs]:
            out[...] = total[start : start + out.shape[0]].astype(out.dtype)
            start += out.shape[0]


def fold_kernel(pairs, own, *refs):
    arrived, pieces = refs[: pairs - 1], refs[pairs - 1 :]
    total = own[...]
    for block in arrived:
        total = total + block[...].astype(jnp.float32)
    rows = pieces[0].shape[0]
    for k, piece in enumerate(pieces):
        piece[...] = total[k * rows : (k + 1) * rows].astype(piece.dtype)


def mix_kernel(n_expert, pairs, ids, weights, *refs):
    own, pieces, out = refs[:pairs], refs[pairs:-1], refs[-1]
    rows = out.shape[0]
    me, expert = lax.axis_index("etp"), lax.axis_index("expert")
    top, tok = ids.shape

    def column(ref, start, i):
        lane = lax.broadcasted_iota(jnp.int32, (rows, ref.shape[1]), 1)
        row = lax.broadcasted_iota(jnp.int32, (rows, ref.shape[1]), 0)
        values = jnp.where(lane == start + row, ref[i : i + 1, :], 0)
        return jnp.sum(values, axis=1, keepdims=True)

    own_ids = [column(ids, me * rows, i) for i in range(top)]
    own_weights = [column(weights, 0, i) for i in range(top)]
    scale = sum(own_weights)
    for k in range(n_expert):
        owner = lax.rem(expert - k + n_expert, n_expert)
        factor = sum(jnp.where(own_ids[i] == owner, own_weights[i], 0.0) for i in range(top)) / scale
        if k == 0:
            total = sum(block[...].astype(jnp.float32) for block in own) * factor
        else:
            total = total + pieces[k - 1][...].astype(jnp.float32) * factor
    out[...] = total.astype(out.dtype)


def on_device(n_expert, n_etp, tokens, expert_ids, route_weights, w_gate, w_up, w_down):
    tok, width = tokens.shape
    rows = tok // n_etp
    pairs = n_etp // 2
    side = n_expert * tok // 2

    own = pl.pallas_call(
        fetch_kernel,
        out_shape=jax.ShapeDtypeStruct((tok, width), tokens.dtype),
        in_specs=[HBM],
        out_specs=VMEM,
        scratch_shapes=[pltpu.SemaphoreType.DMA],
        compiler_params=GRANT,
        name="fetch",
    )(pltpu.with_memory_space_constraint(tokens, pltpu.HBM))
    order = pl.pallas_call(
        functools.partial(order_kernel, n_expert, pairs, rows),
        out_shape=jax.ShapeDtypeStruct((2 * side, 2 * side), jnp.bfloat16),
        in_specs=[VMEM],
        out_specs=VMEM,
        cost_estimate=AHEAD,
        compiler_params=GRANT,
        name="order",
    )(own)

    swap = [(t, t ^ 1) for t in range(n_etp)]
    far = []
    for k in range(2, n_expert, 2):
        route = [
            (e * n_etp + t, (e ^ (k + t % 2)) * n_etp + t)
            for e in range(n_expert)
            for t in range(n_etp)
        ]
        far.append(lax.ppermute(tokens, ("expert", "etp"), route))
    next_block = lax.ppermute(tokens, "expert", [(e, e ^ 1) for e in range(n_expert)])
    far = [b for block in far for b in (block, lax.ppermute(block, "etp", swap))]

    parts = 4
    halves = [
        jax.ShapeDtypeStruct((side // 2, width), jnp.float32),
        jax.ShapeDtypeStruct((side // 2, width), jnp.bfloat16),
    ]
    far_kept, far_sent, near_kept, near_sent = pl.pallas_call(
        functools.partial(ffn_kernel, n_expert, parts),
        out_shape=halves * 2,
        in_specs=[VMEM] * (n_expert + 4),
        out_specs=[VMEM] * 4,
        scratch_shapes=[pltpu.VMEM((n_expert * tok, width), jnp.bfloat16)],
        compiler_params=GRANT,
        name="ffn",
    )(own, next_block, order, *far, w_gate, w_up, w_down)

    turns = [
        [(t, 2 * ((t // 2 + h) % pairs) + t % 2) for t in range(n_etp)] for h in range(1, pairs)
    ]

    def add(kept, sent, counts):
        shapes = [
            jax.ShapeDtypeStruct((count * rows, width), jnp.bfloat16 if h else jnp.float32)
            for count in counts
            for h in range(pairs)
        ]
        sums = pl.pallas_call(
            functools.partial(add_kernel, pairs),
            out_shape=shapes,
            in_specs=[VMEM] * 2,
            out_specs=[VMEM] * len(shapes),
            compiler_params=GRANT,
            name="add",
        )(kept, lax.ppermute(sent, "etp", swap))
        return [sums[i * pairs : (i + 1) * pairs] for i in range(len(counts))]

    def over_pairs(own, *others):
        take = own.shape[0] // rows
        landed = [lax.ppermute(piece, "etp", turn) for piece, turn in zip(others, turns)]
        return list(
            pl.pallas_call(
                functools.partial(fold_kernel, pairs),
                out_shape=[jax.ShapeDtypeStruct((rows, width), jnp.bfloat16)] * take,
                in_specs=[VMEM] * pairs,
                out_specs=[VMEM] * take,
                compiler_params=GRANT,
                name="fold",
            )(own, *landed)
        )

    half = n_expert // 2
    first, second = add(far_kept, far_sent, (half // 2, half - half // 2))
    near_kept, first, second = lax.optimization_barrier((near_kept, first, second))
    pieces = over_pairs(*first) + over_pairs(*second)
    own, last = add(near_kept, near_sent, (1, half - 1))
    last = over_pairs(*last)
    pieces += last
    own, *others = own
    own = [own] + [lax.ppermute(piece, "etp", turn) for piece, turn in zip(others, turns)]
    landed = []
    for k, piece in enumerate(pieces, 1):
        route = [(e, (e + k) % n_expert) for e in range(n_expert)]
        landed.append(lax.ppermute(piece, "expert", route))

    return pl.pallas_call(
        functools.partial(mix_kernel, n_expert, pairs),
        out_shape=jax.ShapeDtypeStruct((rows, width), jnp.bfloat16),
        in_specs=[VMEM] * (1 + n_expert + pairs),
        out_specs=VMEM,
        compiler_params=GRANT,
        name="mix",
    )(expert_ids.T, route_weights.T, *own, *landed)


def solution(mesh):
    in_specs = (
        P(("group", "expert"), None),
        P(("group", "expert"), None),
        P(("group", "expert", "etp"), None),
        P("expert", "etp", None),
        P("expert", "etp", None),
        P("expert", "etp", None),
    )
    out_specs = P(("group", "expert", "etp"), None)
    return jax.shard_map(
        functools.partial(on_device, mesh.shape["expert"], mesh.shape["etp"]),
        mesh=mesh,
        in_specs=in_specs,
        out_specs=out_specs,
        check_vma=False,
    )
```

```python
import functools

import jax
import jax.numpy as jnp
from jax import lax
from jax.experimental import pallas as pl
from jax.experimental.pallas import tpu as pltpu
from jax.sharding import PartitionSpec as P

VMEM = pl.BlockSpec(memory_space=pltpu.VMEM)
GRANT = pltpu.CompilerParams(vmem_limit_bytes=16 * 1024 * 1024)
AHEAD = pl.CostEstimate(flops=10**10, bytes_accessed=0, transcendentals=0)
HBM = pl.BlockSpec(memory_space=pltpu.HBM)


def fetch_kernel(tokens, own, sem):
    copy = pltpu.make_async_copy(tokens, own, sem)
    copy.start()
    copy.wait()


def order_kernel(n_expert, pairs, rows, own, out):
    del own
    total = out.shape[0]
    me = lax.axis_index("etp")
    core, pair = lax.rem(me, 2), lax.div(me, 2)
    place = lax.broadcasted_iota(jnp.int32, (total, total), 0)
    source = lax.broadcasted_iota(jnp.int32, (total, total), 1)
    far = total - 4 * pairs * rows
    is_near = place >= far
    place = jnp.where(is_near, place - far, place)
    count = jnp.where(is_near, 1, n_expert // 2 - 1)
    row = lax.rem(place, rows)
    side = lax.rem(lax.div(place, rows), 2)
    two = lax.rem(lax.div(place, rows * 2), count)
    h = lax.rem(lax.div(place, rows * 2 * count), pairs)
    sent = lax.div(place, rows * 2 * count * pairs)
    k = jnp.where(is_near, 0, 2 * two + 2) + lax.rem(core + sent, 2)
    block = 2 * lax.rem(pair + h, pairs) + lax.rem(core + sent + side, 2)
    wanted = (k * pairs * 2 + block) * rows + row
    out[...] = jnp.where(source == wanted, 1.0, 0.0).astype(jnp.bfloat16)


def ffn_kernel(n_expert, parts, own, next_block, order, *refs):
    far = refs[: n_expert - 2]
    w_gate, w_up, w_down, kept, sent, rest, x = refs[n_expert - 2 :]
    core = lax.rem(lax.axis_index("etp"), 2)
    tok = own.shape[0]
    x[0:tok, :] = own[...]
    x[tok : 2 * tok, :] = next_block[...]
    for i in range(0, n_expert - 2, 2):
        for block, k in ((far[i], i + 2 + core), (far[i + 1], i + 3 - core)):
            x[pl.ds(pl.multiple_of(k * tok, tok), tok), :] = block[...]
    contract = (((1,), (1,)), ((), ()))
    gate = lax.dot_general(w_gate[0], x[...], contract, preferred_element_type=jnp.float32)
    upper = lax.dot_general(w_up[0], x[...], contract, preferred_element_type=jnp.float32)
    hidden = (gate / (1.0 + jnp.exp(-gate)) * upper).astype(jnp.bfloat16)
    hidden = lax.dot_general(order[...], hidden, contract, preferred_element_type=jnp.float32)
    hidden = hidden.astype(jnp.bfloat16)
    now = hidden.shape[0] - rest.shape[0]
    rest[...] = hidden[now:]
    down(parts, hidden[:now], w_down, kept, sent)


def down(parts, hidden, w_down, kept, sent):
    side, width = kept.shape
    step = width // parts
    for c in range(parts):
        cols = slice(c * step, (c + 1) * step)
        out = jnp.dot(hidden, w_down[0, :, cols], preferred_element_type=jnp.float32)
        kept[:, cols] = out[:side]
        sent[:, cols] = out[side:].astype(jnp.bfloat16)


def down_kernel(parts, hidden, w_down, kept, sent):
    down(parts, hidden[...], w_down, kept, sent)


def add_kernel(kept, arrived, own, *pieces):
    span = own.shape[0]
    own[...] = kept[:span, :] + arrived[:span, :].astype(jnp.float32)
    for i, piece in enumerate(pieces):
        at = slice((i + 1) * span, (i + 2) * span)
        piece[...] = (kept[at, :] + arrived[at, :].astype(jnp.float32)).astype(jnp.bfloat16)


def fold_kernel(pairs, own, *refs):
    arrived, pieces = refs[: pairs - 1], refs[pairs - 1 :]
    total = own[...]
    for block in arrived:
        total = total + block[...].astype(jnp.float32)
    rows = pieces[0].shape[0]
    for k, piece in enumerate(pieces):
        piece[...] = total[k * rows : (k + 1) * rows].astype(piece.dtype)


def pack_kernel(near_landed, *refs):
    far, out = refs[:-1], refs[-1]
    rows = near_landed.shape[0] // 2
    out[:rows] = near_landed[rows:]
    for i, piece in enumerate(far, 1):
        out[i * rows : (i + 1) * rows] = piece[rows:]


def mix_kernel(ids, weights, swapped, near_landed, *refs):
    far, out = refs[:-1], refs[-1]
    rows = out.shape[0]
    me, expert = lax.axis_index("etp"), lax.axis_index("expert")
    core = lax.rem(me, 2)
    top, tok = ids.shape

    def column(ref, start, i):
        lane = lax.broadcasted_iota(jnp.int32, (rows, ref.shape[1]), 1)
        row = lax.broadcasted_iota(jnp.int32, (rows, ref.shape[1]), 0)
        values = jnp.where(lane == start + row, ref[i : i + 1, :], 0)
        return jnp.sum(values, axis=1, keepdims=True)

    own_ids = [column(ids, me * rows, i) for i in range(top)]
    own_weights = [column(weights, 0, i) for i in range(top)]
    scale = sum(own_weights)
    total = None
    for i in range(len(far) + 1):
        if i == 0:
            mine = near_landed[:rows]
        else:
            mine = far[i - 1][:rows]
        for part, k in ((mine, 2 * i + core), (swapped[i * rows : (i + 1) * rows], 2 * i + 1 - core)):
            owner = lax.bitwise_xor(expert, k)
            factor = (
                sum(jnp.where(own_ids[j] == owner, own_weights[j], 0.0) for j in range(top)) / scale
            )
            term = part.astype(jnp.float32) * factor
            total = term if total is None else total + term
    out[...] = total.astype(out.dtype)


def on_device(n_expert, n_etp, tokens, expert_ids, route_weights, w_gate, w_up, w_down):
    tok, width = tokens.shape
    rows = tok // n_etp
    pairs = n_etp // 2
    side = n_expert * tok // 2

    own = pl.pallas_call(
        fetch_kernel,
        out_shape=jax.ShapeDtypeStruct((tok, width), tokens.dtype),
        in_specs=[HBM],
        out_specs=VMEM,
        scratch_shapes=[pltpu.SemaphoreType.DMA],
        compiler_params=GRANT,
        name="fetch",
    )(pltpu.with_memory_space_constraint(tokens, pltpu.HBM))
    order = pl.pallas_call(
        functools.partial(order_kernel, n_expert, pairs, rows),
        out_shape=jax.ShapeDtypeStruct((2 * side, 2 * side), jnp.bfloat16),
        in_specs=[VMEM],
        out_specs=VMEM,
        cost_estimate=AHEAD,
        compiler_params=GRANT,
        name="order",
    )(own)

    swap = [(t, t ^ 1) for t in range(n_etp)]
    routes = [
        [
            (e * n_etp + t, (e ^ (k + t % 2)) * n_etp + t)
            for e in range(n_expert)
            for t in range(n_etp)
        ]
        for k in range(2, n_expert, 2)
    ]
    far = [lax.ppermute(tokens, ("expert", "etp"), route) for route in routes]
    next_block = lax.ppermute(tokens, "expert", [(e, e ^ 1) for e in range(n_expert)])
    far = [b for block in far for b in (block, lax.ppermute(block, "etp", swap))]

    parts = 4
    def halves(experts):
        shape = (experts * tok // 2, width)
        return [jax.ShapeDtypeStruct(shape, dtype) for dtype in (jnp.float32, jnp.bfloat16)]

    far_kept, far_sent, rest = pl.pallas_call(
        functools.partial(ffn_kernel, n_expert, parts),
        out_shape=halves(n_expert - 2)
        + [jax.ShapeDtypeStruct((2 * tok, w_gate.shape[1]), jnp.bfloat16)],
        in_specs=[VMEM] * (n_expert + 4),
        out_specs=[VMEM] * 3,
        scratch_shapes=[pltpu.VMEM((n_expert * tok, width), jnp.bfloat16)],
        compiler_params=GRANT,
        name="ffn",
    )(own, next_block, order, *far, w_gate, w_up, w_down)
    near_kept, near_sent = pl.pallas_call(
        functools.partial(down_kernel, parts),
        out_shape=halves(2),
        in_specs=[VMEM] * 2,
        out_specs=[VMEM] * 2,
        compiler_params=GRANT,
        name="down",
    )(rest, w_down)

    turns = [
        [(t, 2 * ((t // 2 + h) % pairs) + t % 2) for t in range(n_etp)] for h in range(1, pairs)
    ]

    def over_etp(kept, sent, twos):
        block = (kept.shape[0] // pairs, width)
        own, *others = pl.pallas_call(
            add_kernel,
            out_shape=[jax.ShapeDtypeStruct(block, jnp.float32)]
            + [jax.ShapeDtypeStruct(block, jnp.bfloat16)] * (pairs - 1),
            in_specs=[VMEM] * 2,
            out_specs=[VMEM] * pairs,
            compiler_params=GRANT,
            name="add",
        )(kept, lax.ppermute(sent, "etp", swap))
        landed = [lax.ppermute(piece, "etp", turn) for piece, turn in zip(others, turns)]
        return pl.pallas_call(
            functools.partial(fold_kernel, pairs),
            out_shape=[jax.ShapeDtypeStruct((2 * rows, width), jnp.bfloat16)] * twos,
            in_specs=[VMEM] * pairs,
            out_specs=[VMEM] * twos,
            compiler_params=GRANT,
            name="fold",
        )(own, *landed)

    twos = n_expert // 2
    far = [
        lax.ppermute(piece, ("expert", "etp"), route)
        for piece, route in zip(over_etp(far_kept, far_sent, twos - 1), routes)
    ]
    (near_kept,) = over_etp(near_kept, near_sent, 1)
    odd = [
        (e * n_etp + t, (e ^ t % 2) * n_etp + t) for e in range(n_expert) for t in range(n_etp)
    ]
    near_landed = lax.ppermute(near_kept, ("expert", "etp"), odd)
    packed = pl.pallas_call(
        pack_kernel,
        out_shape=jax.ShapeDtypeStruct((twos * rows, width), jnp.bfloat16),
        in_specs=[VMEM] * twos,
        out_specs=VMEM,
        compiler_params=GRANT,
        name="pack",
    )(near_landed, *far)
    swapped = lax.ppermute(packed, "etp", swap)

    return pl.pallas_call(
        mix_kernel,
        out_shape=jax.ShapeDtypeStruct((rows, width), jnp.bfloat16),
        in_specs=[VMEM] * (twos + 3),
        out_specs=VMEM,
        compiler_params=GRANT,
        name="mix",
    )(expert_ids.T, route_weights.T, swapped, near_landed, *far)


def solution(mesh):
    in_specs = (
        P(("group", "expert"), None),
        P(("group", "expert"), None),
        P(("group", "expert", "etp"), None),
        P("expert", "etp", None),
        P("expert", "etp", None),
        P("expert", "etp", None),
    )
    out_specs = P(("group", "expert", "etp"), None)
    return jax.shard_map(
        functools.partial(on_device, mesh.shape["expert"], mesh.shape["etp"]),
        mesh=mesh,
        in_specs=in_specs,
        out_specs=out_specs,
        check_vma=False,
    )
```

```python
import functools

import jax
import jax.numpy as jnp
from jax import lax
from jax.experimental import pallas as pl
from jax.experimental.pallas import tpu as pltpu
from jax.sharding import PartitionSpec as P

VMEM = pl.BlockSpec(memory_space=pltpu.VMEM)
GRANT = pltpu.CompilerParams(vmem_limit_bytes=16 * 1024 * 1024)
AHEAD = pl.CostEstimate(flops=10**10, bytes_accessed=0, transcendentals=0)
HBM = pl.BlockSpec(memory_space=pltpu.HBM)


def fetch_kernel(tokens, own, sem):
    copy = pltpu.make_async_copy(tokens, own, sem)
    copy.start()
    copy.wait()


def order_kernel(n_expert, pairs, rows, own, out):
    del own
    total = out.shape[0]
    me = lax.axis_index("etp")
    core, pair = lax.rem(me, 2), lax.div(me, 2)
    place = lax.broadcasted_iota(jnp.int32, (total, total), 0)
    source = lax.broadcasted_iota(jnp.int32, (total, total), 1)
    half = n_expert // 2
    row = lax.rem(place, rows)
    k = lax.rem(lax.div(place, rows), half)
    h = lax.rem(lax.div(place, rows * half), pairs)
    sent = lax.rem(lax.div(place, rows * half * pairs), 2)
    second = lax.div(place, rows * half * pairs * 2)
    shift = jnp.where(second == 0, k + 1, jnp.where(k == 0, 0, k + half))
    expert = lax.axis_index("expert")
    k = lax.bitwise_xor(expert, lax.rem(expert + shift, n_expert))
    block = 2 * lax.rem(pair + h, pairs) + lax.rem(core + sent, 2)
    wanted = (k * pairs * 2 + block) * rows + row
    out[...] = jnp.where(source == wanted, 1.0, 0.0).astype(jnp.bfloat16)


def ffn_kernel(n_expert, parts, own, next_block, order, *refs):
    far = refs[: n_expert - 2]
    w_gate, w_up, w_down, kept, sent, rest, x = refs[n_expert - 2 :]
    core = lax.rem(lax.axis_index("etp"), 2)
    tok = own.shape[0]
    x[0:tok, :] = own[...]
    x[tok : 2 * tok, :] = next_block[...]
    for i in range(0, n_expert - 2, 2):
        for block, k in ((far[i], i + 2 + core), (far[i + 1], i + 3 - core)):
            x[pl.ds(pl.multiple_of(k * tok, tok), tok), :] = block[...]
    contract = (((1,), (1,)), ((), ()))
    gate = lax.dot_general(w_gate[0], x[...], contract, preferred_element_type=jnp.float32)
    upper = lax.dot_general(w_up[0], x[...], contract, preferred_element_type=jnp.float32)
    hidden = (gate / (1.0 + jnp.exp(-gate)) * upper).astype(jnp.bfloat16)
    hidden = lax.dot_general(order[...], hidden, contract, preferred_element_type=jnp.float32)
    hidden = hidden.astype(jnp.bfloat16)
    now = rest.shape[0]
    rest[...] = hidden[now:]
    down(parts, hidden[:now], w_down, kept, sent)


def down(parts, hidden, w_down, kept, sent):
    side, width = kept.shape
    step = width // parts
    for c in range(parts):
        cols = slice(c * step, (c + 1) * step)
        out = jnp.dot(hidden, w_down[0, :, cols], preferred_element_type=jnp.float32)
        kept[:, cols] = out[:side]
        sent[:, cols] = out[side:].astype(jnp.bfloat16)


def down_kernel(parts, hidden, w_down, kept, sent):
    down(parts, hidden[...], w_down, kept, sent)


def add_kernel(pairs, kept, arrived, *refs):
    total = kept[...] + arrived[...].astype(jnp.float32)
    start = 0
    for h in range(pairs):
        for out in refs[h::pairs]:
            out[...] = total[start : start + out.shape[0]].astype(out.dtype)
            start += out.shape[0]


def fold_kernel(pairs, own, *refs):
    arrived, pieces = refs[: pairs - 1], refs[pairs - 1 :]
    total = own[...]
    for block in arrived:
        total = total + block[...].astype(jnp.float32)
    rows = pieces[0].shape[0]
    for k, piece in enumerate(pieces):
        piece[...] = total[k * rows : (k + 1) * rows].astype(piece.dtype)


def weigh_kernel(n_expert, pairs, ids, weights, *refs):
    own, pieces, (out, last_factor) = refs[:pairs], refs[pairs:-2], refs[-2:]
    rows = out.shape[0]
    me, expert = lax.axis_index("etp"), lax.axis_index("expert")
    top, tok = ids.shape

    def column(ref, start, i):
        lane = lax.broadcasted_iota(jnp.int32, (rows, ref.shape[1]), 1)
        row = lax.broadcasted_iota(jnp.int32, (rows, ref.shape[1]), 0)
        values = jnp.where(lane == start + row, ref[i : i + 1, :], 0)
        return jnp.sum(values, axis=1, keepdims=True)

    own_ids = [column(ids, me * rows, i) for i in range(top)]
    own_weights = [column(weights, 0, i) for i in range(top)]
    scale = sum(own_weights)
    for k in range(n_expert):
        owner = lax.rem(expert - k + n_expert, n_expert)
        factor = sum(jnp.where(own_ids[i] == owner, own_weights[i], 0.0) for i in range(top)) / scale
        if k == 0:
            total = sum(block[...].astype(jnp.float32) for block in own) * factor
        elif k < n_expert - 1:
            total = total + pieces[k - 1][...].astype(jnp.float32) * factor
        else:
            last_factor[...] = jnp.broadcast_to(factor, last_factor.shape)
    out[...] = total


def finish_kernel(partial, factor, piece, out):
    total = partial[...] + piece[...].astype(jnp.float32) * factor[:, :1]
    out[...] = total.astype(out.dtype)


def on_device(n_expert, n_etp, tokens, expert_ids, route_weights, w_gate, w_up, w_down):
    tok, width = tokens.shape
    rows = tok // n_etp
    pairs = n_etp // 2
    side = n_expert * tok // 2

    own = pl.pallas_call(
        fetch_kernel,
        out_shape=jax.ShapeDtypeStruct((tok, width), tokens.dtype),
        in_specs=[HBM],
        out_specs=VMEM,
        scratch_shapes=[pltpu.SemaphoreType.DMA],
        compiler_params=GRANT,
        name="fetch",
    )(pltpu.with_memory_space_constraint(tokens, pltpu.HBM))
    order = pl.pallas_call(
        functools.partial(order_kernel, n_expert, pairs, rows),
        out_shape=jax.ShapeDtypeStruct((2 * side, 2 * side), jnp.bfloat16),
        in_specs=[VMEM],
        out_specs=VMEM,
        cost_estimate=AHEAD,
        compiler_params=GRANT,
        name="order",
    )(own)

    swap = [(t, t ^ 1) for t in range(n_etp)]
    far = []
    for k in range(2, n_expert, 2):
        route = [
            (e * n_etp + t, (e ^ (k + t % 2)) * n_etp + t)
            for e in range(n_expert)
            for t in range(n_etp)
        ]
        far.append(lax.ppermute(tokens, ("expert", "etp"), route))
    next_block = lax.ppermute(tokens, "expert", [(e, e ^ 1) for e in range(n_expert)])
    far = [b for block in far for b in (block, lax.ppermute(block, "etp", swap))]

    parts = 4
    halves = [
        jax.ShapeDtypeStruct((side // 2, width), jnp.float32),
        jax.ShapeDtypeStruct((side // 2, width), jnp.bfloat16),
    ]
    far_kept, far_sent, rest = pl.pallas_call(
        functools.partial(ffn_kernel, n_expert, parts),
        out_shape=halves + [jax.ShapeDtypeStruct((side, w_gate.shape[1]), jnp.bfloat16)],
        in_specs=[VMEM] * (n_expert + 4),
        out_specs=[VMEM] * 3,
        scratch_shapes=[pltpu.VMEM((n_expert * tok, width), jnp.bfloat16)],
        compiler_params=GRANT,
        name="ffn",
    )(own, next_block, order, *far, w_gate, w_up, w_down)
    near_kept, near_sent = pl.pallas_call(
        functools.partial(down_kernel, parts),
        out_shape=halves,
        in_specs=[VMEM] * 2,
        out_specs=[VMEM] * 2,
        compiler_params=GRANT,
        name="down",
    )(rest, w_down)

    turns = [
        [(t, 2 * ((t // 2 + h) % pairs) + t % 2) for t in range(n_etp)] for h in range(1, pairs)
    ]

    def add(kept, sent, counts):
        shapes = [
            jax.ShapeDtypeStruct((count * rows, width), jnp.bfloat16 if h else jnp.float32)
            for count in counts
            for h in range(pairs)
        ]
        sums = pl.pallas_call(
            functools.partial(add_kernel, pairs),
            out_shape=shapes,
            in_specs=[VMEM] * 2,
            out_specs=[VMEM] * len(shapes),
            compiler_params=GRANT,
            name="add",
        )(kept, lax.ppermute(sent, "etp", swap))
        return [sums[i * pairs : (i + 1) * pairs] for i in range(len(counts))]

    def over_pairs(own, *others):
        take = own.shape[0] // rows
        landed = [lax.ppermute(piece, "etp", turn) for piece, turn in zip(others, turns)]
        return list(
            pl.pallas_call(
                functools.partial(fold_kernel, pairs),
                out_shape=[jax.ShapeDtypeStruct((rows, width), jnp.bfloat16)] * take,
                in_specs=[VMEM] * pairs,
                out_specs=[VMEM] * take,
                compiler_params=GRANT,
                name="fold",
            )(own, *landed)
        )

    half = n_expert // 2
    first, second = add(far_kept, far_sent, (half // 2, half - half // 2))
    pieces = over_pairs(*first) + over_pairs(*second)
    own, last = add(near_kept, near_sent, (1, half - 1))
    last = over_pairs(*last)
    pieces += last
    own, *others = own
    own = [own] + [lax.ppermute(piece, "etp", turn) for piece, turn in zip(others, turns)]
    landed = []
    for k, piece in enumerate(pieces, 1):
        route = [(e, (e + k) % n_expert) for e in range(n_expert)]
        landed.append(lax.ppermute(piece, "expert", route))

    partial, factor = pl.pallas_call(
        functools.partial(weigh_kernel, n_expert, pairs),
        out_shape=[
            jax.ShapeDtypeStruct((rows, width), jnp.float32),
            jax.ShapeDtypeStruct((rows, 128), jnp.float32),
        ],
        in_specs=[VMEM] * (n_expert + pairs),
        out_specs=[VMEM] * 2,
        compiler_params=GRANT,
        name="weigh",
    )(expert_ids.T, route_weights.T, *own, *landed[:-1])
    return pl.pallas_call(
        finish_kernel,
        out_shape=jax.ShapeDtypeStruct((rows, width), jnp.bfloat16),
        in_specs=[VMEM] * 3,
        out_specs=VMEM,
        compiler_params=GRANT,
        name="finish",
    )(partial, factor, landed[-1])


def solution(mesh):
    in_specs = (
        P(("group", "expert"), None),
        P(("group", "expert"), None),
        P(("group", "expert", "etp"), None),
        P("expert", "etp", None),
        P("expert", "etp", None),
        P("expert", "etp", None),
    )
    out_specs = P(("group", "expert", "etp"), None)
    return jax.shard_map(
        functools.partial(on_device, mesh.shape["expert"], mesh.shape["etp"]),
        mesh=mesh,
        in_specs=in_specs,
        out_specs=out_specs,
        check_vma=False,
    )
```

```python
import functools

import jax
import jax.numpy as jnp
from jax import lax
from jax.experimental import pallas as pl
from jax.experimental.pallas import tpu as pltpu
from jax.sharding import PartitionSpec as P

VMEM = pl.BlockSpec(memory_space=pltpu.VMEM)
GRANT = pltpu.CompilerParams(vmem_limit_bytes=16 * 1024 * 1024)
AHEAD = pl.CostEstimate(flops=10**10, bytes_accessed=0, transcendentals=0)
HBM = pl.BlockSpec(memory_space=pltpu.HBM)


def fetch_kernel(tokens, own, sem):
    copy = pltpu.make_async_copy(tokens, own, sem)
    copy.start()
    copy.wait()


def order_kernel(n_expert, pairs, rows, own, out):
    del own
    total = out.shape[0]
    me = lax.axis_index("etp")
    core, pair = lax.rem(me, 2), lax.div(me, 2)
    place = lax.broadcasted_iota(jnp.int32, (total, total), 0)
    source = lax.broadcasted_iota(jnp.int32, (total, total), 1)
    half = n_expert // 2
    row = lax.rem(place, rows)
    k = lax.rem(lax.div(place, rows), half)
    h = lax.rem(lax.div(place, rows * half), pairs)
    sent = lax.rem(lax.div(place, rows * half * pairs), 2)
    second = lax.div(place, rows * half * pairs * 2)
    first = jnp.where(lax.rem(core + sent, 2) == 0, k + 1, half - k)
    shift = jnp.where(second == 0, first, jnp.where(k == 0, 0, k + half))
    expert = lax.axis_index("expert")
    k = lax.bitwise_xor(expert, lax.rem(expert + shift, n_expert))
    block = 2 * lax.rem(pair + h, pairs) + lax.rem(core + sent, 2)
    wanted = (k * pairs * 2 + block) * rows + row
    out[...] = jnp.where(source == wanted, 1.0, 0.0).astype(jnp.bfloat16)


def ffn_kernel(n_expert, parts, own, next_block, order, *refs):
    far = refs[: n_expert - 2]
    w_gate, w_up, w_down, kept, sent, rest, x = refs[n_expert - 2 :]
    core = lax.rem(lax.axis_index("etp"), 2)
    tok = own.shape[0]
    x[0:tok, :] = own[...]
    x[tok : 2 * tok, :] = next_block[...]
    for i in range(0, n_expert - 2, 2):
        for block, k in ((far[i], i + 2 + core), (far[i + 1], i + 3 - core)):
            x[pl.ds(pl.multiple_of(k * tok, tok), tok), :] = block[...]
    contract = (((1,), (1,)), ((), ()))
    gate = lax.dot_general(w_gate[0], x[...], contract, preferred_element_type=jnp.float32)
    upper = lax.dot_general(w_up[0], x[...], contract, preferred_element_type=jnp.float32)
    hidden = (gate / (1.0 + jnp.exp(-gate)) * upper).astype(jnp.bfloat16)
    hidden = lax.dot_general(order[...], hidden, contract, preferred_element_type=jnp.float32)
    hidden = hidden.astype(jnp.bfloat16)
    now = rest.shape[0]
    rest[...] = hidden[now:]
    down(parts, hidden[:now], w_down, kept, sent)


def down(parts, hidden, w_down, kept, sent):
    side, width = kept.shape
    step = width // parts
    for c in range(parts):
        cols = slice(c * step, (c + 1) * step)
        out = jnp.dot(hidden, w_down[0, :, cols], preferred_element_type=jnp.float32)
        kept[:, cols] = out[:side]
        sent[:, cols] = out[side:].astype(jnp.bfloat16)


def down_kernel(parts, hidden, w_down, kept, sent):
    down(parts, hidden[...], w_down, kept, sent)


def add_kernel(pairs, kept, arrived, *refs):
    total = kept[...] + arrived[...].astype(jnp.float32)
    start = 0
    for h in range(pairs):
        for out in refs[h::pairs]:
            out[...] = total[start : start + out.shape[0]].astype(out.dtype)
            start += out.shape[0]


def fold_kernel(pairs, own, *refs):
    arrived, pieces = refs[: pairs - 1], refs[pairs - 1 :]
    total = own[...]
    for block in arrived:
        total = total + block[...].astype(jnp.float32)
    rows = pieces[0].shape[0]
    for k, piece in enumerate(pieces):
        piece[...] = total[k * rows : (k + 1) * rows].astype(piece.dtype)


def weigh_kernel(n_expert, pairs, ids, weights, *refs):
    own, pieces, (out, last_factor) = refs[:pairs], refs[pairs:-2], refs[-2:]
    rows = out.shape[0]
    me, expert = lax.axis_index("etp"), lax.axis_index("expert")
    top, tok = ids.shape

    def column(ref, start, i):
        lane = lax.broadcasted_iota(jnp.int32, (rows, ref.shape[1]), 1)
        row = lax.broadcasted_iota(jnp.int32, (rows, ref.shape[1]), 0)
        values = jnp.where(lane == start + row, ref[i : i + 1, :], 0)
        return jnp.sum(values, axis=1, keepdims=True)

    own_ids = [column(ids, me * rows, i) for i in range(top)]
    own_weights = [column(weights, 0, i) for i in range(top)]
    scale = sum(own_weights)
    for k in range(n_expert):
        half = n_expert // 2
        shift = jnp.where(lax.rem(me, 2) == 0, k, half + 1 - k) if 0 < k <= half else k
        owner = lax.rem(expert - shift + n_expert, n_expert)
        factor = sum(jnp.where(own_ids[i] == owner, own_weights[i], 0.0) for i in range(top)) / scale
        if k == 0:
            total = sum(block[...].astype(jnp.float32) for block in own) * factor
        elif k < n_expert - 1:
            total = total + pieces[k - 1][...].astype(jnp.float32) * factor
        else:
            last_factor[...] = jnp.broadcast_to(factor, last_factor.shape)
    out[...] = total


def finish_kernel(partial, factor, piece, out):
    total = partial[...] + piece[...].astype(jnp.float32) * factor[:, :1]
    out[...] = total.astype(out.dtype)


def on_device(n_expert, n_etp, tokens, expert_ids, route_weights, w_gate, w_up, w_down):
    tok, width = tokens.shape
    rows = tok // n_etp
    pairs = n_etp // 2
    side = n_expert * tok // 2

    own = pl.pallas_call(
        fetch_kernel,
        out_shape=jax.ShapeDtypeStruct((tok, width), tokens.dtype),
        in_specs=[HBM],
        out_specs=VMEM,
        scratch_shapes=[pltpu.SemaphoreType.DMA],
        compiler_params=GRANT,
        name="fetch",
    )(pltpu.with_memory_space_constraint(tokens, pltpu.HBM))
    order = pl.pallas_call(
        functools.partial(order_kernel, n_expert, pairs, rows),
        out_shape=jax.ShapeDtypeStruct((2 * side, 2 * side), jnp.bfloat16),
        in_specs=[VMEM],
        out_specs=VMEM,
        cost_estimate=AHEAD,
        compiler_params=GRANT,
        name="order",
    )(own)

    swap = [(t, t ^ 1) for t in range(n_etp)]
    far = []
    for k in range(2, n_expert, 2):
        route = [
            (e * n_etp + t, (e ^ (k + t % 2)) * n_etp + t)
            for e in range(n_expert)
            for t in range(n_etp)
        ]
        far.append(lax.ppermute(tokens, ("expert", "etp"), route))
    next_block = lax.ppermute(tokens, "expert", [(e, e ^ 1) for e in range(n_expert)])
    far = [b for block in far for b in (block, lax.ppermute(block, "etp", swap))]

    parts = 4
    halves = [
        jax.ShapeDtypeStruct((side // 2, width), jnp.float32),
        jax.ShapeDtypeStruct((side // 2, width), jnp.bfloat16),
    ]
    far_kept, far_sent, rest = pl.pallas_call(
        functools.partial(ffn_kernel, n_expert, parts),
        out_shape=halves + [jax.ShapeDtypeStruct((side, w_gate.shape[1]), jnp.bfloat16)],
        in_specs=[VMEM] * (n_expert + 4),
        out_specs=[VMEM] * 3,
        scratch_shapes=[pltpu.VMEM((n_expert * tok, width), jnp.bfloat16)],
        compiler_params=GRANT,
        name="ffn",
    )(own, next_block, order, *far, w_gate, w_up, w_down)
    near_kept, near_sent = pl.pallas_call(
        functools.partial(down_kernel, parts),
        out_shape=halves,
        in_specs=[VMEM] * 2,
        out_specs=[VMEM] * 2,
        compiler_params=GRANT,
        name="down",
    )(rest, w_down)

    turns = [
        [(t, 2 * ((t // 2 + h) % pairs) + t % 2) for t in range(n_etp)] for h in range(1, pairs)
    ]

    def add(kept, sent, counts):
        shapes = [
            jax.ShapeDtypeStruct((count * rows, width), jnp.bfloat16 if h else jnp.float32)
            for count in counts
            for h in range(pairs)
        ]
        sums = pl.pallas_call(
            functools.partial(add_kernel, pairs),
            out_shape=shapes,
            in_specs=[VMEM] * 2,
            out_specs=[VMEM] * len(shapes),
            compiler_params=GRANT,
            name="add",
        )(kept, lax.ppermute(sent, "etp", swap))
        return [sums[i * pairs : (i + 1) * pairs] for i in range(len(counts))]

    def over_pairs(own, *others):
        take = own.shape[0] // rows
        landed = [lax.ppermute(piece, "etp", turn) for piece, turn in zip(others, turns)]
        return list(
            pl.pallas_call(
                functools.partial(fold_kernel, pairs),
                out_shape=[jax.ShapeDtypeStruct((rows, width), jnp.bfloat16)] * take,
                in_specs=[VMEM] * pairs,
                out_specs=[VMEM] * take,
                compiler_params=GRANT,
                name="fold",
            )(own, *landed)
        )

    half = n_expert // 2
    first, second = add(far_kept, far_sent, (half // 2, half - half // 2))
    pieces = over_pairs(*first) + over_pairs(*second)
    own, last = add(near_kept, near_sent, (1, half - 1))
    last = over_pairs(*last)
    pieces += last
    own, *others = own
    own = [own] + [lax.ppermute(piece, "etp", turn) for piece, turn in zip(others, turns)]
    landed = []
    for k, piece in enumerate(pieces, 1):
        route = [
            (e * n_etp + t, (e + (half + 1 - k if t % 2 and k <= half else k)) % n_expert * n_etp + t)
            for e in range(n_expert)
            for t in range(n_etp)
        ]
        landed.append(lax.ppermute(piece, ("expert", "etp"), route))

    partial, factor = pl.pallas_call(
        functools.partial(weigh_kernel, n_expert, pairs),
        out_shape=[
            jax.ShapeDtypeStruct((rows, width), jnp.float32),
            jax.ShapeDtypeStruct((rows, 128), jnp.float32),
        ],
        in_specs=[VMEM] * (n_expert + pairs),
        out_specs=[VMEM] * 2,
        compiler_params=GRANT,
        name="weigh",
    )(expert_ids.T, route_weights.T, *own, *landed[:-1])
    return pl.pallas_call(
        finish_kernel,
        out_shape=jax.ShapeDtypeStruct((rows, width), jnp.bfloat16),
        in_specs=[VMEM] * 3,
        out_specs=VMEM,
        compiler_params=GRANT,
        name="finish",
    )(partial, factor, landed[-1])


def solution(mesh):
    in_specs = (
        P(("group", "expert"), None),
        P(("group", "expert"), None),
        P(("group", "expert", "etp"), None),
        P("expert", "etp", None),
        P("expert", "etp", None),
        P("expert", "etp", None),
    )
    out_specs = P(("group", "expert", "etp"), None)
    return jax.shard_map(
        functools.partial(on_device, mesh.shape["expert"], mesh.shape["etp"]),
        mesh=mesh,
        in_specs=in_specs,
        out_specs=out_specs,
        check_vma=False,
    )
```

```python
import functools

import jax
import jax.numpy as jnp
from jax import lax
from jax.experimental import pallas as pl
from jax.experimental.pallas import tpu as pltpu
from jax.sharding import PartitionSpec as P

VMEM = pl.BlockSpec(memory_space=pltpu.VMEM)
GRANT = pltpu.CompilerParams(vmem_limit_bytes=16 * 1024 * 1024)
AHEAD = pl.CostEstimate(flops=10**10, bytes_accessed=0, transcendentals=0)
HBM = pl.BlockSpec(memory_space=pltpu.HBM)


def fetch_kernel(tokens, own, sem):
    copy = pltpu.make_async_copy(tokens, own, sem)
    copy.start()
    copy.wait()


def order_kernel(n_expert, pairs, rows, own, out):
    del own
    total = out.shape[0]
    me = lax.axis_index("etp")
    core, pair = lax.rem(me, 2), lax.div(me, 2)
    place = lax.broadcasted_iota(jnp.int32, (total, total), 0)
    source = lax.broadcasted_iota(jnp.int32, (total, total), 1)
    half = n_expert // 2
    row = lax.rem(place, rows)
    k = lax.rem(lax.div(place, rows), half)
    h = lax.rem(lax.div(place, rows * half), pairs)
    sent = lax.rem(lax.div(place, rows * half * pairs), 2)
    second = lax.div(place, rows * half * pairs * 2)
    shift = jnp.where(second == 0, k + 1, jnp.where(k == 0, 0, k + half))
    expert = lax.axis_index("expert")
    k = lax.bitwise_xor(expert, lax.rem(expert + shift, n_expert))
    block = 2 * lax.rem(pair + h, pairs) + lax.rem(core + sent, 2)
    wanted = (k * pairs * 2 + block) * rows + row
    out[...] = jnp.where(source == wanted, 1.0, 0.0).astype(jnp.bfloat16)


def ffn_kernel(n_expert, parts, own, next_block, order, *refs):
    far = refs[: n_expert - 2]
    w_gate, w_up, w_down, kept, sent, rest, x = refs[n_expert - 2 :]
    core = lax.rem(lax.axis_index("etp"), 2)
    tok = own.shape[0]
    x[0:tok, :] = own[...]
    x[tok : 2 * tok, :] = next_block[...]
    for i in range(0, n_expert - 2, 2):
        for block, k in ((far[i], i + 2 + core), (far[i + 1], i + 3 - core)):
            x[pl.ds(pl.multiple_of(k * tok, tok), tok), :] = block[...]
    contract = (((1,), (1,)), ((), ()))
    gate = lax.dot_general(w_gate[0], x[...], contract, preferred_element_type=jnp.float32)
    upper = lax.dot_general(w_up[0], x[...], contract, preferred_element_type=jnp.float32)
    hidden = (gate / (1.0 + jnp.exp(-gate)) * upper).astype(jnp.bfloat16)
    hidden = lax.dot_general(order[...], hidden, contract, preferred_element_type=jnp.float32)
    hidden = hidden.astype(jnp.bfloat16)
    now = rest.shape[0]
    rest[...] = hidden[now:]
    down(parts, hidden[:now], w_down, kept, sent)


def down(parts, hidden, w_down, kept, sent):
    side, width = kept.shape
    step = width // parts
    for c in range(parts):
        cols = slice(c * step, (c + 1) * step)
        out = jnp.dot(hidden, w_down[0, :, cols], preferred_element_type=jnp.float32)
        kept[:, cols] = out[:side]
        sent[:, cols] = out[side:].astype(jnp.bfloat16)


def down_kernel(parts, hidden, w_down, kept, sent):
    down(parts, hidden[...], w_down, kept, sent)


def add_kernel(pairs, kept, arrived, *refs):
    total = kept[...] + arrived[...].astype(jnp.float32)
    start = 0
    for h in range(pairs):
        for out in refs[h::pairs]:
            out[...] = total[start : start + out.shape[0]].astype(out.dtype)
            start += out.shape[0]


def fold_kernel(pairs, own, *refs):
    arrived, pieces = refs[: pairs - 1], refs[pairs - 1 :]
    total = own[...]
    for block in arrived:
        total = total + block[...].astype(jnp.float32)
    rows = pieces[0].shape[0]
    for k, piece in enumerate(pieces):
        piece[...] = total[k * rows : (k + 1) * rows].astype(piece.dtype)


def weigh_kernel(n_expert, pairs, ids, weights, *refs):
    own, pieces, (out, last_factor) = refs[:pairs], refs[pairs:-2], refs[-2:]
    rows = out.shape[0]
    me, expert = lax.axis_index("etp"), lax.axis_index("expert")
    top, tok = ids.shape

    def column(ref, start, i):
        lane = lax.broadcasted_iota(jnp.int32, (rows, ref.shape[1]), 1)
        row = lax.broadcasted_iota(jnp.int32, (rows, ref.shape[1]), 0)
        values = jnp.where(lane == start + row, ref[i : i + 1, :], 0)
        return jnp.sum(values, axis=1, keepdims=True)

    own_ids = [column(ids, me * rows, i) for i in range(top)]
    own_weights = [column(weights, 0, i) for i in range(top)]
    scale = sum(own_weights)
    for k in range(n_expert):
        owner = lax.rem(expert - k + n_expert, n_expert)
        factor = sum(jnp.where(own_ids[i] == owner, own_weights[i], 0.0) for i in range(top)) / scale
        if k == 0:
            total = sum(block[...].astype(jnp.float32) for block in own) * factor
        elif k < n_expert - 1:
            total = total + pieces[k - 1][...].astype(jnp.float32) * factor
        else:
            last_factor[...] = jnp.broadcast_to(factor, last_factor.shape)
    out[...] = total


def finish_kernel(partial, factor, piece, out):
    total = partial[...] + piece[...].astype(jnp.float32) * factor[:, :1]
    out[...] = total.astype(out.dtype)


def on_device(n_expert, n_etp, tokens, expert_ids, route_weights, w_gate, w_up, w_down):
    tok, width = tokens.shape
    rows = tok // n_etp
    pairs = n_etp // 2
    side = n_expert * tok // 2

    own = pl.pallas_call(
        fetch_kernel,
        out_shape=jax.ShapeDtypeStruct((tok, width), tokens.dtype),
        in_specs=[HBM],
        out_specs=VMEM,
        scratch_shapes=[pltpu.SemaphoreType.DMA],
        compiler_params=GRANT,
        name="fetch",
    )(pltpu.with_memory_space_constraint(tokens, pltpu.HBM))
    order = pl.pallas_call(
        functools.partial(order_kernel, n_expert, pairs, rows),
        out_shape=jax.ShapeDtypeStruct((2 * side, 2 * side), jnp.bfloat16),
        in_specs=[VMEM],
        out_specs=VMEM,
        cost_estimate=AHEAD,
        compiler_params=GRANT,
        name="order",
    )(own)

    swap = [(t, t ^ 1) for t in range(n_etp)]
    far = []
    for k in range(2, n_expert, 2):
        route = [
            (e * n_etp + t, (e ^ (k + t % 2)) * n_etp + t)
            for e in range(n_expert)
            for t in range(n_etp)
        ]
        far.append(lax.ppermute(tokens, ("expert", "etp"), route))
    next_block = lax.ppermute(tokens, "expert", [(e, e ^ 1) for e in range(n_expert)])
    far = [b for block in far for b in (block, lax.ppermute(block, "etp", swap))]

    parts = 8
    halves = [
        jax.ShapeDtypeStruct((side // 2, width), jnp.float32),
        jax.ShapeDtypeStruct((side // 2, width), jnp.bfloat16),
    ]
    far_kept, far_sent, rest = pl.pallas_call(
        functools.partial(ffn_kernel, n_expert, parts),
        out_shape=halves + [jax.ShapeDtypeStruct((side, w_gate.shape[1]), jnp.bfloat16)],
        in_specs=[VMEM] * (n_expert + 4),
        out_specs=[VMEM] * 3,
        scratch_shapes=[pltpu.VMEM((n_expert * tok, width), jnp.bfloat16)],
        compiler_params=GRANT,
        name="ffn",
    )(own, next_block, order, *far, w_gate, w_up, w_down)
    near_kept, near_sent = pl.pallas_call(
        functools.partial(down_kernel, parts),
        out_shape=halves,
        in_specs=[VMEM] * 2,
        out_specs=[VMEM] * 2,
        compiler_params=GRANT,
        name="down",
    )(rest, w_down)

    turns = [
        [(t, 2 * ((t // 2 + h) % pairs) + t % 2) for t in range(n_etp)] for h in range(1, pairs)
    ]

    def add(kept, sent, counts):
        shapes = [
            jax.ShapeDtypeStruct((count * rows, width), jnp.bfloat16 if h else jnp.float32)
            for count in counts
            for h in range(pairs)
        ]
        sums = pl.pallas_call(
            functools.partial(add_kernel, pairs),
            out_shape=shapes,
            in_specs=[VMEM] * 2,
            out_specs=[VMEM] * len(shapes),
            compiler_params=GRANT,
            name="add",
        )(kept, lax.ppermute(sent, "etp", swap))
        return [sums[i * pairs : (i + 1) * pairs] for i in range(len(counts))]

    def over_pairs(own, *others):
        take = own.shape[0] // rows
        landed = [lax.ppermute(piece, "etp", turn) for piece, turn in zip(others, turns)]
        return list(
            pl.pallas_call(
                functools.partial(fold_kernel, pairs),
                out_shape=[jax.ShapeDtypeStruct((rows, width), jnp.bfloat16)] * take,
                in_specs=[VMEM] * pairs,
                out_specs=[VMEM] * take,
                compiler_params=GRANT,
                name="fold",
            )(own, *landed)
        )

    half = n_expert // 2
    first, second = add(far_kept, far_sent, (half // 2, half - half // 2))
    pieces = over_pairs(*first) + over_pairs(*second)
    own, last = add(near_kept, near_sent, (1, half - 1))
    last = over_pairs(*last)
    pieces += last
    own, *others = own
    own = [own] + [lax.ppermute(piece, "etp", turn) for piece, turn in zip(others, turns)]
    landed = []
    for k, piece in enumerate(pieces, 1):
        route = [(e, (e + k) % n_expert) for e in range(n_expert)]
        landed.append(lax.ppermute(piece, "expert", route))

    partial, factor = pl.pallas_call(
        functools.partial(weigh_kernel, n_expert, pairs),
        out_shape=[
            jax.ShapeDtypeStruct((rows, width), jnp.float32),
            jax.ShapeDtypeStruct((rows, 128), jnp.float32),
        ],
        in_specs=[VMEM] * (n_expert + pairs),
        out_specs=[VMEM] * 2,
        compiler_params=GRANT,
        name="weigh",
    )(expert_ids.T, route_weights.T, *own, *landed[:-1])
    return pl.pallas_call(
        finish_kernel,
        out_shape=jax.ShapeDtypeStruct((rows, width), jnp.bfloat16),
        in_specs=[VMEM] * 3,
        out_specs=VMEM,
        compiler_params=GRANT,
        name="finish",
    )(partial, factor, landed[-1])


def solution(mesh):
    in_specs = (
        P(("group", "expert"), None),
        P(("group", "expert"), None),
        P(("group", "expert", "etp"), None),
        P("expert", "etp", None),
        P("expert", "etp", None),
        P("expert", "etp", None),
    )
    out_specs = P(("group", "expert", "etp"), None)
    return jax.shard_map(
        functools.partial(on_device, mesh.shape["expert"], mesh.shape["etp"]),
        mesh=mesh,
        in_specs=in_specs,
        out_specs=out_specs,
        check_vma=False,
    )
```
